32 devices in a mesh: dp: 8 (over y, x, core), mp: 4 (over z).
Axes of the slice: x: 2, y: 2, z: 4, core: 2. Of those that a mesh axis runs over, the one named last changes fastest.
Arguments:
- inputs: bfloat16 [8192, 1024], P(('dp', 'mp')), may hold values from -6 to 6
- query_key_value_weight: bfloat16 [2, 1024, 3, 1024], P(None, 'dp', None, 'mp'), may hold values from -0.1875 to 0.1875
- query_key_value_bias: bfloat16 [2, 3, 1024], P(None, None, 'mp'), may hold values from -2 to 2
- attention_out_weight: bfloat16 [2, 1024, 1024], P(None, 'mp', 'dp'), may hold values from -1 to 1
- attention_out_bias: bfloat16 [2, 1024], P(None, 'dp'), may hold values from -2 to 2
- feed_input_weight: bfloat16 [2, 1024, 4096], P(None, 'dp', 'mp'), may hold values from -0.1875 to 0.1875
- feed_input_bias: bfloat16 [2, 4096], P(None, 'mp'), may hold values from -2 to 2
- feed_output_weight: bfloat16 [2, 4096, 1024], P(None, 'mp', 'dp'), may hold values from -0.09375 to 0.09375
- feed_output_bias: bfloat16 [2, 1024], P(None, 'dp'), may hold values from -2 to 2
- layer_norm_gain: bfloat16 [2, 2, 1024], P(None, None, 'dp'), may hold values from 0.25 to 1.75
- layer_norm_shift: bfloat16 [2, 2, 1024], P(None, None, 'dp'), may hold values from -2 to 2
- adapter_first_weight: bfloat16 [2, 2, 1024, 4], replicated, may hold values from -0.1875 to 0.1875
- adapter_second_weight: bfloat16 [2, 2, 4, 1024], P(None, None, None, 'mp'), may hold values from -0.375 to 0.375
- cotangent: bfloat16 [8192, 1024], P(('dp', 'mp')), may hold values from -6 to 6
Outputs:
- output: bfloat16 [8192, 1024], P(('dp', 'mp'))
- grad_input: bfloat16 [8192, 1024], P(('dp', 'mp'))
- grad_a: float32 [2, 2, 1024, 4], replicated
- grad_b: float32 [2, 2, 4, 1024], replicated
The draws below stay inside these ranges and needn't reach their ends.
All inputs are finite; a program needn't handle non-finite values.
Results may differ from the reference program's by a relative error of at most 0.02.
Values may be sent and summed in bfloat16 or wider, within the bound.
A program may use at most 128 MiB of HBM per device.

```python
import jax
import jax.numpy as jnp
from jax import lax

MODEL_WIDTH = 1024
HEADS = 16
HD = 64
FF = 4096
ADAPTER_RANK = 4
BLOCK_COUNT = 2
SEQ = 1024
TOKENS = 8192


def steps_of(rng, dims, cuts, low, high):
    loudness = 1.0
    for position, parts in cuts:
        heights = jax.random.uniform(jax.random.fold_in(jax.random.fold_in(rng, 6), position), (parts,), jnp.float32, low / len(cuts), high / len(cuts))
        loudness = loudness * jnp.repeat(jnp.exp(heights), dims[position] // parts).reshape((-1,) + (1,) * (len(dims) - 1 - position))
    return loudness


def gaussian(stream_key, shape, width, most, shards=(), dtype=jnp.bfloat16):
    entries = width * jax.random.normal(stream_key, shape, jnp.float32)
    if shards:
        entries = entries * steps_of(stream_key, shape, shards, -0.22, 0.18)
    return jnp.clip(entries, -most, most).astype(dtype)


def setup_inputs(seed: int = 0) -> dict:
    streams_of = jax.random.split(jax.random.key(seed), 15)
    return {
        "inputs": gaussian(streams_of[0], (TOKENS, MODEL_WIDTH), 1.0, 6.0, ((0, 32),)),
        "query_key_value_weight": gaussian(streams_of[1], (BLOCK_COUNT, MODEL_WIDTH, 3, MODEL_WIDTH), MODEL_WIDTH ** -0.5, 0.1875, ((1, 8), (3, 4))),
        "query_key_value_bias": gaussian(streams_of[2], (BLOCK_COUNT, 3, MODEL_WIDTH), 0.3, 2.0, ((2, 4),)),
        "attention_out_weight": gaussian(streams_of[3], (BLOCK_COUNT, MODEL_WIDTH, MODEL_WIDTH), (MODEL_WIDTH // 32) ** -0.5, 1.0, ((1, 4), (2, 8))),
        "attention_out_bias": gaussian(streams_of[4], (BLOCK_COUNT, MODEL_WIDTH), 0.3, 2.0, ((1, 8),)),
        "feed_input_weight": gaussian(streams_of[5], (BLOCK_COUNT, MODEL_WIDTH, FF), MODEL_WIDTH ** -0.5, 0.1875, ((1, 8), (2, 4))),
        "feed_input_bias": gaussian(streams_of[6], (BLOCK_COUNT, FF), 0.3, 2.0, ((1, 4),)),
        "feed_output_weight": gaussian(streams_of[7], (BLOCK_COUNT, FF, MODEL_WIDTH), FF ** -0.5, 0.09375, ((1, 4), (2, 8))),
        "feed_output_bias": gaussian(streams_of[8], (BLOCK_COUNT, MODEL_WIDTH), 0.3, 2.0, ((1, 8),)),
        "layer_norm_gain": jnp.clip(1.0 + 0.15 * jax.random.normal(streams_of[9], (BLOCK_COUNT, 2, MODEL_WIDTH), jnp.float32), 0.25, 1.75).astype(jnp.bfloat16),
        "layer_norm_shift": gaussian(streams_of[10], (BLOCK_COUNT, 2, MODEL_WIDTH), 0.3, 2.0, ((2, 8),)),
        "adapter_first_weight": gaussian(streams_of[11], (BLOCK_COUNT, 2, MODEL_WIDTH, ADAPTER_RANK), MODEL_WIDTH ** -0.5, 0.1875),
        "adapter_second_weight": gaussian(streams_of[12], (BLOCK_COUNT, 2, ADAPTER_RANK, MODEL_WIDTH), (64 * ADAPTER_RANK) ** -0.5, 0.375, ((3, 4),)),
        "cotangent": gaussian(streams_of[13], (TOKENS, MODEL_WIDTH), 1.0, 6.0, ((0, 32),)),
    }


NORM_EPS = 1e-05
ADAPTER_SCALE = 8.0
EXACT_PRECISION = lax.Precision.HIGHEST

@jax.custom_vjp
def low(v):
    return lax.optimization_barrier(v.astype(jnp.bfloat16)).astype(jnp.float32)

@jax.custom_vjp
def low_back(v):
    return v

def low_keep(v):
    return (low(v), None)

def low_pass(retained_state, grad):
    return (grad,)

def back_keep(v):
    return (v, None)

def back_low(retained_state, grad):
    return (low(grad),)
low.defvjp(low_keep, low_pass)
low_back.defvjp(back_keep, back_low)

def layer_norm(stream, gain, shift):
    average = lax.optimization_barrier(jnp.mean(stream, axis=-1, keepdims=True))
    centred = stream - average
    spread = lax.optimization_barrier(jnp.mean(centred * centred, axis=-1, keepdims=True))
    return centred * lax.rsqrt(spread + NORM_EPS) * gain + shift

def gelu_tanh(values):
    return jax.nn.gelu(values, approximate=True)

def attend_doc(pieces):
    query_rows_all, key_rows, value_matrix = pieces
    scores = jnp.einsum('qhd,khd->hqk', query_rows_all, key_rows, precision=EXACT_PRECISION) * HD ** (-0.5)
    scores = low_back(scores)
    places = jnp.arange(query_rows_all.shape[0])
    allowed = places[:, None] >= places[None, :]
    scores = jnp.where(allowed[None], scores, -1e+30)
    attn_prob = low(jax.nn.softmax(scores, axis=-1))
    return jnp.einsum('hqk,khd->qhd', attn_prob, value_matrix, precision=EXACT_PRECISION)

def block_forward(stream, adapt_a, adapter_second, frozen):
    query_key_value_weight, query_key_value_bias, attention_out_weight, attention_out_bias, feed_input_weight, feed_input_bias, feed_output_weight, feed_output_bias, layer_norm_gain, layer_norm_shift = frozen
    normalized_rows = low(layer_norm(stream, layer_norm_gain[0], layer_norm_shift[0]))
    lowered_query = jnp.dot(normalized_rows, adapt_a[0], precision=EXACT_PRECISION)
    lowered_value = jnp.dot(normalized_rows, adapt_a[1], precision=EXACT_PRECISION)
    query_rows_all = jnp.dot(normalized_rows, query_key_value_weight[:, 0], precision=EXACT_PRECISION) + query_key_value_bias[0] + ADAPTER_SCALE * jnp.dot(lowered_query, adapter_second[0], precision=EXACT_PRECISION)
    key_rows = jnp.dot(normalized_rows, query_key_value_weight[:, 1], precision=EXACT_PRECISION) + query_key_value_bias[1]
    value_matrix = jnp.dot(normalized_rows, query_key_value_weight[:, 2], precision=EXACT_PRECISION) + query_key_value_bias[2] + ADAPTER_SCALE * jnp.dot(lowered_value, adapter_second[1], precision=EXACT_PRECISION)
    query_rows_all = low(low_back(query_rows_all))
    key_rows = low(low_back(key_rows))
    value_matrix = low(low_back(value_matrix))
    doc_shape = (-1, SEQ, HEADS, HD)
    context = lax.map(jax.checkpoint(attend_doc), (query_rows_all.reshape(doc_shape), key_rows.reshape(doc_shape), value_matrix.reshape(doc_shape)))
    context = low(low_back(context.reshape(stream.shape[0], -1)))
    midway = stream + low_back(jnp.dot(context, attention_out_weight, precision=EXACT_PRECISION) + attention_out_bias)
    normed_two = low(layer_norm(midway, layer_norm_gain[1], layer_norm_shift[1]))
    pre_act = low_back(jnp.dot(normed_two, feed_input_weight, precision=EXACT_PRECISION) + feed_input_bias)
    hidden = low(gelu_tanh(pre_act))
    return midway + low_back(jnp.dot(hidden, feed_output_weight, precision=EXACT_PRECISION) + feed_output_bias)

def expand_width(array):
    return array.astype(jnp.float32)

def reference(inputs, query_key_value_weight, query_key_value_bias, attention_out_weight, attention_out_bias, feed_input_weight, feed_input_bias, feed_output_weight, feed_output_bias, layer_norm_gain, layer_norm_shift, adapter_first_weight, adapter_second_weight, cotangent):
    frozen = [expand_width(array) for array in (query_key_value_weight, query_key_value_bias, attention_out_weight, attention_out_bias, feed_input_weight, feed_input_bias, feed_output_weight, feed_output_bias, layer_norm_gain, layer_norm_shift)]

    def forward_step(stream, all_a, all_b):
        for layer_selector in range(BLOCK_COUNT):
            stream = block_forward(stream, all_a[layer_selector], all_b[layer_selector], [array[layer_selector] for array in frozen])
        return stream
    final_output, backward_map = jax.vjp(forward_step, expand_width(inputs), expand_width(adapter_first_weight), expand_width(adapter_second_weight))
    grad_x, grad_a, grad_b = backward_map(expand_width(cotangent))
    return (final_output.astype(jnp.bfloat16), grad_x.astype(jnp.bfloat16), grad_a, grad_b)
```

```python
import functools

import jax
import jax.numpy as jnp
from jax import lax
from jax.experimental import pallas as pl
from jax.experimental.pallas import tpu as pltpu
from jax.sharding import PartitionSpec as P

MESH = pl.DeviceIdType.MESH
F32 = jnp.float32
BF = jnp.bfloat16
D = 1024
BLK = 256
HD = 64
LAYERS = 2
NORM_EPS = 1e-05
ADAPTER_SCALE = 8.0
C0 = 0.7978845608
C1 = 0.044715
NEG = -1e30

PIECE = ((0, 1, 3), (5, 6, 7))
PIECES = 8


def nt(a, b):
    return lax.dot_general(a, b, (((1,), (1,)), ((), ())), preferred_element_type=F32)


def nn(a, b):
    return lax.dot_general(a, b, (((1,), (0,)), ((), ())), preferred_element_type=F32)


def flip(value, bit):
    return value + (1 << bit) * (1 - 2 * ((value // (1 << bit)) % 2))


def gelu(u):
    return 0.5 * u * (1.0 + jnp.tanh(C0 * (u + C1 * u * u * u)))


def gelu_slope(u):
    square = u * u
    th = jnp.tanh(C0 * u * (1.0 + C1 * square))
    return 0.5 * (1.0 + th) + 0.5 * u * (1.0 - th * th) * (C0 * (1.0 + 3.0 * C1 * square))


def normed(x):
    c = x - jnp.mean(x, axis=-1, keepdims=True)
    rstd = lax.rsqrt(jnp.mean(c * c, axis=-1, keepdims=True) + NORM_EPS)
    return c * rstd, rstd


def norm_back(x, grad, gain):
    xhat, rstd = normed(x)
    gx = grad * gain
    return rstd * (
        gx
        - jnp.mean(gx, axis=-1, keepdims=True)
        - xhat * jnp.mean(gx * xhat, axis=-1, keepdims=True)
    )


def kernel(
    ndp,
    x_in, cot_in, wsh, apad, bpad, bqkv, b1, vec,
    out_ref, gin_ref, G,
    W, n1, ga, gmx, q_ref, k_ref, v_ref, tr, low, x0, x1, m1, u0, u1, act, ctx, gctx, ctxT,
    part, rs1, rs2s, rs2r, party, rs1y, rs2ys, rs2yr, nx0, sys_, syr, gqkv, gt_ref,
    acc, g_ref, gmid, gsend, grecv, lse,
    ssem, rsem, p0r, lsem,
):
    R = wsh.shape[1]
    gk, gv = acc, g_ref
    ob0, ob1 = rs2ys, sys_
    d = lax.axis_index("dp")
    z = lax.axis_index("mp")
    k = d % 2
    j = d // 2
    zl = z % 2
    zh = z // 2
    qi = 2 * k + zl
    chip_bits = (ndp // 2).bit_length() - 1

    def col(dc, dz):
        zz = z
        if dz & 1:
            zz = zz + 1 - 2 * zl
        if dz & 2:
            zz = zz + 2 - 4 * zh
        return (d + 1 - 2 * k if dc else d, zz)

    sib, zp, swap = col(1, 0), col(0, 1), col(1, 2)
    count = [0]
    sends = []

    def sem():
        count[0] += 1
        return count[0] - 1

    def rcopy(src, dst, dev, keep=True):
        i = sem()
        cp = pltpu.make_async_remote_copy(
            src, dst, ssem.at[i], rsem.at[i], device_id=dev, device_id_type=MESH
        )
        cp.start()
        if keep:
            sends.append(cp.wait_send)
        return cp

    peers = [col(dc, dz) for dc in range(2) for dz in range(4) if dc or dz]
    peers += [(flip(d, bit + 1), z) for bit in range(chip_bits)]
    barrier = pltpu.get_barrier_semaphore()
    for dev in peers:
        pl.semaphore_signal(barrier, inc=1, device_id=dev, device_id_type=MESH)
    pl.semaphore_wait(barrier, len(peers))

    def swap_rows(src, dst_own, dst_other):
        i = sem()
        keep = pltpu.make_async_copy(src, dst_own, rsem.at[i])
        move = pltpu.make_async_remote_copy(
            src, dst_other, ssem.at[i], rsem.at[i], device_id=swap, device_id_type=MESH
        )

        @pl.when(k == zh)
        def _():
            keep.start()

        @pl.when(k != zh)
        def _():
            move.start()

        def finish_send():
            @pl.when(k != zh)
            def _():
                move.wait_send()

        sends.append(finish_send)
        return keep.wait

    def block(b):
        return pl.ds(pl.multiple_of(b * BLK, BLK), BLK)

    own_rows = pl.ds(pl.multiple_of(d * R, R), R)

    def start_p0(layer, mat):
        single = layer == 1 or mat == 0
        piece = PIECE[layer][mat] if single else PIECE[layer][mat] + zl
        src = wsh.at[layer * 3 + mat]
        dst = W.at[piece, own_rows, :]
        arrived = p0r.at[piece]
        holder = 2 * j + zh
        i = sem()
        near = pltpu.make_async_remote_copy(
            src, dst, ssem.at[i], arrived, device_id=(holder, z), device_id_type=MESH
        )

        @pl.when(k == zh)
        def _():
            pltpu.make_async_copy(src, dst, arrived).start()

        @pl.when(k != zh)
        def _():
            near.start()

        def finish():
            @pl.when(k != zh)
            def _():
                near.wait_send()

        sends.append(finish)
        for r in (2,) if single else (1, 2, 3):
            i = sem()
            far = pltpu.make_async_remote_copy(
                src, dst, ssem.at[i], arrived, device_id=(holder, col(0, r)[1]), device_id_type=MESH
            )
            far.start()
            sends.append(far.wait_send)

    def wait_p0(piece):
        slab = W.at[piece, pl.ds(0, 2 * R), :]
        pltpu.make_async_copy(slab, slab, p0r.at[piece]).wait()

    half_cols = (pl.ds(0, D // 2), pl.ds(D // 2, D // 2))
    order = (tuple(range(chip_bits)), tuple(reversed(range(chip_bits))))
    stage_wait = {}

    def start_stage(piece, stage):
        waits = []
        for half in range(2):
            bits = order[half]
            dev = (flip(d, bits[stage] + 1), z)
            i = sem()
            cols = half_cols[half]

            def send(m, bits=bits, cols=cols, dev=dev, i=i):
                chip = j
                for n, bit in enumerate(bits[:stage]):
                    chip = chip + ((m // (1 << n)) % 2) * (flip(j, bit) - j)
                ref = W.at[piece, pl.ds(pl.multiple_of(chip * (2 * R), 2 * R), 2 * R), cols]
                pltpu.make_async_remote_copy(
                    ref, ref, ssem.at[i], rsem.at[i], device_id=dev, device_id_type=MESH
                ).start()

            if stage <= 1:
                for m in range(1 << stage):
                    send(m)
            else:

                def body(m, carry, send=send):
                    send(m)
                    return carry

                lax.fori_loop(0, 1 << stage, body, 0)
            slab = W.at[piece, pl.ds(0, (1 << stage) * 2 * R), cols]
            waits.append(pltpu.make_async_copy(slab, slab, rsem.at[i]).wait)
            sends.append(pltpu.make_async_copy(slab, slab, ssem.at[i]).wait)
        stage_wait[piece, stage] = waits

    def wait_stage(piece, stage):
        for w in stage_wait[piece, stage]:
            w()

    def first_stage(piece):
        wait_p0(piece)
        start_stage(piece, 0)

    def later_stages(piece):
        for stage in range(1, chip_bits):
            wait_stage(piece, stage - 1)
            start_stage(piece, stage)

    def ready(piece):
        wait_stage(piece, chip_bits - 1)

    def pump(n):
        if n == 0:
            start_p0(0, 2)
        if n == 2:
            start_p0(1, 0)
        if n == 3:
            start_p0(1, 1)
        if n == 4:
            start_p0(1, 2)
        later_stages(n)
        if n + 2 < PIECES:
            first_stage(n + 2)

    def gather4(buf):
        mine = buf.at[block(qi)]
        to_z = rcopy(mine, mine, zp, keep=False)
        to_s = rcopy(mine, mine, sib, keep=False)
        other = buf.at[block(2 * k + 1 - zl)]

        def forward():
            to_z.wait_recv()
            return rcopy(other, other, sib, keep=False)

        def finish(fwd):
            to_s.wait_recv()
            fwd.wait_recv()
            for cp in (to_z, to_s, fwd):
                cp.wait_send()

        return forward, finish

    def scatter4(partial, p, r1, r2s, r2r):
        cps = []
        for s in (1 - zl, zl):
            p[s] = partial(2 * (1 - k) + s).astype(BF)
            cps.append(rcopy(p.at[s], r1.at[s], sib, keep=False))
        mine = partial(2 * k + 1 - zl)
        cps[0].wait_recv()
        r2s[...] = (mine + r1[1 - zl].astype(F32)).astype(BF)
        cp2 = rcopy(r2s, r2r, zp, keep=False)

        def finish(dst):
            dst[...] = partial(qi)
            cps[1].wait_recv()
            dst[...] += r1[zl].astype(F32)
            cp2.wait_recv()
            dst[...] += r2r[...].astype(F32)
            for cp in cps:
                cp.wait_send()
            cp2.wait_send()

        return finish

    def rowwise(f):
        def body(c, carry):
            f(pl.ds(pl.multiple_of(c * 64, 64), 64))
            return carry

        lax.fori_loop(0, BLK // 64, body, 0)

    def norm_into(src, dst, layer, which):
        gain, shift = vec[layer, 2 * which], vec[layer, 2 * which + 1]

        def f(rows):
            xhat, _ = normed(src[rows, :].astype(F32))
            dst[rows, :] = (xhat * gain + shift).astype(BF)

        rowwise(f)

    tri = lax.broadcasted_iota(jnp.int32, (BLK, BLK), 0) <= lax.broadcasted_iota(
        jnp.int32, (BLK, BLK), 1
    )
    lane_head = lax.broadcasted_iota(jnp.int32, (1, BLK), 1) // HD

    def project(layer):
        w = W.at[PIECE[layer][0]]

        def body(c, carry):
            rows = block(c)
            n = n1[layer, rows, :]
            t = nn(n, apad[layer]).astype(BF)
            low[layer, rows, :] = t
            pr = nn(n, w[:, 0:768]) + bqkv[layer] + nn(t, bpad[layer])
            pr = pr.astype(BF)
            q_ref[layer, rows, :] = pr[:, 0:256]
            k_ref[layer, rows, :] = pr[:, 256:512]
            v = pr[:, 512:768]
            v_ref[layer, rows, :] = v
            tr[:, rows] = v.astype(F32).T.astype(BF)
            return carry

        lax.fori_loop(0, 4, body, 0)

    def attend(layer, i):
        lo = i * BLK
        kk, qq = k_ref.at[layer], q_ref.at[layer]

        def pair(hp, carry):
            for s in range(2):
                h = hp * 2 + s
                qm = qq[lo : lo + BLK, :] * jnp.where(lane_head == h, 0.125, 0.0).astype(BF)
                head = pl.ds(pl.multiple_of(h * HD, HD), HD)
                sd = jnp.where(tri, nt(kk[lo : lo + BLK, :], qm), NEG)
                top = jnp.max(sd, axis=0, keepdims=True)
                if i:
                    sa = nt(kk[0:lo, :], qm)
                    top = jnp.maximum(top, jnp.max(sa, axis=0, keepdims=True))
                ed = jnp.exp(sd - top)
                total = jnp.sum(ed, axis=0, keepdims=True)
                o = nn(tr[head, lo : lo + BLK], ed.astype(BF))
                if i:
                    ea = jnp.exp(sa - top)
                    total = total + jnp.sum(ea, axis=0, keepdims=True)
                    o = o + nn(tr[head, 0:lo], ea.astype(BF))
                ctxT[head, :] = o / total
                lse[layer, pl.ds(h, 1), lo : lo + BLK] = top + jnp.log(total)
            return carry

        lax.fori_loop(0, 2, pair, 0)
        ctx[lo : lo + BLK, :] = ctxT[...].T.astype(BF)

    def attend_back(layer, i):
        lo = i * BLK
        kk, qq, vv = k_ref.at[layer], q_ref.at[layer], v_ref.at[layer]

        def pair(hp, carry):
            for s in range(2):
                h = hp * 2 + s
                on = lane_head == h
                qm = qq[lo : lo + BLK, :] * jnp.where(on, 0.125, 0.0).astype(BF)
                gm = gctx[lo : lo + BLK, :] * jnp.where(on, 1.0, 0.0).astype(BF)
                head = pl.ds(pl.multiple_of(h * HD, HD), HD)
                ls = lse[layer, pl.ds(h, 1), lo : lo + BLK]
                spans = [(lo, lo + BLK)] + ([(0, lo)] if i else [])
                ps, ts = [], []
                for a, b in spans:
                    p = jnp.exp(nt(kk[a:b, :], qm) - ls)
                    if a == lo:
                        p = jnp.where(tri, p, 0.0)
                    ps.append(p)
                    ts.append(p * nt(vv[a:b, :], gm))
                dsum = sum(jnp.sum(t, axis=0, keepdims=True) for t in ts)
                o = None
                for (a, b), p, t in zip(spans, ps, ts):
                    gs = (t - p * dsum).astype(BF)
                    dv = nn(p.astype(BF), gm)
                    dk = nn(gs, qm)
                    for c in range(a // BLK, b // BLK):
                        at = pl.ds(c * BLK, BLK)
                        gv[:, at] += dv[c * BLK - a : (c + 1) * BLK - a]
                        gk[:, at] += dk[c * BLK - a : (c + 1) * BLK - a]
                    dq = nn(tr[head, a:b], gs)
                    o = dq if o is None else o + dq
                ctxT[head, :] = o * 0.125
            return carry

        lax.fori_loop(0, 2, pair, 0)
        gqkv[lo : lo + BLK, 0:256] = ctxT[...].T.astype(BF)

    def out_partial(layer):
        w = W.at[PIECE[layer][0]]
        return lambda b: nt(ctx[block(b), :], w[:, 768:1024])

    own0 = x0.at[...]
    x_here = swap_rows(x_in, own0, own0)
    start_p0(0, 0)
    start_p0(0, 1)
    first_stage(0)
    first_stage(1)
    x_here()
    norm_into(x0, n1.at[0, block(qi)], 0, 0)
    forward, finish = gather4(n1.at[0])
    pump(0)
    fwd = forward()
    finish(fwd)
    ready(0)
    pump(1)
    project(0)
    cot_here = swap_rows(
        cot_in, gmx.at[block(qi)], gmx.at[block(2 * (1 - k) + zl)]
    )
    for i in range(4):
        attend(0, i)
        if i == 2:
            pump(2)
    fin = scatter4(out_partial(0), part, rs1, rs2s, rs2r)
    fin(acc)
    m1[0] = x0[...].astype(F32) + acc[...] + vec[0, 4]
    cot_here()
    gm_forward, gm_finish = gather4(gmx)
    pump(3)
    norm_into(m1.at[0], nx0.at[k], 0, 1)
    nx = rcopy(nx0.at[k], nx0.at[k], sib, keep=False)
    nx.wait_recv()

    def hidden0(s):
        def body(c, carry):
            r, hc = c // 2, c % 2
            cols = pl.ds(pl.multiple_of(hc * 512, 512), 512)
            u = nn(nx0[r], W[1 + s, :, cols]) + b1[0, 2 * k + s, :, cols]
            u0[r, s, :, cols] = u.astype(BF)
            act[2 * r + s, :, cols] = gelu(u).astype(BF)
            return carry

        lax.fori_loop(0, 4, body, 0)

    ready(1)
    hidden0(0)
    ready(2)
    pump(4)
    hidden0(1)
    gm_fwd = gm_forward()
    nx.wait_send()
    ready(3)
    pump(5)
    ready(4)

    def mix0(r):
        return nt(act[2 * r], W[3]) + nt(act[2 * r + 1], W[4])

    sys_[...] = mix0(1 - k).astype(BF)
    cp = rcopy(sys_, syr, sib, keep=False)
    acc[...] = mix0(k)
    cp.wait_recv()
    x1[...] = m1[0] + (acc[...] + syr[...].astype(F32)) + vec[0, 5]
    cp.wait_send()
    norm_into(x1, n1.at[1, block(qi)], 1, 0)
    forward, finish = gather4(n1.at[1])
    pump(6)
    finish(forward())
    ready(5)
    project(1)
    pump(7)
    for i in range(4):
        attend(1, i)
    fin = scatter4(out_partial(1), part, rs1, rs2s, rs2r)
    fin(acc)
    m1[1] = x1[...] + acc[...] + vec[1, 4]
    norm_into(m1.at[1], ga.at[block(qi)], 1, 1)
    forward, finish = gather4(ga)
    finish(forward())
    gm_finish(gm_fwd)
    ready(6)

    def hidden1(c, carry):
        b, hc = c // 2, c % 2
        cols = pl.ds(pl.multiple_of(hc * 512, 512), 512)
        u = nn(ga[block(b), :], W[6, :, cols]) + b1[1, qi, :, cols]
        u1[b, :, cols] = u.astype(BF)
        act[b, :, cols] = gelu(u).astype(BF)
        return carry

    lax.fori_loop(0, 8, hidden1, 0)
    ready(7)

    def feed_back1(b):
        gh = nn(gmx[block(b), :], W[7])
        gu = (gh * gelu_slope(u1[b].astype(F32))).astype(BF)
        return nt(gu, W[6])

    fin = scatter4(feed_back1, part, rs1, rs2s, rs2r)
    fin(acc)

    def mid_back(layer, g_rows):
        gain = vec[layer, 2]

        def f(rows):
            v = g_rows(rows) + norm_back(m1[layer, rows, :], acc[rows, :], gain)
            gmid[rows, :] = v
            ga[block_rows(rows), :] = v.astype(BF)

        def block_rows(rows):
            return pl.ds(pl.multiple_of(qi * BLK + rows.start, 64), 64)

        rowwise(f)

    def cot_rows(rows):
        return gmx[pl.ds(pl.multiple_of(qi * BLK + rows.start, 64), 64), :].astype(F32)

    def attention_back(layer, extra=None):
        w = W.at[PIECE[layer][0]]
        forward, finish = gather4(ga)

        def turn(c, carry):
            tr[:, block(c)] = k_ref[layer, block(c), :].astype(F32).T.astype(BF)
            return carry

        lax.fori_loop(0, 4, turn, 0)
        gk[...] = jnp.zeros_like(gk)
        gv[...] = jnp.zeros_like(gv)
        finish(forward())
        end = extra() if extra else None

        def down(c, carry):
            gctx[block(c), :] = nn(ga[block(c), :], w[:, 768:1024]).astype(BF)
            return carry

        lax.fori_loop(0, 4, down, 0)
        for i in range(4):
            attend_back(layer, i)

        def lows(c, carry):
            gqkv[block(c), 256:512] = gk[:, block(c)].astype(BF)
            gqkv[block(c), 512:768] = gv[:, block(c)].astype(BF)
            gt_ref[block(c), :] = nt(gqkv[block(c), :], bpad[layer]).astype(BF)
            return carry

        lax.fori_loop(0, 4, lows, 0)
        fin = scatter4(
            lambda b: nt(gqkv[block(b), :], w[:, 0:768]) + nt(gt_ref[block(b), :], apad[layer]),
            part, rs1, rs2s, rs2r,
        )

        def grads(c, carry):
            ga_sum, gb_sum = carry
            gtt = gt_ref[block(c), :].astype(F32).T[0:16, :].astype(BF)
            tt = low[layer, block(c), :].astype(F32).T[0:16, :].astype(BF)
            return (
                ga_sum + nn(gtt, n1[layer, block(c), :]),
                gb_sum + nn(tt, gqkv[block(c), :]),
            )

        ga_sum, gb_sum = lax.fori_loop(
            0, 4, grads, (jnp.zeros((16, D), F32), jnp.zeros((16, 768), F32))
        )
        gb = ADAPTER_SCALE * jnp.where(
            lax.broadcasted_iota(jnp.int32, (8, 256), 0) < 4, gb_sum[0:8, 0:256], gb_sum[0:8, 512:768]
        )
        base = 16 * layer
        gsend[0, base : base + 8, :] = ga_sum[0:8, :]
        gsend[0, base + 8 : base + 16, :] = jnp.zeros((8, D), F32)
        gsend[0, base + 8 : base + 16, pl.ds(pl.multiple_of(qi * 256, 256), 256)] = gb
        fin(acc)
        return end

    mid_back(1, cot_rows)
    end_y = attention_back(
        1, lambda: scatter4(lambda b: nt(act[b], W[7]), party, rs1y, rs2ys, rs2yr)
    )

    def step_back(layer, src):
        gain = vec[layer, 0]

        def f(rows):
            g_ref[rows, :] = gmid[rows, :] + norm_back(src[rows, :].astype(F32), acc[rows, :], gain)

        rowwise(f)

    step_back(1, x1)
    nx0[k] = g_ref[...].astype(BF)
    nx = rcopy(nx0.at[k], nx0.at[k], sib, keep=False)
    end_y(acc)
    ob0[...] = (m1[1] + acc[...] + vec[1, 5]).astype(BF)
    out_here = swap_rows(ob0, out_ref, out_ref)
    nx.wait_recv()

    def feed_back0(r):
        total = None
        for s in range(2):
            gh = nn(nx0[r], W[3 + s])
            gu = (gh * gelu_slope(u0[r, s].astype(F32))).astype(BF)
            y = nt(gu, W[1 + s])
            total = y if total is None else total + y
        return total

    sys_[...] = feed_back0(1 - k).astype(BF)
    cp = rcopy(sys_, syr, sib, keep=False)
    acc[...] = feed_back0(k)
    cp.wait_recv()
    acc[...] += syr[...].astype(F32)
    nx.wait_send()
    cp.wait_send()
    mid_back(0, lambda rows: g_ref[rows, :])
    attention_back(0)
    step_back(0, x0)
    ob1[...] = g_ref[...].astype(BF)
    gin_here = swap_rows(ob1, gin_ref, gin_ref)

    hops = [(flip(d, b), z) for b in range(chip_bits + 1)] + [zp, col(0, 2)]
    for n, dev in enumerate(hops):
        cp = rcopy(gsend.at[n], grecv.at[n], dev)
        cp.wait_recv()
        total = gsend[n] + grecv[n]
        if n + 1 < len(hops):
            gsend[n + 1] = total
        else:
            G[...] = total
    out_here()
    gin_here()
    for w in sends:
        w()


def shards(
    inputs, qkv_w, qkv_b, out_w, out_b, fin_w, fin_b, fout_w, fout_b, gains, shifts, first, second,
    cotangent,
):
    ndp = lax.axis_size("dp")
    R = qkv_w.shape[1]
    hops = ndp.bit_length() - 1 + 2
    att = jnp.concatenate([qkv_w.reshape(LAYERS, R, 768), jnp.swapaxes(out_w, 1, 2)], axis=2)
    wsh = jnp.stack([att, fin_w, jnp.swapaxes(fout_w, 1, 2)], axis=1).reshape(LAYERS * 3, R, D)
    small = jnp.concatenate(
        [gains[:, 0:1], shifts[:, 0:1], gains[:, 1:2], shifts[:, 1:2], out_b[:, None], fout_b[:, None]],
        axis=1,
    )
    vec = lax.all_gather(small, "dp", axis=2, tiled=True).astype(F32).reshape(LAYERS, 6, 1, D)
    heads = jnp.concatenate(
        [qkv_b.reshape(LAYERS, 768), fin_b, second.reshape(LAYERS, 2048)], axis=1
    )
    heads = lax.all_gather(heads, "mp", axis=0)
    mine = 2 * (lax.axis_index("dp") % 2) + lax.axis_index("mp") % 2
    own = lax.dynamic_index_in_dim(heads, mine, 0, keepdims=False)
    bqkv = own[:, 0:768].astype(F32).reshape(LAYERS, 1, 768)
    b1 = jnp.swapaxes(heads[:, :, 768:1792], 0, 1).astype(F32).reshape(LAYERS, 4, 1, D)
    up = own[:, 1792:].reshape(LAYERS, 2, 4, 256) * jnp.asarray(ADAPTER_SCALE, BF)
    bpad = jnp.zeros((LAYERS, 128, 768), BF)
    bpad = bpad.at[:, 0:4, 0:256].set(up[:, 0]).at[:, 4:8, 512:768].set(up[:, 1])
    apad = jnp.concatenate(
        [first[:, 0], first[:, 1], jnp.zeros((LAYERS, D, 120), BF)], axis=2
    )
    anyspec = pl.BlockSpec(memory_space=pl.ANY)
    vm = pl.BlockSpec(memory_space=pltpu.VMEM)
    V = pltpu.VMEM
    scratch = [
        V((PIECES, D, D), BF),
        V((LAYERS, D, D), BF),
        V((D, D), BF),
        V((D, D), BF),
        V((LAYERS, D, 256), BF),
        V((LAYERS, D, 256), BF),
        V((LAYERS, D, 256), BF),
        V((256, D), BF),
        V((LAYERS, D, 128), BF),
        V((BLK, D), BF),
        V((BLK, D), F32),
        V((LAYERS, BLK, D), F32),
        V((2, 2, BLK, D), BF),
        V((4, BLK, D), BF),
        V((4, BLK, D), BF),
        V((D, 256), BF),
        V((D, 256), BF),
        V((256, 256), F32),
        V((2, BLK, D), BF),
        V((2, BLK, D), BF),
        V((BLK, D), BF),
        V((BLK, D), BF),
        V((2, BLK, D), BF),
        V((2, BLK, D), BF),
        V((BLK, D), BF),
        V((BLK, D), BF),
        V((2, BLK, D), BF),
        V((BLK, D), BF),
        V((BLK, D), BF),
        V((D, 768), BF),
        V((D, 128), BF),
        V((BLK, D), F32),
        V((BLK, D), F32),
        V((BLK, D), F32),
        V((hops, 32, D), F32),
        V((hops, 32, D), F32),
        V((LAYERS, 8, D), F32),
        pltpu.SemaphoreType.DMA((200,)),
        pltpu.SemaphoreType.DMA((200,)),
        pltpu.SemaphoreType.DMA((PIECES,)),
        pltpu.SemaphoreType.DMA((4,)),
    ]
    out, gin, G = pl.pallas_call(
        functools.partial(kernel, ndp),
        out_shape=(
            jax.ShapeDtypeStruct((BLK, D), BF),
            jax.ShapeDtypeStruct((BLK, D), BF),
            jax.ShapeDtypeStruct((32, D), F32),
        ),
        in_specs=[anyspec, anyspec, anyspec, vm, vm, vm, vm, vm],
        out_specs=(anyspec, anyspec, vm),
        scratch_shapes=scratch,
        compiler_params=pltpu.CompilerParams(
            collective_id=0, has_side_effects=True, vmem_limit_bytes=63 * 2**20
        ),
        name="two_blocks",
    )(inputs, cotangent, wsh, apad, bpad, bqkv, b1, vec)
    G = G.reshape(LAYERS, 16, D)
    grad_a = jnp.swapaxes(G[:, 0:8].reshape(LAYERS, 2, 4, D), 2, 3)
    grad_b = G[:, 8:16].reshape(LAYERS, 2, 4, D)
    return (out, gin, grad_a, grad_b)


def solution(mesh):
    placed = (
        P(("dp", "mp"), None),
        P(None, "dp", None, "mp"),
        P(None, None, "mp"),
        P(None, "mp", "dp"),
        P(None, "dp"),
        P(None, "dp", "mp"),
        P(None, "mp"),
        P(None, "mp", "dp"),
        P(None, "dp"),
        P(None, None, "dp"),
        P(None, None, "dp"),
        P(),
        P(None, None, None, "mp"),
        P(("dp", "mp"), None),
    )
    return jax.shard_map(
        shards,
        mesh=mesh,
        in_specs=placed,
        out_specs=(P(("dp", "mp"), None), P(("dp", "mp"), None), P(), P()),
        check_vma=False,
    )
```

```python
import functools

import jax
import jax.numpy as jnp
from jax import lax
from jax.experimental import pallas as pl
from jax.experimental.pallas import tpu as pltpu
from jax.sharding import PartitionSpec as P

MESH = pl.DeviceIdType.MESH
F32 = jnp.float32
BF = jnp.bfloat16
D = 1024
BLK = 256
HALF = 128
HD = 64
LAYERS = 2
NORM_EPS = 1e-05
ADAPTER_SCALE = 8.0
C0 = 0.7978845608
C1 = 0.044715
NEG = -1e30

ATTENTION = (0, 5)
PIECES = 8


def nt(a, b):
    return lax.dot_general(a, b, (((1,), (1,)), ((), ())), preferred_element_type=F32)


def nn(a, b):
    return lax.dot_general(a, b, (((1,), (0,)), ((), ())), preferred_element_type=F32)


def flip(value, bit):
    return value + (1 << bit) * (1 - 2 * ((value // (1 << bit)) % 2))


def gelu(u):
    return 0.5 * u * (1.0 + jnp.tanh(C0 * (u + C1 * u * u * u)))


def gelu_slope(u):
    square = u * u
    th = jnp.tanh(C0 * u * (1.0 + C1 * square))
    return 0.5 * (1.0 + th) + 0.5 * u * (1.0 - th * th) * (C0 * (1.0 + 3.0 * C1 * square))


def normed(x):
    c = x - jnp.mean(x, axis=-1, keepdims=True)
    rstd = lax.rsqrt(jnp.mean(c * c, axis=-1, keepdims=True) + NORM_EPS)
    return c * rstd, rstd


def norm_back(x, grad, gain):
    xhat, rstd = normed(x)
    gx = grad * gain
    return rstd * (
        gx
        - jnp.mean(gx, axis=-1, keepdims=True)
        - xhat * jnp.mean(gx * xhat, axis=-1, keepdims=True)
    )


def kernel(
    ndp,
    x_in, cot_in, qkvw, finw, outw, foutw, apad, small_dp, small_mp,
    out_ref, gin_ref, G,
    W, n1, ga, gmx, q_ref, k_ref, v_ref, tr, low, x0, x1, m1, u0, u1, act, ctx, gctx, ctxT,
    part, rs1, rs2s, rs2r, party, rs1y, rs2ys, rs2yr, nx0, sy, syr, gqkv, gt_ref,
    acc, g_ref, gmid, own2, gsend, grecv, lse, outT, foutT, sdp, smp, vecs, bpad, bqkv, b1,
    ssem, rsem, p0r,
):
    R = finw.shape[1]
    gk, gv = acc, g_ref
    d = lax.axis_index("dp")
    z = lax.axis_index("mp")
    k = d % 2
    j = d // 2
    zl = z % 2
    zh = z // 2
    qi = 2 * k + zl
    chip_bits = (ndp // 2).bit_length() - 1

    def col(dc, dz):
        zz = z
        if dz & 1:
            zz = zz + 1 - 2 * zl
        if dz & 2:
            zz = zz + 2 - 4 * zh
        return (d + 1 - 2 * k if dc else d, zz)

    sib, zp, swap = col(1, 0), col(0, 1), col(1, 2)
    count = [0]
    sends = []

    def sem():
        count[0] += 1
        return count[0] - 1

    def rcopy(src, dst, dev, keep=False):
        i = sem()
        cp = pltpu.make_async_remote_copy(
            src, dst, ssem.at[i], rsem.at[i], device_id=dev, device_id_type=MESH
        )
        cp.start()
        if keep:
            sends.append(cp.wait_send)
        return cp

    peers = [col(dc, dz) for dc in range(2) for dz in range(4) if dc or dz]
    peers += [(flip(d, bit + 1), z) for bit in range(chip_bits)]
    barrier = pltpu.get_barrier_semaphore()
    for dev in peers:
        pl.semaphore_signal(barrier, inc=1, device_id=dev, device_id_type=MESH)
    pl.semaphore_wait(barrier, len(peers))

    def swap_rows(src, dst_own, dst_other):
        i = sem()
        keep = pltpu.make_async_copy(src, dst_own, rsem.at[i])
        move = pltpu.make_async_remote_copy(
            src, dst_other, ssem.at[i], rsem.at[i], device_id=swap, device_id_type=MESH
        )

        @pl.when(k == zh)
        def _():
            keep.start()

        @pl.when(k != zh)
        def _():
            move.start()

        def finish_send():
            @pl.when(k != zh)
            def _():
                move.wait_send()

        sends.append(finish_send)
        return keep.wait

    def many(start, size):
        return pl.ds(pl.multiple_of(start, size), size)

    def block(b):
        return many(b * BLK, BLK)

    def half(h):
        return pl.ds(h * HALF, HALF)

    def spot(b, h):
        return many(h * 4 * HALF + b * HALF, HALF)

    def chunk(c):
        return many(c * BLK, BLK)

    def plain_rows(c):
        at = (c % 2) * 2 * BLK + (c // 2) * HALF
        return many(at, HALF), many(at + BLK, HALF)

    def plain(ref, c):
        one, two = plain_rows(c)
        return jnp.concatenate([ref[one, :], ref[two, :]], axis=0)

    def plain_store(ref, c, value):
        one, two = plain_rows(c)
        ref[one, :] = value[0:HALF]
        ref[two, :] = value[HALF:BLK]

    own_rows = pl.ds(pl.multiple_of(d * R, R), R)
    chip_rows = pl.ds(pl.multiple_of(j * (2 * R), 2 * R), 2 * R)
    slots = (0, 1 + zl, 2 - zl, 3 + zl, 4 - zl, 5, 6, 7)
    sources = {
        0: [(qkvw.at[0, n], n * 256, 256) for n in range(3)] + [(outT.at[0], 768, 256)],
        1: [(finw.at[0], 0, D)],
        3: [(foutT.at[0], 0, D)],
        5: [(qkvw.at[1, n], n * 256, 256) for n in range(3)] + [(outT.at[1], 768, 256)],
        6: [(finw.at[1], 0, D)],
        7: [(foutT.at[1], 0, D)],
    }

    def collect(item):
        arrived = p0r.at[item]
        holder = 2 * j + zh
        near, far = sem(), sem()
        for src, at, width in sources[item]:
            dst = W.at[slots[item], own_rows, pl.ds(at, width)]

            @pl.when(k == zh)
            def _(src=src, dst=dst):
                pltpu.make_async_copy(src, dst, arrived).start()

            @pl.when(k != zh)
            def _(src=src, dst=dst):
                pltpu.make_async_remote_copy(
                    src, dst, ssem.at[near], arrived, device_id=(holder, z), device_id_type=MESH
                ).start()

            pltpu.make_async_remote_copy(
                src, dst, ssem.at[far], arrived, device_id=(holder, swap[1]), device_id_type=MESH
            ).start()
        slab = W.at[slots[item], own_rows, :]

        def finish():
            @pl.when(k != zh)
            def _():
                pltpu.make_async_copy(slab, slab, ssem.at[near]).wait()

            pltpu.make_async_copy(slab, slab, ssem.at[far]).wait()

        sends.append(finish)

    passed = {}

    def arrive(item):
        slab = W.at[slots[item], chip_rows, :]
        if item in (2, 4):
            passed[item].wait_recv()
            return
        pltpu.make_async_copy(slab, slab, p0r.at[item]).wait()
        if item in (1, 3):
            passed[item + 1] = rcopy(slab, slab, zp, keep=True)

    half_cols = (pl.ds(0, D // 2), pl.ds(D // 2, D // 2))
    order = (tuple(range(chip_bits)), tuple(reversed(range(chip_bits))))
    stage_wait = {}

    def start_stage(item, stage):
        waits = []
        for half in range(2):
            bits = order[half]
            dev = (flip(d, bits[stage] + 1), z)
            i = sem()
            cols = half_cols[half]

            def send(m, bits=bits, cols=cols, dev=dev, i=i):
                chip = j
                for n, bit in enumerate(bits[:stage]):
                    chip = chip + ((m // (1 << n)) % 2) * (flip(j, bit) - j)
                ref = W.at[slots[item], pl.ds(pl.multiple_of(chip * (2 * R), 2 * R), 2 * R), cols]
                pltpu.make_async_remote_copy(
                    ref, ref, ssem.at[i], rsem.at[i], device_id=dev, device_id_type=MESH
                ).start()

            if stage <= 1:
                for m in range(1 << stage):
                    send(m)
            else:

                def body(m, carry, send=send):
                    send(m)
                    return carry

                lax.fori_loop(0, 1 << stage, body, 0)
            slab = W.at[slots[item], pl.ds(0, (1 << stage) * 2 * R), cols]
            waits.append(pltpu.make_async_copy(slab, slab, rsem.at[i]).wait)
            sends.append(pltpu.make_async_copy(slab, slab, ssem.at[i]).wait)
        stage_wait[item, stage] = waits

    def wait_stage(item, stage):
        for w in stage_wait[item, stage]:
            w()

    def first_stage(item):
        arrive(item)
        start_stage(item, 0)

    def later_stages(item):
        for stage in range(1, chip_bits):
            wait_stage(item, stage - 1)
            start_stage(item, stage)

    def ready(item):
        wait_stage(item, chip_bits - 1)

    def pump(n):
        later_stages(n)
        if n + 2 < PIECES:
            first_stage(n + 2)

    def share_heads():
        i = sem()
        mine = smp.at[z]
        for r in (1, 2, 3):
            pltpu.make_async_remote_copy(
                small_mp, mine, ssem.at[i], rsem.at[i], device_id=col(0, r), device_id_type=MESH
            ).start()
        pltpu.make_async_copy(small_mp, mine, rsem.at[i]).start()
        sends.append(pltpu.make_async_copy(smp.at[0:3], smp.at[0:3], ssem.at[i]).wait)
        return pltpu.make_async_copy(smp, smp, rsem.at[i]).wait

    def share_small():
        sdp[d] = small_dp[...]
        bits = tuple(range(1, chip_bits + 1)) + (0,)
        for stage, bit in enumerate(bits):
            i = sem()

            def send(m, carry=0, i=i, bit=bit, stage=stage):
                slot = d
                for n, b in enumerate(bits[:stage]):
                    slot = slot + ((m // (1 << n)) % 2) * (flip(d, b) - d)
                pltpu.make_async_remote_copy(
                    sdp.at[slot], sdp.at[slot], ssem.at[i], rsem.at[i],
                    device_id=(flip(d, bit), z), device_id_type=MESH,
                ).start()
                return carry

            if stage <= 2:
                for m in range(1 << stage):
                    send(m)
            else:
                lax.fori_loop(0, 1 << stage, send, 0)
            slab = sdp.at[pl.ds(0, 1 << stage)]
            pltpu.make_async_copy(slab, slab, rsem.at[i]).wait()
            sends.append(pltpu.make_async_copy(slab, slab, ssem.at[i]).wait)
        for n in range(ndp):
            vecs[:, n * R : (n + 1) * R] = sdp[n].astype(F32)[:, 0:R]

    def unpack_small():
        keep = lax.broadcasted_iota(jnp.int32, (16, 768), 0) < 8
        for layer in range(LAYERS):
            tile = smp[qi, 16 * layer : 16 * layer + 16, :].astype(F32)
            bpad[layer] = jnp.zeros((128, 768), BF)
            bpad[layer, 0:16, :] = jnp.where(keep, tile[:, 0:768], 0.0).astype(BF)
            bqkv[layer] = tile[8:9, 0:768]
            for q in range(4):
                b1[layer, q] = smp[q, 16 * layer : 16 * layer + 16, :].astype(F32)[9:10, :]

    def vec(layer, n):
        return vecs[layer * 6 + n : layer * 6 + n + 1, :]

    class Gather:
        def __init__(self, buf, h):
            mine = buf.at[spot(qi, h)]
            self.other = buf.at[spot(2 * k + 1 - zl, h)]
            self.to_z = rcopy(mine, mine, zp)
            self.to_s = rcopy(mine, mine, sib)

        def forward(self):
            self.to_z.wait_recv()
            self.fwd = rcopy(self.other, self.other, sib)

        def chip(self):
            self.to_s.wait_recv()

        def finish(self, chip=True):
            if chip:
                self.chip()
            self.fwd.wait_recv()
            for cp in (self.to_z, self.to_s, self.fwd):
                cp.wait_send()

    first_sums = (part, rs1, rs2s, rs2r)
    late_sums = (party, rs1y, rs2ys, rs2yr)

    class Scatter:
        def __init__(self, partial, h, buffers, dst, base=None):
            p, r1, r2s, r2r = buffers
            self.h, self.dst, self.r2r = h, dst, r2r
            p[h] = partial(2 * h + 1 - k).astype(BF)
            self.first = rcopy(p.at[h], r1.at[h], sib)
            own2[...] = partial(2 * h + k)
            self.first.wait_recv()
            away, here = many((1 - zl) * HALF, HALF), many(zl * HALF, HALF)
            r2s[h] = (own2[away, :] + r1[h, away, :].astype(F32)).astype(BF)
            self.second = rcopy(r2s.at[h], r2r.at[h], zp)
            total = own2[here, :] + r1[h, here, :].astype(F32)
            dst[half(h), :] = total if base is None else total + base(half(h))

        def finish(self):
            self.second.wait_recv()
            self.dst[half(self.h), :] += self.r2r[self.h].astype(F32)
            self.first.wait_send()
            self.second.wait_send()

    def by_rows(h, f):
        def body(c, carry):
            f(many(h * HALF + c * 64, 64), c * 64)
            return carry

        lax.fori_loop(0, HALF // 64, body, 0)

    def norm_into(src, h, layer, which, dst, start):
        gain, shift = vec(layer, 2 * which), vec(layer, 2 * which + 1)

        def f(rows, at):
            xhat, _ = normed(src[rows, :].astype(F32))
            dst[many(start + at, 64), :] = (xhat * gain + shift).astype(BF)

        by_rows(h, f)

    def spot_start(h):
        return h * 4 * HALF + qi * HALF

    tri = lax.broadcasted_iota(jnp.int32, (BLK, BLK), 0) <= lax.broadcasted_iota(
        jnp.int32, (BLK, BLK), 1
    )
    lane_head = lax.broadcasted_iota(jnp.int32, (1, BLK), 1) // HD

    def project(layer, h):
        w = W.at[ATTENTION[layer]]

        def body(core, carry):
            c = 2 * h + core
            n = n1[layer, chunk(c), :]
            t = nn(n, apad[layer]).astype(BF)
            low[layer, chunk(c), :] = t
            pr = nn(n, w[:, 0:768]) + bqkv[layer] + nn(t, bpad[layer])
            pr = pr.astype(BF)
            plain_store(q_ref.at[layer], c, pr[:, 0:256])
            plain_store(k_ref.at[layer], c, pr[:, 256:512])
            v = pr[:, 512:768]
            plain_store(v_ref.at[layer], c, v)
            vt = v.astype(F32).T.astype(BF)
            one, two = plain_rows(c)
            tr[:, one] = vt[:, 0:HALF]
            tr[:, two] = vt[:, HALF:BLK]
            return carry

        lax.fori_loop(0, 2, body, 0)

    def attend(layer, i):
        lo = i * BLK
        kk, qq = k_ref.at[layer], q_ref.at[layer]

        def pair(hp, carry):
            for s in range(2):
                h = hp * 2 + s
                qm = qq[lo : lo + BLK, :] * jnp.where(lane_head == h, 0.125, 0.0).astype(BF)
                head = pl.ds(pl.multiple_of(h * HD, HD), HD)
                sd = jnp.where(tri, nt(kk[lo : lo + BLK, :], qm), NEG)
                top = jnp.max(sd, axis=0, keepdims=True)
                if i:
                    sa = nt(kk[0:lo, :], qm)
                    top = jnp.maximum(top, jnp.max(sa, axis=0, keepdims=True))
                ed = jnp.exp(sd - top)
                total = jnp.sum(ed, axis=0, keepdims=True)
                o = nn(tr[head, lo : lo + BLK], ed.astype(BF))
                if i:
                    ea = jnp.exp(sa - top)
                    total = total + jnp.sum(ea, axis=0, keepdims=True)
                    o = o + nn(tr[head, 0:lo], ea.astype(BF))
                ctxT[head, :] = o / total
                lse[layer, pl.ds(h, 1), lo : lo + BLK] = top + jnp.log(total)
            return carry

        lax.fori_loop(0, 2, pair, 0)
        ctx[lo : lo + BLK, :] = ctxT[...].T.astype(BF)

    def attend_back(layer, i):
        lo = i * BLK
        kk, qq, vv = k_ref.at[layer], q_ref.at[layer], v_ref.at[layer]

        def pair(hp, carry):
            for s in range(2):
                h = hp * 2 + s
                on = lane_head == h
                qm = qq[lo : lo + BLK, :] * jnp.where(on, 0.125, 0.0).astype(BF)
                gm = gctx[lo : lo + BLK, :] * jnp.where(on, 1.0, 0.0).astype(BF)
                head = pl.ds(pl.multiple_of(h * HD, HD), HD)
                ls = lse[layer, pl.ds(h, 1), lo : lo + BLK]
                spans = [(lo, lo + BLK)] + ([(0, lo)] if i else [])
                ps, ts = [], []
                for a, b in spans:
                    p = jnp.exp(nt(kk[a:b, :], qm) - ls)
                    if a == lo:
                        p = jnp.where(tri, p, 0.0)
                    ps.append(p)
                    ts.append(p * nt(vv[a:b, :], gm))
                dsum = sum(jnp.sum(t, axis=0, keepdims=True) for t in ts)
                o = None
                for (a, b), p, t in zip(spans, ps, ts):
                    gs = (t - p * dsum).astype(BF)
                    dv = nn(p.astype(BF), gm)
                    dk = nn(gs, qm)
                    for c in range(a // BLK, b // BLK):
                        at = pl.ds(c * BLK, BLK)
                        gv[:, at] += dv[c * BLK - a : (c + 1) * BLK - a]
                        gk[:, at] += dk[c * BLK - a : (c + 1) * BLK - a]
                    dq = nn(tr[head, a:b], gs)
                    o = dq if o is None else o + dq
                ctxT[head, :] = o * 0.125
            return carry

        lax.fori_loop(0, 2, pair, 0)
        gqkv[lo : lo + BLK, 0:256] = ctxT[...].T.astype(BF)

    def out_partial(layer):
        w = W.at[ATTENTION[layer]]
        return lambda c: nt(plain(ctx, c), w[:, 768:1024])

    heads_here = share_heads()
    x_here = [swap_rows(x_in.at[half(h)], x0.at[half(h)], x0.at[half(h)]) for h in range(2)]
    outT[0] = outw[0].astype(F32).T.astype(BF)
    collect(0)
    collect(1)
    share_small()
    outT[1] = outw[1].astype(F32).T.astype(BF)
    for layer in range(LAYERS):
        foutT[layer] = foutw[layer].astype(F32).T.astype(BF)
    heads_here()
    unpack_small()
    ag = []
    for h in range(2):
        x_here[h]()
        norm_into(x0, h, 0, 0, n1.at[0], spot_start(h))
        ag.append(Gather(n1.at[0], h))
    first_stage(0)
    ag[0].forward()
    ag[1].forward()
    later_stages(0)
    first_stage(1)
    collect(3)
    ag[0].finish()
    ag[1].finish()
    first_stage(2)
    pump(1)
    ready(0)
    project(0, 0)
    project(0, 1)
    collect(5)
    attend(0, 0)
    attend(0, 1)
    attend(0, 2)
    pump(2)
    attend(0, 3)
    sums = [Scatter(out_partial(0), h, first_sums, acc) for h in range(2)]
    nx = []
    for h in range(2):
        sums[h].finish()
        m1[0, half(h), :] = x0[half(h), :].astype(F32) + acc[half(h), :] + vec(0, 4)
        norm_into(m1.at[0], h, 0, 1, nx0.at[h], k * HALF)
        mine = nx0.at[h, many(k * HALF, HALF)]
        nx.append(rcopy(mine, mine, sib))
    pump(3)
    collect(6)
    cot_here = [
        swap_rows(
            cot_in.at[half(h)], gmx.at[spot(qi, h)], gmx.at[spot(2 * (1 - k) + zl, h)]
        )
        for h in range(2)
    ]
    for cp in nx:
        cp.wait_recv()

    def hidden0(s):
        def body(c, carry):
            h, hc = c // 2, c % 2
            cols = many(hc * 512, 512)
            u = nn(nx0[h], W[1 + s, :, cols]) + b1[0, 2 * k + s, :, cols]
            u0[h, s, :, cols] = u.astype(BF)
            act[2 * h + s, :, cols] = gelu(u).astype(BF)
            return carry

        lax.fori_loop(0, 4, body, 0)

    ready(1)
    hidden0(zl)
    ready(2)
    hidden0(1 - zl)
    for cp in nx:
        cp.wait_send()
    pump(4)
    collect(7)
    ready(3)
    pump(5)
    ready(4)

    def share0(h, value):
        own2[...] = value
        sy[h] = own2[many((1 - k) * HALF, HALF), :].astype(BF)
        cp = rcopy(sy.at[h], syr.at[h], sib)
        acc[half(h), :] = own2[many(k * HALF, HALF), :]

        def finish():
            cp.wait_recv()
            acc[half(h), :] += syr[h].astype(F32)
            cp.wait_send()

        return finish

    ag = []
    ends = [share0(h, nt(act[2 * h], W[3]) + nt(act[2 * h + 1], W[4])) for h in range(2)]
    for h in range(2):
        ends[h]()
        x1[half(h), :] = m1[0, half(h), :] + acc[half(h), :] + vec(0, 5)
        norm_into(x1, h, 1, 0, n1.at[1], spot_start(h))
        ag.append(Gather(n1.at[1], h))
    pump(6)
    ag[0].forward()
    ag[0].finish()
    ready(5)
    project(1, 0)
    ag[1].forward()
    ag[1].finish()
    project(1, 1)
    pump(7)
    for h in range(2):
        cot_here[h]()
    gm = [Gather(gmx, h) for h in range(2)]
    attend(1, 0)
    attend(1, 1)
    attend(1, 2)
    gm[0].forward()
    attend(1, 3)
    gm[1].forward()
    sums = [Scatter(out_partial(1), h, first_sums, acc) for h in range(2)]
    ag = []
    for h in range(2):
        sums[h].finish()
        m1[1, half(h), :] = x1[half(h), :] + acc[half(h), :] + vec(1, 4)
        norm_into(m1.at[1], h, 1, 1, ga, spot_start(h))
        ag.append(Gather(ga, h))
    gm[0].finish()
    gm[1].finish()
    ready(6)

    def hidden1(h):
        def body(i, carry):
            c, hc = 2 * h + i // 2, i % 2
            cols = many(hc * 512, 512)
            u = nn(ga[chunk(c), :], W[6, :, cols]) + b1[1, qi, :, cols]
            u1[c, :, cols] = u.astype(BF)
            act[c, :, cols] = gelu(u).astype(BF)
            return carry

        lax.fori_loop(0, 4, body, 0)

    def feed_back1(c):
        gh = nn(gmx[chunk(c), :], W[7])
        gu = (gh * gelu_slope(u1[c].astype(F32))).astype(BF)
        return nt(gu, W[6])

    sums = []
    for h in range(2):
        ag[h].forward()
        ag[h].finish()
        hidden1(h)
        if h == 0:
            ready(7)
        sums.append(Scatter(feed_back1, h, first_sums, acc))

    def mid_back(layer, h, g_rows):
        gain = vec(layer, 2)

        def f(rows, at):
            v = g_rows(rows, at) + norm_back(m1[layer, rows, :], acc[rows, :], gain)
            gmid[rows, :] = v
            ga[many(spot_start(h) + at, 64), :] = v.astype(BF)

        by_rows(h, f)

    hops = [sib, zp, col(0, 2)] + [(flip(d, b), z) for b in range(1, chip_bits + 1)]

    def reduce_all(layer):
        flight = []

        def hop():
            n = len(flight)
            if n:
                if n > len(hops):
                    return
                flight[-1].wait_recv()
                total = gsend[layer, n - 1] + grecv[layer, n - 1]
                if n == len(hops):
                    G[16 * layer : 16 * layer + 16, :] = total
                    flight.append(None)
                    return
                gsend[layer, n] = total
            flight.append(rcopy(gsend.at[layer, n], grecv.at[layer, n], hops[n], keep=True))

        return hop

    def turn(layer):
        def body(c, carry):
            tr[:, block(c)] = k_ref[layer, block(c), :].astype(F32).T.astype(BF)
            return carry

        lax.fori_loop(0, 4, body, 0)

    def attention_back(layer, ag, extra, hop):
        w = W.at[ATTENTION[layer]]

        def down(b):
            rows = jnp.concatenate([ga[spot(b, 0), :], ga[spot(b, 1), :]], axis=0)
            gctx[block(b), :] = nn(rows, w[:, 768:1024]).astype(BF)

        def back(mine, upper):
            for zz in range(2):
                i = 2 * upper + (zz if mine else 1 - zz)

                @pl.when(zl == zz)
                def _(i=i):
                    attend_back(layer, i)

        gk[...] = jnp.zeros_like(gk)
        gv[...] = jnp.zeros_like(gv)
        ag[0].chip()
        ag[1].chip()
        down(zl)
        down(2 + zl)
        back(True, 1)
        ag[0].forward()
        back(True, 0)
        hop()
        ag[1].forward()
        ag[0].finish(False)
        ag[1].finish(False)
        extra()
        down(1 - zl)
        down(3 - zl)
        back(False, 1)
        back(False, 0)
        hop()

        def lows(c, carry):
            gqkv[block(c), 256:512] = gk[:, block(c)].astype(BF)
            gqkv[block(c), 512:768] = gv[:, block(c)].astype(BF)
            gt_ref[block(c), :] = nt(gqkv[block(c), :], bpad[layer]).astype(BF)
            return carry

        lax.fori_loop(0, 4, lows, 0)
        sums = [
            Scatter(
                lambda c: nt(plain(gqkv, c), w[:, 0:768]) + nt(plain(gt_ref, c), apad[layer]),
                h, first_sums, acc,
            )
            for h in range(2)
        ]

        def grads(c, carry):
            ga_sum, gb_sum = carry
            gtt = plain(gt_ref, c).astype(F32).T[0:16, :].astype(BF)
            tt = low[layer, chunk(c), :].astype(F32).T[0:16, :].astype(BF)
            return (
                ga_sum + nn(gtt, n1[layer, chunk(c), :]),
                gb_sum + nn(tt, plain(gqkv, c)),
            )

        ga_sum, gb_sum = lax.fori_loop(
            0, 4, grads, (jnp.zeros((16, D), F32), jnp.zeros((16, 768), F32))
        )
        gb = ADAPTER_SCALE * jnp.where(
            lax.broadcasted_iota(jnp.int32, (8, 256), 0) < 4, gb_sum[0:8, 0:256], gb_sum[0:8, 512:768]
        )
        gsend[layer, 0, 0:8, :] = ga_sum[0:8, :]
        gsend[layer, 0, 8:16, :] = jnp.zeros((8, D), F32)
        gsend[layer, 0, 8:16, many(qi * 256, 256)] = gb
        step = reduce_all(layer)
        step()
        return sums, step

    def step_back(layer, h, src):
        gain = vec(layer, 0)

        def f(rows, at):
            g_ref[rows, :] = gmid[rows, :] + norm_back(src[rows, :].astype(F32), acc[rows, :], gain)

        by_rows(h, f)

    turn(1)
    ag = []
    for h in range(2):
        sums[h].finish()
        mid_back(
            1, h, lambda rows, at, h=h: gmx[many(spot_start(h) + at, 64), :].astype(F32)
        )
        ag.append(Gather(ga, h))
    late = []

    def first_output():
        for h in range(2):
            late.append(
                Scatter(
                    lambda c: nt(act[c], W[7]), h, late_sums, m1.at[1],
                    lambda rows: m1[1, rows, :] + vec(1, 5),
                )
            )

    sums, hop1 = attention_back(1, ag, first_output, lambda: None)

    def feed_back0(h):
        total = None
        for s in range(2):
            gh = nn(nx0[h], W[3 + s])
            gu = (gh * gelu_slope(u0[h, s].astype(F32))).astype(BF)
            y = nt(gu, W[1 + s])
            total = y if total is None else total + y
        return total

    def next_rows(h):
        sums[h].finish()
        step_back(1, h, x1)
        nx0[h, many(k * HALF, HALF), :] = g_ref[half(h), :].astype(BF)
        mine = nx0.at[h, many(k * HALF, HALF)]
        return rcopy(mine, mine, sib)

    def after(h):
        ends[h]()
        mid_back(0, h, lambda rows, at: g_ref[rows, :])
        ag.append(Gather(ga, h))

    ag, ends = [], []
    nx = [next_rows(0)]
    turn(0)
    hop1()
    nx[0].wait_recv()
    ends.append(share0(0, feed_back0(0)))
    nx.append(next_rows(1))
    after(0)
    nx[1].wait_recv()
    ends.append(share0(1, feed_back0(1)))
    after(1)
    hop1()
    for cp in nx:
        cp.wait_send()
    out_here = []
    for h in range(2):
        late[h].finish()
        party[0, half(h), :] = m1[1, half(h), :].astype(BF)
        out_here.append(swap_rows(party.at[0, half(h)], out_ref.at[half(h)], out_ref.at[half(h)]))
    sums, hop0 = attention_back(0, ag, lambda: None, hop1)
    gin_here = []
    hop0()
    for h in range(2):
        sums[h].finish()
        step_back(0, h, x0)
        party[1, half(h), :] = g_ref[half(h), :].astype(BF)
        gin_here.append(swap_rows(party.at[1, half(h)], gin_ref.at[half(h)], gin_ref.at[half(h)]))
        hop0()
    for _ in range(len(hops)):
        hop1()
        hop0()
    for h in range(2):
        out_here[h]()
        gin_here[h]()
    for w in sends:
        w()


def shards(
    inputs, qkv_w, qkv_b, out_w, out_b, fin_w, fin_b, fout_w, fout_b, gains, shifts, first, second,
    cotangent,
):
    ndp = lax.axis_size("dp")
    R = qkv_w.shape[1]
    hops = ndp.bit_length() - 1 + 2
    small_dp = jnp.stack(
        [gains[:, 0], shifts[:, 0], gains[:, 1], shifts[:, 1], out_b, fout_b], axis=1
    ).reshape(LAYERS * 6, R)
    small_dp = jnp.pad(small_dp, ((0, 16 - LAYERS * 6), (0, 128 - R)))
    up = second * jnp.asarray(ADAPTER_SCALE, BF)
    small_mp = jnp.concatenate(
        [
            jnp.pad(up[:, 0], ((0, 0), (0, 0), (0, 768))),
            jnp.pad(up[:, 1], ((0, 0), (0, 0), (512, 256))),
            jnp.pad(qkv_b.reshape(LAYERS, 1, 768), ((0, 0), (0, 0), (0, 256))),
            jnp.pad(fin_b[:, None], ((0, 0), (0, 6), (0, 0))),
        ],
        axis=1,
    ).reshape(LAYERS * 16, D)
    apad = jnp.concatenate(
        [first[:, 0], first[:, 1], jnp.zeros((LAYERS, D, 120), BF)], axis=2
    )
    anyspec = pl.BlockSpec(memory_space=pl.ANY)
    vm = pl.BlockSpec(memory_space=pltpu.VMEM)
    V = pltpu.VMEM
    scratch = [
        V((PIECES, D, D), BF),
        V((LAYERS, D, D), BF),
        V((D, D), BF),
        V((D, D), BF),
        V((LAYERS, D, 256), BF),
        V((LAYERS, D, 256), BF),
        V((LAYERS, D, 256), BF),
        V((256, D), BF),
        V((LAYERS, D, 128), BF),
        V((BLK, D), BF),
        V((BLK, D), F32),
        V((LAYERS, BLK, D), F32),
        V((2, 2, BLK, D), BF),
        V((4, BLK, D), BF),
        V((4, BLK, D), BF),
        V((D, 256), BF),
        V((D, 256), BF),
        V((256, 256), F32),
        V((2, BLK, D), BF),
        V((2, BLK, D), BF),
        V((2, HALF, D), BF),
        V((2, HALF, D), BF),
        V((2, BLK, D), BF),
        V((2, BLK, D), BF),
        V((2, HALF, D), BF),
        V((2, HALF, D), BF),
        V((2, BLK, D), BF),
        V((2, HALF, D), BF),
        V((2, HALF, D), BF),
        V((D, 768), BF),
        V((D, 128), BF),
        V((BLK, D), F32),
        V((BLK, D), F32),
        V((BLK, D), F32),
        V((BLK, D), F32),
        V((LAYERS, hops, 16, D), F32),
        V((LAYERS, hops, 16, D), F32),
        V((LAYERS, 8, D), F32),
        V((LAYERS, R, 256), BF),
        V((LAYERS, R, D), BF),
        V((ndp, 16, 128), BF),
        V((4, 32, D), BF),
        V((16, D), F32),
        V((LAYERS, 128, 768), BF),
        V((LAYERS, 1, 768), F32),
        V((LAYERS, 4, 1, D), F32),
        pltpu.SemaphoreType.DMA((200,)),
        pltpu.SemaphoreType.DMA((200,)),
        pltpu.SemaphoreType.DMA((PIECES,)),
    ]
    out, gin, G = pl.pallas_call(
        functools.partial(kernel, ndp),
        out_shape=(
            jax.ShapeDtypeStruct((BLK, D), BF),
            jax.ShapeDtypeStruct((BLK, D), BF),
            jax.ShapeDtypeStruct((32, D), F32),
        ),
        in_specs=[anyspec, anyspec, anyspec, anyspec, vm, vm, vm, vm, vm],
        out_specs=(anyspec, anyspec, vm),
        scratch_shapes=scratch,
        compiler_params=pltpu.CompilerParams(
            collective_id=0, has_side_effects=True, vmem_limit_bytes=63 * 2**20
        ),
        name="two_blocks",
    )(inputs, cotangent, jnp.swapaxes(qkv_w, 1, 2), fin_w, out_w, fout_w, apad, small_dp, small_mp)
    G = G.reshape(LAYERS, 16, D)
    grad_a = jnp.swapaxes(G[:, 0:8].reshape(LAYERS, 2, 4, D), 2, 3)
    grad_b = G[:, 8:16].reshape(LAYERS, 2, 4, D)
    return (out, gin, grad_a, grad_b)


def solution(mesh):
    placed = (
        P(("dp", "mp"), None),
        P(None, "dp", None, "mp"),
        P(None, None, "mp"),
        P(None, "mp", "dp"),
        P(None, "dp"),
        P(None, "dp", "mp"),
        P(None, "mp"),
        P(None, "mp", "dp"),
        P(None, "dp"),
        P(None, None, "dp"),
        P(None, None, "dp"),
        P(),
        P(None, None, None, "mp"),
        P(("dp", "mp"), None),
    )
    return jax.shard_map(
        shards,
        mesh=mesh,
        in_specs=placed,
        out_specs=(P(("dp", "mp"), None), P(("dp", "mp"), None), P(), P()),
        check_vma=False,
    )
```

```python
import functools

import jax
import jax.numpy as jnp
from jax import lax
from jax.experimental import pallas as pl
from jax.experimental.pallas import tpu as pltpu
from jax.sharding import PartitionSpec as P

MESH = pl.DeviceIdType.MESH
F32 = jnp.float32
BF = jnp.bfloat16
D = 1024
BLK = 256
HALF = 128
HD = 64
LAYERS = 2
NORM_EPS = 1e-05
ADAPTER_SCALE = 8.0
C0 = 0.7978845608
C1 = 0.044715
NEG = -1e30

ATTENTION = (0, 5)
PIECES = 8


def nt(a, b):
    return lax.dot_general(a, b, (((1,), (1,)), ((), ())), preferred_element_type=F32)


def nn(a, b):
    return lax.dot_general(a, b, (((1,), (0,)), ((), ())), preferred_element_type=F32)


def flip(value, bit):
    return value + (1 << bit) * (1 - 2 * ((value // (1 << bit)) % 2))


def gelu(u):
    return 0.5 * u * (1.0 + jnp.tanh(C0 * (u + C1 * u * u * u)))


def gelu_slope(u):
    square = u * u
    th = jnp.tanh(C0 * u * (1.0 + C1 * square))
    return 0.5 * (1.0 + th) + 0.5 * u * (1.0 - th * th) * (C0 * (1.0 + 3.0 * C1 * square))


def normed(x):
    c = x - jnp.mean(x, axis=-1, keepdims=True)
    rstd = lax.rsqrt(jnp.mean(c * c, axis=-1, keepdims=True) + NORM_EPS)
    return c * rstd, rstd


def norm_back(x, grad, gain):
    xhat, rstd = normed(x)
    gx = grad * gain
    return rstd * (
        gx
        - jnp.mean(gx, axis=-1, keepdims=True)
        - xhat * jnp.mean(gx * xhat, axis=-1, keepdims=True)
    )


def kernel(
    ndp,
    x_in, cot_in, qkvw, finw, outw, foutw, apad, small_dp, small_mp,
    out_ref, gin_ref, G,
    W, n1, ga, gmx, q_ref, k_ref, v_ref, tr, low, x0, x1, m1, u0, u1, act, ctx, gctx, ctxT,
    part, rs1, rs2s, rs2r, party, rs1y, rs2ys, rs2yr, nx0, sy, syr, gqkv, gt_ref,
    acc, g_ref, gmid, own2, gsend, grecv, lse, outT, foutT, sdp, smp, vecs, bpad, bqkv, b1,
    ssem, rsem, p0r,
):
    R = finw.shape[1]
    gk, gv = acc, g_ref
    d = lax.axis_index("dp")
    z = lax.axis_index("mp")
    k = d % 2
    j = d // 2
    zl = z % 2
    zh = z // 2
    qi = 2 * k + zl
    chip_bits = (ndp // 2).bit_length() - 1

    def col(dc, dz):
        zz = z
        if dz & 1:
            zz = zz + 1 - 2 * zl
        if dz & 2:
            zz = zz + 2 - 4 * zh
        return (d + 1 - 2 * k if dc else d, zz)

    sib, zp, swap = col(1, 0), col(0, 1), col(1, 2)
    count = [0]
    sends = []

    def sem():
        count[0] += 1
        return count[0] - 1

    def rcopy(src, dst, dev, keep=False):
        i = sem()
        cp = pltpu.make_async_remote_copy(
            src, dst, ssem.at[i], rsem.at[i], device_id=dev, device_id_type=MESH
        )
        cp.start()
        if keep:
            sends.append(cp.wait_send)
        return cp

    peers = [col(dc, dz) for dc in range(2) for dz in range(4) if dc or dz]
    peers += [(flip(d, bit + 1), z) for bit in range(chip_bits)]
    barrier = pltpu.get_barrier_semaphore()
    for dev in peers:
        pl.semaphore_signal(barrier, inc=1, device_id=dev, device_id_type=MESH)
    pl.semaphore_wait(barrier, len(peers))

    def swap_rows(src, dst_own, dst_other):
        i = sem()
        keep = pltpu.make_async_copy(src, dst_own, rsem.at[i])
        move = pltpu.make_async_remote_copy(
            src, dst_other, ssem.at[i], rsem.at[i], device_id=swap, device_id_type=MESH
        )

        @pl.when(k == zh)
        def _():
            keep.start()

        @pl.when(k != zh)
        def _():
            move.start()

        def finish_send():
            @pl.when(k != zh)
            def _():
                move.wait_send()

        sends.append(finish_send)
        return keep.wait

    def many(start, size):
        return pl.ds(pl.multiple_of(start, size), size)

    def block(b):
        return many(b * BLK, BLK)

    def half(h):
        return pl.ds(h * HALF, HALF)

    def spot(b, h):
        return many(h * 4 * HALF + b * HALF, HALF)

    def chunk(c):
        return many(c * BLK, BLK)

    def plain_rows(c):
        at = (c % 2) * 2 * BLK + (c // 2) * HALF
        return many(at, HALF), many(at + BLK, HALF)

    def plain(ref, c):
        one, two = plain_rows(c)
        return jnp.concatenate([ref[one, :], ref[two, :]], axis=0)

    def plain_store(ref, c, value):
        one, two = plain_rows(c)
        ref[one, :] = value[0:HALF]
        ref[two, :] = value[HALF:BLK]

    own_rows = pl.ds(pl.multiple_of(d * R, R), R)
    chip_rows = pl.ds(pl.multiple_of(j * (2 * R), 2 * R), 2 * R)
    slots = (0, 1 + zl, 2 - zl, 3 + zl, 4 - zl, 5, 6, 7)
    sources = {
        0: [(qkvw.at[0, n], n * 256, 256) for n in range(3)] + [(outT.at[0], 768, 256)],
        1: [(finw.at[0], 0, D)],
        3: [(foutT.at[0], 0, D)],
        5: [(qkvw.at[1, n], n * 256, 256) for n in range(3)] + [(outT.at[1], 768, 256)],
        6: [(finw.at[1], 0, D)],
        7: [(foutT.at[1], 0, D)],
    }

    holder = 2 * j + zh
    home = k == zh

    def near(item):
        arrived = p0r.at[item]
        i = sem()
        for src, at, width in sources[item]:
            dst = W.at[slots[item], own_rows, pl.ds(at, width)]

            @pl.when(home)
            def _(src=src, dst=dst):
                pltpu.make_async_copy(src, dst, arrived).start()

            @pl.when(jnp.logical_not(home))
            def _(src=src, dst=dst):
                pltpu.make_async_remote_copy(
                    src, dst, ssem.at[i], arrived, device_id=(holder, z), device_id_type=MESH
                ).start()

        slab = W.at[slots[item], own_rows, :]

        def finish():
            @pl.when(jnp.logical_not(home))
            def _():
                pltpu.make_async_copy(slab, slab, ssem.at[i]).wait()

        sends.append(finish)

    def far(item):
        i = sem()
        for src, at, width in sources[item]:
            dst = W.at[slots[item], own_rows, pl.ds(at, width)]
            pltpu.make_async_remote_copy(
                src, dst, ssem.at[i], p0r.at[item], device_id=(holder, swap[1]), device_id_type=MESH
            ).start()
        slab = W.at[slots[item], own_rows, :]
        sends.append(pltpu.make_async_copy(slab, slab, ssem.at[i]).wait)

    pass_sem = {1: sem(), 3: sem()}

    def passing(item):
        slab = W.at[slots[item], chip_rows, :]
        i = pass_sem[item]
        return pltpu.make_async_remote_copy(
            slab, slab, ssem.at[i], rsem.at[i], device_id=zp, device_id_type=MESH
        )

    def pass_on(item):
        passing(item).start()

    for item in pass_sem:
        sends.append(passing(item).wait_send)

    def arrive(item):
        if item in (2, 4):
            passing(item - 1).wait_recv()
            return
        slab = W.at[slots[item], chip_rows, :]
        pltpu.make_async_copy(slab, slab, p0r.at[item]).wait()

    half_cols = (pl.ds(0, D // 2), pl.ds(D // 2, D // 2))
    order = (tuple(range(chip_bits)), tuple(reversed(range(chip_bits))))
    stage_sem = {
        (item, stage): (sem(), sem()) for item in range(PIECES) for stage in range(chip_bits)
    }

    def stage_slabs(item, stage):
        for cols, i in zip(half_cols, stage_sem[item, stage]):
            yield W.at[slots[item], pl.ds(0, (1 << stage) * 2 * R), cols], i

    for item, stage in stage_sem:
        for slab, i in stage_slabs(item, stage):
            sends.append(pltpu.make_async_copy(slab, slab, ssem.at[i]).wait)

    def start_stage(item, stage):
        for cols, bits, i in zip(half_cols, order, stage_sem[item, stage]):
            dev = (flip(d, bits[stage] + 1), z)

            def send(m, carry=0, bits=bits, cols=cols, dev=dev, i=i):
                chip = j
                for n, bit in enumerate(bits[:stage]):
                    chip = chip + ((m // (1 << n)) % 2) * (flip(j, bit) - j)
                ref = W.at[slots[item], pl.ds(pl.multiple_of(chip * (2 * R), 2 * R), 2 * R), cols]
                pltpu.make_async_remote_copy(
                    ref, ref, ssem.at[i], rsem.at[i], device_id=dev, device_id_type=MESH
                ).start()
                return carry

            if stage <= 1:
                for m in range(1 << stage):
                    send(m)
            else:
                lax.fori_loop(0, 1 << stage, send, 0)

    def wait_stage(item, stage):
        for slab, i in stage_slabs(item, stage):
            pltpu.make_async_copy(slab, slab, rsem.at[i]).wait()

    def first(*items):
        for item in items:
            arrive(item)
            start_stage(item, 0)

    def later(*items):
        for item in items:
            for stage in range(1, chip_bits):
                wait_stage(item, stage - 1)
                start_stage(item, stage)

    def ready(item):
        wait_stage(item, chip_bits - 1)

    def at_home(f):
        pl.when(home)(f)

    def away(f):
        pl.when(jnp.logical_not(home))(f)

    def share_heads():
        i = sem()
        mine = smp.at[zl]
        copies = [
            pltpu.make_async_remote_copy(
                small_mp, mine, ssem.at[i], rsem.at[i], device_id=col(0, r), device_id_type=MESH
            )
            for r in (1, 2, 3)
        ]
        slab = W.at[0, pl.ds(0, 3 * 32), :]

        @at_home
        def _():
            for cp in copies:
                cp.start()
            pltpu.make_async_copy(small_mp, mine, rsem.at[i]).start()

        def finish():
            at_home(pltpu.make_async_copy(slab, slab, ssem.at[i]).wait)

        sends.append(finish)
        return pltpu.make_async_copy(smp, smp, rsem.at[i]).wait

    def share_small():
        sdp[d] = small_dp[...]
        bits = tuple(range(1, chip_bits + 1)) + (0,)
        for stage, bit in enumerate(bits):
            i = sem()

            def send(m, carry=0, i=i, bit=bit, stage=stage):
                slot = d
                for n, b in enumerate(bits[:stage]):
                    slot = slot + ((m // (1 << n)) % 2) * (flip(d, b) - d)
                pltpu.make_async_remote_copy(
                    sdp.at[slot], sdp.at[slot], ssem.at[i], rsem.at[i],
                    device_id=(flip(d, bit), z), device_id_type=MESH,
                ).start()
                return carry

            if stage <= 2:
                for m in range(1 << stage):
                    send(m)
            else:
                lax.fori_loop(0, 1 << stage, send, 0)
            slab = sdp.at[pl.ds(0, 1 << stage)]
            pltpu.make_async_copy(slab, slab, rsem.at[i]).wait()
            sends.append(pltpu.make_async_copy(slab, slab, ssem.at[i]).wait)
        for n in range(ndp):
            vecs[:, n * R : (n + 1) * R] = sdp[n].astype(F32)[:, 0:R]

    def unpack_small():
        keep = lax.broadcasted_iota(jnp.int32, (16, 768), 0) < 8
        for layer in range(LAYERS):
            tile = smp[zl, 16 * layer : 16 * layer + 16, :].astype(F32)
            bpad[layer] = jnp.zeros((128, 768), BF)
            bpad[layer, 0:16, :] = jnp.where(keep, tile[:, 0:768], 0.0).astype(BF)
            bqkv[layer] = tile[8:9, 0:768]
            for s in range(2):
                b1[layer, s] = smp[s, 16 * layer : 16 * layer + 16, :].astype(F32)[9:10, :]

    def vec(layer, n):
        return vecs[layer * 6 + n : layer * 6 + n + 1, :]

    class Gather:
        def __init__(self, buf, h):
            mine = buf.at[spot(qi, h)]
            self.other = buf.at[spot(2 * k + 1 - zl, h)]
            self.to_z = rcopy(mine, mine, zp)
            self.to_s = rcopy(mine, mine, sib)

        def forward(self):
            self.to_z.wait_recv()
            self.fwd = rcopy(self.other, self.other, sib)

        def chip(self):
            self.to_s.wait_recv()

        def finish(self, chip=True):
            if chip:
                self.chip()
            self.fwd.wait_recv()
            for cp in (self.to_z, self.to_s, self.fwd):
                cp.wait_send()

    first_sums = (part, rs1, rs2s, rs2r)
    late_sums = (party, rs1y, rs2ys, rs2yr)

    class Scatter:
        def __init__(self, partial, h, buffers, dst, base=None):
            p, r1, r2s, r2r = buffers
            self.h, self.dst, self.r2r = h, dst, r2r
            p[h] = partial(2 * h + 1 - k).astype(BF)
            self.first = rcopy(p.at[h], r1.at[h], sib)
            own2[...] = partial(2 * h + k)
            self.first.wait_recv()
            away, here = many((1 - zl) * HALF, HALF), many(zl * HALF, HALF)
            r2s[h] = (own2[away, :] + r1[h, away, :].astype(F32)).astype(BF)
            self.second = rcopy(r2s.at[h], r2r.at[h], zp)
            total = own2[here, :] + r1[h, here, :].astype(F32)
            dst[half(h), :] = total if base is None else total + base(half(h))

        def finish(self):
            self.second.wait_recv()
            self.dst[half(self.h), :] += self.r2r[self.h].astype(F32)
            self.first.wait_send()
            self.second.wait_send()

    def by_rows(h, f):
        def body(c, carry):
            f(many(h * HALF + c * 64, 64), c * 64)
            return carry

        lax.fori_loop(0, HALF // 64, body, 0)

    def norm_into(src, h, layer, which, dst, start):
        gain, shift = vec(layer, 2 * which), vec(layer, 2 * which + 1)

        def f(rows, at):
            xhat, _ = normed(src[rows, :].astype(F32))
            dst[many(start + at, 64), :] = (xhat * gain + shift).astype(BF)

        by_rows(h, f)

    def spot_start(h):
        return h * 4 * HALF + qi * HALF

    tri = lax.broadcasted_iota(jnp.int32, (BLK, BLK), 0) <= lax.broadcasted_iota(
        jnp.int32, (BLK, BLK), 1
    )
    lane_head = lax.broadcasted_iota(jnp.int32, (1, BLK), 1) // HD

    def project(layer, h):
        w = W.at[ATTENTION[layer]]

        def body(core, carry):
            c = 2 * h + core
            n = n1[layer, chunk(c), :]
            t = nn(n, apad[layer]).astype(BF)
            low[layer, chunk(c), :] = t
            pr = nn(n, w[:, 0:768]) + bqkv[layer] + nn(t, bpad[layer])
            pr = pr.astype(BF)
            plain_store(q_ref.at[layer], c, pr[:, 0:256])
            plain_store(k_ref.at[layer], c, pr[:, 256:512])
            v = pr[:, 512:768]
            plain_store(v_ref.at[layer], c, v)
            vt = v.astype(F32).T.astype(BF)
            one, two = plain_rows(c)
            tr[:, one] = vt[:, 0:HALF]
            tr[:, two] = vt[:, HALF:BLK]
            return carry

        lax.fori_loop(0, 2, body, 0)

    def attend(layer, i):
        lo = i * BLK
        kk, qq = k_ref.at[layer], q_ref.at[layer]

        def pair(hp, carry):
            for s in range(2):
                h = hp * 2 + s
                qm = qq[lo : lo + BLK, :] * jnp.where(lane_head == h, 0.125, 0.0).astype(BF)
                head = pl.ds(pl.multiple_of(h * HD, HD), HD)
                sd = jnp.where(tri, nt(kk[lo : lo + BLK, :], qm), NEG)
                top = jnp.max(sd, axis=0, keepdims=True)
                if i:
                    sa = nt(kk[0:lo, :], qm)
                    top = jnp.maximum(top, jnp.max(sa, axis=0, keepdims=True))
                ed = jnp.exp(sd - top)
                total = jnp.sum(ed, axis=0, keepdims=True)
                o = nn(tr[head, lo : lo + BLK], ed.astype(BF))
                if i:
                    ea = jnp.exp(sa - top)
                    total = total + jnp.sum(ea, axis=0, keepdims=True)
                    o = o + nn(tr[head, 0:lo], ea.astype(BF))
                ctxT[head, :] = o / total
                lse[layer, pl.ds(h, 1), lo : lo + BLK] = top + jnp.log(total)
            return carry

        lax.fori_loop(0, 2, pair, 0)
        ctx[lo : lo + BLK, :] = ctxT[...].T.astype(BF)

    def attend_back(layer, i):
        lo = i * BLK
        kk, qq, vv = k_ref.at[layer], q_ref.at[layer], v_ref.at[layer]

        def pair(hp, carry):
            for s in range(2):
                h = hp * 2 + s
                on = lane_head == h
                qm = qq[lo : lo + BLK, :] * jnp.where(on, 0.125, 0.0).astype(BF)
                gm = gctx[lo : lo + BLK, :] * jnp.where(on, 1.0, 0.0).astype(BF)
                head = pl.ds(pl.multiple_of(h * HD, HD), HD)
                ls = lse[layer, pl.ds(h, 1), lo : lo + BLK]
                spans = [(lo, lo + BLK)] + ([(0, lo)] if i else [])
                ps, ts = [], []
                for a, b in spans:
                    p = jnp.exp(nt(kk[a:b, :], qm) - ls)
                    if a == lo:
                        p = jnp.where(tri, p, 0.0)
                    ps.append(p)
                    ts.append(p * nt(vv[a:b, :], gm))
                dsum = sum(jnp.sum(t, axis=0, keepdims=True) for t in ts)
                o = None
                for (a, b), p, t in zip(spans, ps, ts):
                    gs = (t - p * dsum).astype(BF)
                    dv = nn(p.astype(BF), gm)
                    dk = nn(gs, qm)
                    for c in range(a // BLK, b // BLK):
                        at = pl.ds(c * BLK, BLK)
                        gv[:, at] += dv[c * BLK - a : (c + 1) * BLK - a]
                        gk[:, at] += dk[c * BLK - a : (c + 1) * BLK - a]
                    dq = nn(tr[head, a:b], gs)
                    o = dq if o is None else o + dq
                ctxT[head, :] = o * 0.125
            return carry

        lax.fori_loop(0, 2, pair, 0)
        gqkv[lo : lo + BLK, 0:256] = ctxT[...].T.astype(BF)

    def out_partial(layer):
        w = W.at[ATTENTION[layer]]
        return lambda c: nt(plain(ctx, c), w[:, 768:1024])

    heads_here = share_heads()
    x_here = [swap_rows(x_in.at[half(h)], x0.at[half(h)], x0.at[half(h)]) for h in range(2)]
    outT[0] = outw[0].astype(F32).T.astype(BF)
    near(0)
    far(0)
    share_small()
    foutT[0] = foutw[0].astype(F32).T.astype(BF)
    near(1)
    near(3)
    at_home(lambda: first(0, 1, 3))
    heads_here()
    unpack_small()
    ag = []
    for h in range(2):
        x_here[h]()
        norm_into(x0, h, 0, 0, n1.at[0], spot_start(h))
        ag.append(Gather(n1.at[0], h))
    far(1)
    at_home(lambda: later(0, 1))
    away(lambda: first(0))
    outT[1] = outw[1].astype(F32).T.astype(BF)
    foutT[1] = foutw[1].astype(F32).T.astype(BF)
    at_home(lambda: later(3))
    ag[0].forward()

    @away
    def _():
        later(0)
        first(1)
        pass_on(1)

    ag[1].forward()
    at_home(lambda: pass_on(1))
    far(3)
    for item in (5, 6, 7):
        near(item)
    ag[0].finish()
    ag[1].finish()
    away(lambda: later(1))
    at_home(lambda: pass_on(3))
    ready(0)
    project(0, 0)
    project(0, 1)
    attend(0, 0)
    attend(0, 1)
    at_home(lambda: first(2))

    @away
    def _():
        first(3)
        pass_on(3)

    attend(0, 2)
    attend(0, 3)
    at_home(lambda: later(2))
    away(lambda: later(3))
    sums = [Scatter(out_partial(0), h, first_sums, acc) for h in range(2)]
    at_home(lambda: first(4))
    away(lambda: first(2))
    nx = []
    for h in range(2):
        sums[h].finish()
        m1[0, half(h), :] = x0[half(h), :].astype(F32) + acc[half(h), :] + vec(0, 4)
        norm_into(m1.at[0], h, 0, 1, nx0.at[h], k * HALF)
        mine = nx0.at[h, many(k * HALF, HALF)]
        nx.append(rcopy(mine, mine, sib))
        if h == 0:
            at_home(lambda: later(4))

            @away
            def _():
                later(2)
                first(4)

    far(5)
    far(6)
    away(lambda: later(4))
    first(5)
    cot_here = [
        swap_rows(
            cot_in.at[half(h)], gmx.at[spot(qi, h)], gmx.at[spot(2 * (1 - k) + zl, h)]
        )
        for h in range(2)
    ]
    for cp in nx:
        cp.wait_recv()

    def hidden0(s):
        def body(c, carry):
            h, hc = c // 2, c % 2
            cols = many(hc * 512, 512)
            u = nn(nx0[h], W[1 + s, :, cols]) + b1[0, s, :, cols]
            u0[h, s, :, cols] = u.astype(BF)
            act[2 * h + s, :, cols] = gelu(u).astype(BF)
            return carry

        lax.fori_loop(0, 4, body, 0)

    ready(1)
    hidden0(zl)
    ready(2)
    hidden0(1 - zl)
    for cp in nx:
        cp.wait_send()
    ready(3)
    ready(4)

    def share0(h, value):
        own2[...] = value
        sy[h] = own2[many((1 - k) * HALF, HALF), :].astype(BF)
        cp = rcopy(sy.at[h], syr.at[h], sib)
        acc[half(h), :] = own2[many(k * HALF, HALF), :]

        def finish():
            cp.wait_recv()
            acc[half(h), :] += syr[h].astype(F32)
            cp.wait_send()

        return finish

    ag = []
    ends = [share0(h, nt(act[2 * h], W[3]) + nt(act[2 * h + 1], W[4])) for h in range(2)]
    later(5)
    first(6)
    for h in range(2):
        ends[h]()
        x1[half(h), :] = m1[0, half(h), :] + acc[half(h), :] + vec(0, 5)
        norm_into(x1, h, 1, 0, n1.at[1], spot_start(h))
        ag.append(Gather(n1.at[1], h))
    ag[0].forward()
    ag[0].finish()
    later(6)
    ready(5)
    project(1, 0)
    ag[1].forward()
    ag[1].finish()
    project(1, 1)
    for h in range(2):
        cot_here[h]()
    far(7)
    gm = [Gather(gmx, h) for h in range(2)]
    attend(1, 0)
    attend(1, 1)
    attend(1, 2)
    gm[0].forward()
    attend(1, 3)
    gm[1].forward()
    first(7)
    sums = [Scatter(out_partial(1), h, first_sums, acc) for h in range(2)]
    later(7)
    ag = []
    for h in range(2):
        sums[h].finish()
        m1[1, half(h), :] = x1[half(h), :] + acc[half(h), :] + vec(1, 4)
        norm_into(m1.at[1], h, 1, 1, ga, spot_start(h))
        ag.append(Gather(ga, h))
    gm[0].finish()
    gm[1].finish()
    ready(6)

    def hidden1(h):
        def body(i, carry):
            c, hc = 2 * h + i // 2, i % 2
            cols = many(hc * 512, 512)
            u = nn(ga[chunk(c), :], W[6, :, cols]) + b1[1, zl, :, cols]
            u1[c, :, cols] = u.astype(BF)
            act[c, :, cols] = gelu(u).astype(BF)
            return carry

        lax.fori_loop(0, 4, body, 0)

    def feed_back1(c):
        gh = nn(gmx[chunk(c), :], W[7])
        gu = (gh * gelu_slope(u1[c].astype(F32))).astype(BF)
        return nt(gu, W[6])

    sums = []
    for h in range(2):
        ag[h].forward()
        ag[h].finish()
        hidden1(h)
        if h == 0:
            ready(7)
        sums.append(Scatter(feed_back1, h, first_sums, acc))

    def mid_back(layer, h, g_rows):
        gain = vec(layer, 2)

        def f(rows, at):
            v = g_rows(rows, at) + norm_back(m1[layer, rows, :], acc[rows, :], gain)
            gmid[rows, :] = v
            ga[many(spot_start(h) + at, 64), :] = v.astype(BF)

        by_rows(h, f)

    hops = [sib, zp, col(0, 2)] + [(flip(d, b), z) for b in range(1, chip_bits + 1)]

    def reduce_all(layer):
        flight = []

        def hop():
            n = len(flight)
            if n:
                if n > len(hops):
                    return
                flight[-1].wait_recv()
                total = gsend[layer, n - 1] + grecv[layer, n - 1]
                if n == len(hops):
                    G[16 * layer : 16 * layer + 16, :] = total
                    flight.append(None)
                    return
                gsend[layer, n] = total
            flight.append(rcopy(gsend.at[layer, n], grecv.at[layer, n], hops[n], keep=True))

        return hop

    def turn(layer):
        def body(c, carry):
            tr[:, block(c)] = k_ref[layer, block(c), :].astype(F32).T.astype(BF)
            return carry

        lax.fori_loop(0, 4, body, 0)

    def attention_back(layer, ag, extra, hop):
        w = W.at[ATTENTION[layer]]

        def down(b):
            rows = jnp.concatenate([ga[spot(b, 0), :], ga[spot(b, 1), :]], axis=0)
            gctx[block(b), :] = nn(rows, w[:, 768:1024]).astype(BF)

        def back(mine, upper):
            for zz in range(2):
                i = 2 * upper + (zz if mine else 1 - zz)

                @pl.when(zl == zz)
                def _(i=i):
                    attend_back(layer, i)

        gk[...] = jnp.zeros_like(gk)
        gv[...] = jnp.zeros_like(gv)
        ag[0].chip()
        ag[1].chip()
        down(zl)
        down(2 + zl)
        back(True, 1)
        ag[0].forward()
        back(True, 0)
        hop()
        ag[1].forward()
        ag[0].finish(False)
        ag[1].finish(False)
        extra()
        down(1 - zl)
        down(3 - zl)
        back(False, 1)
        back(False, 0)
        hop()

        def lows(c, carry):
            gqkv[block(c), 256:512] = gk[:, block(c)].astype(BF)
            gqkv[block(c), 512:768] = gv[:, block(c)].astype(BF)
            gt_ref[block(c), :] = nt(gqkv[block(c), :], bpad[layer]).astype(BF)
            return carry

        lax.fori_loop(0, 4, lows, 0)
        sums = [
            Scatter(
                lambda c: nt(plain(gqkv, c), w[:, 0:768]) + nt(plain(gt_ref, c), apad[layer]),
                h, first_sums, acc,
            )
            for h in range(2)
        ]

        def grads(c, carry):
            ga_sum, gb_sum = carry
            gtt = plain(gt_ref, c).astype(F32).T[0:16, :].astype(BF)
            tt = low[layer, chunk(c), :].astype(F32).T[0:16, :].astype(BF)
            return (
                ga_sum + nn(gtt, n1[layer, chunk(c), :]),
                gb_sum + nn(tt, plain(gqkv, c)),
            )

        ga_sum, gb_sum = lax.fori_loop(
            0, 4, grads, (jnp.zeros((16, D), F32), jnp.zeros((16, 768), F32))
        )
        gb = ADAPTER_SCALE * jnp.where(
            lax.broadcasted_iota(jnp.int32, (8, 256), 0) < 4, gb_sum[0:8, 0:256], gb_sum[0:8, 512:768]
        )
        gsend[layer, 0, 0:8, :] = ga_sum[0:8, :]
        gsend[layer, 0, 8:16, :] = jnp.zeros((8, D), F32)
        gsend[layer, 0, 8:16, many(qi * 256, 256)] = gb
        step = reduce_all(layer)
        step()
        return sums, step

    def step_back(layer, h, src):
        gain = vec(layer, 0)

        def f(rows, at):
            g_ref[rows, :] = gmid[rows, :] + norm_back(src[rows, :].astype(F32), acc[rows, :], gain)

        by_rows(h, f)

    turn(1)
    ag = []
    for h in range(2):
        sums[h].finish()
        mid_back(
            1, h, lambda rows, at, h=h: gmx[many(spot_start(h) + at, 64), :].astype(F32)
        )
        ag.append(Gather(ga, h))
    late = []

    def first_output():
        for h in range(2):
            late.append(
                Scatter(
                    lambda c: nt(act[c], W[7]), h, late_sums, m1.at[1],
                    lambda rows: m1[1, rows, :] + vec(1, 5),
                )
            )

    sums, hop1 = attention_back(1, ag, first_output, lambda: None)

    def feed_back0(h):
        total = None
        for s in range(2):
            gh = nn(nx0[h], W[3 + s])
            gu = (gh * gelu_slope(u0[h, s].astype(F32))).astype(BF)
            y = nt(gu, W[1 + s])
            total = y if total is None else total + y
        return total

    def next_rows(h):
        sums[h].finish()
        step_back(1, h, x1)
        nx0[h, many(k * HALF, HALF), :] = g_ref[half(h), :].astype(BF)
        mine = nx0.at[h, many(k * HALF, HALF)]
        return rcopy(mine, mine, sib)

    def after(h):
        ends[h]()
        mid_back(0, h, lambda rows, at: g_ref[rows, :])
        ag.append(Gather(ga, h))

    ag, ends = [], []
    nx = [next_rows(0)]
    turn(0)
    hop1()
    nx[0].wait_recv()
    ends.append(share0(0, feed_back0(0)))
    nx.append(next_rows(1))
    after(0)
    nx[1].wait_recv()
    ends.append(share0(1, feed_back0(1)))
    after(1)
    hop1()
    for cp in nx:
        cp.wait_send()
    out_here = []
    for h in range(2):
        late[h].finish()
        party[0, half(h), :] = m1[1, half(h), :].astype(BF)
        out_here.append(swap_rows(party.at[0, half(h)], out_ref.at[half(h)], out_ref.at[half(h)]))
    sums, hop0 = attention_back(0, ag, lambda: None, hop1)
    gin_here = []
    hop0()
    for h in range(2):
        sums[h].finish()
        step_back(0, h, x0)
        party[1, half(h), :] = g_ref[half(h), :].astype(BF)
        gin_here.append(swap_rows(party.at[1, half(h)], gin_ref.at[half(h)], gin_ref.at[half(h)]))
        hop0()
    for _ in range(len(hops)):
        hop1()
        hop0()
    for h in range(2):
        out_here[h]()
        gin_here[h]()
    for w in sends:
        w()


def shards(
    inputs, qkv_w, qkv_b, out_w, out_b, fin_w, fin_b, fout_w, fout_b, gains, shifts, first, second,
    cotangent,
):
    ndp = lax.axis_size("dp")
    R = qkv_w.shape[1]
    hops = ndp.bit_length() - 1 + 2
    small_dp = jnp.stack(
        [gains[:, 0], shifts[:, 0], gains[:, 1], shifts[:, 1], out_b, fout_b], axis=1
    ).reshape(LAYERS * 6, R)
    small_dp = jnp.pad(small_dp, ((0, 16 - LAYERS * 6), (0, 128 - R)))
    up = second * jnp.asarray(ADAPTER_SCALE, BF)
    small_mp = jnp.concatenate(
        [
            jnp.pad(up[:, 0], ((0, 0), (0, 0), (0, 768))),
            jnp.pad(up[:, 1], ((0, 0), (0, 0), (512, 256))),
            jnp.pad(qkv_b.reshape(LAYERS, 1, 768), ((0, 0), (0, 0), (0, 256))),
            jnp.pad(fin_b[:, None], ((0, 0), (0, 6), (0, 0))),
        ],
        axis=1,
    ).reshape(LAYERS * 16, D)
    apad = jnp.concatenate(
        [first[:, 0], first[:, 1], jnp.zeros((LAYERS, D, 120), BF)], axis=2
    )
    anyspec = pl.BlockSpec(memory_space=pl.ANY)
    vm = pl.BlockSpec(memory_space=pltpu.VMEM)
    V = pltpu.VMEM
    scratch = [
        V((PIECES, D, D), BF),
        V((LAYERS, D, D), BF),
        V((D, D), BF),
        V((D, D), BF),
        V((LAYERS, D, 256), BF),
        V((LAYERS, D, 256), BF),
        V((LAYERS, D, 256), BF),
        V((256, D), BF),
        V((LAYERS, D, 128), BF),
        V((BLK, D), BF),
        V((BLK, D), F32),
        V((LAYERS, BLK, D), F32),
        V((2, 2, BLK, D), BF),
        V((4, BLK, D), BF),
        V((4, BLK, D), BF),
        V((D, 256), BF),
        V((D, 256), BF),
        V((256, 256), F32),
        V((2, BLK, D), BF),
        V((2, BLK, D), BF),
        V((2, HALF, D), BF),
        V((2, HALF, D), BF),
        V((2, BLK, D), BF),
        V((2, BLK, D), BF),
        V((2, HALF, D), BF),
        V((2, HALF, D), BF),
        V((2, BLK, D), BF),
        V((2, HALF, D), BF),
        V((2, HALF, D), BF),
        V((D, 768), BF),
        V((D, 128), BF),
        V((BLK, D), F32),
        V((BLK, D), F32),
        V((BLK, D), F32),
        V((BLK, D), F32),
        V((LAYERS, hops, 16, D), F32),
        V((LAYERS, hops, 16, D), F32),
        V((LAYERS, 8, D), F32),
        V((LAYERS, R, 256), BF),
        V((LAYERS, R, D), BF),
        V((ndp, 16, 128), BF),
        V((2, 32, D), BF),
        V((16, D), F32),
        V((LAYERS, 128, 768), BF),
        V((LAYERS, 1, 768), F32),
        V((LAYERS, 2, 1, D), F32),
        pltpu.SemaphoreType.DMA((200,)),
        pltpu.SemaphoreType.DMA((200,)),
        pltpu.SemaphoreType.DMA((PIECES,)),
    ]
    out, gin, G = pl.pallas_call(
        functools.partial(kernel, ndp),
        out_shape=(
            jax.ShapeDtypeStruct((BLK, D), BF),
            jax.ShapeDtypeStruct((BLK, D), BF),
            jax.ShapeDtypeStruct((32, D), F32),
        ),
        in_specs=[anyspec, anyspec, anyspec, anyspec, vm, vm, vm, vm, vm],
        out_specs=(anyspec, anyspec, vm),
        scratch_shapes=scratch,
        compiler_params=pltpu.CompilerParams(
            collective_id=0, has_side_effects=True, vmem_limit_bytes=63 * 2**20
        ),
        name="two_blocks",
    )(inputs, cotangent, jnp.swapaxes(qkv_w, 1, 2), fin_w, out_w, fout_w, apad, small_dp, small_mp)
    G = G.reshape(LAYERS, 16, D)
    grad_a = jnp.swapaxes(G[:, 0:8].reshape(LAYERS, 2, 4, D), 2, 3)
    grad_b = G[:, 8:16].reshape(LAYERS, 2, 4, D)
    return (out, gin, grad_a, grad_b)


def solution(mesh):
    placed = (
        P(("dp", "mp"), None),
        P(None, "dp", None, "mp"),
        P(None, None, "mp"),
        P(None, "mp", "dp"),
        P(None, "dp"),
        P(None, "dp", "mp"),
        P(None, "mp"),
        P(None, "mp", "dp"),
        P(None, "dp"),
        P(None, None, "dp"),
        P(None, None, "dp"),
        P(),
        P(None, None, None, "mp"),
        P(("dp", "mp"), None),
    )
    return jax.shard_map(
        shards,
        mesh=mesh,
        in_specs=placed,
        out_specs=(P(("dp", "mp"), None), P(("dp", "mp"), None), P(), P()),
        check_vma=False,
    )
```

```python
import functools

import jax
import jax.numpy as jnp
from jax import lax
from jax.experimental import pallas as pl
from jax.experimental.pallas import tpu as pltpu
from jax.sharding import PartitionSpec as P

MESH = pl.DeviceIdType.MESH
F32 = jnp.float32
BF = jnp.bfloat16
D = 1024
BLK = 256
HALF = 128
HD = 64
LAYERS = 2
NORM_EPS = 1e-05
ADAPTER_SCALE = 8.0
C0 = 0.7978845608
C1 = 0.044715
NEG = -1e30

ATTENTION = (0, 5)
PIECES = 8


def nt(a, b):
    return lax.dot_general(a, b, (((1,), (1,)), ((), ())), preferred_element_type=F32)


def nn(a, b):
    return lax.dot_general(a, b, (((1,), (0,)), ((), ())), preferred_element_type=F32)


def flip(value, bit):
    return value + (1 << bit) * (1 - 2 * ((value // (1 << bit)) % 2))


def gelu(u):
    return 0.5 * u * (1.0 + jnp.tanh(C0 * (u + C1 * u * u * u)))


def gelu_slope(u):
    square = u * u
    th = jnp.tanh(C0 * u * (1.0 + C1 * square))
    return 0.5 * (1.0 + th) + 0.5 * u * (1.0 - th * th) * (C0 * (1.0 + 3.0 * C1 * square))


def normed(x):
    c = x - jnp.mean(x, axis=-1, keepdims=True)
    rstd = lax.rsqrt(jnp.mean(c * c, axis=-1, keepdims=True) + NORM_EPS)
    return c * rstd, rstd


def norm_back(x, grad, gain):
    xhat, rstd = normed(x)
    gx = grad * gain
    return rstd * (
        gx
        - jnp.mean(gx, axis=-1, keepdims=True)
        - xhat * jnp.mean(gx * xhat, axis=-1, keepdims=True)
    )


def kernel(
    ndp,
    x_in, cot_in, qkvw, finw, outw, foutw, apad, small_dp, small_mp,
    out_ref, gin_ref, G,
    W, n1, ga, gmx, q_ref, k_ref, v_ref, tr, low, x0, x1, m1, u0, u1, act, ctx, gctx, ctxT,
    part, heldy, rs1, rs2s, rs2r, party, rs1y, rs2ys, rs2yr, nx0, sy, syr, gqkv, gt_ref,
    acc, g_ref, gmid, own2, gsend, grecv, lse, outT, foutT, sdp, smp, vecs, bpad, bqkv, b1,
    ssem, rsem, p0r,
):
    R = finw.shape[1]
    gk, gv = acc, g_ref
    d = lax.axis_index("dp")
    z = lax.axis_index("mp")
    k = d % 2
    j = d // 2
    zl = z % 2
    zh = z // 2
    qi = 2 * k + zl
    chip_bits = (ndp // 2).bit_length() - 1

    def col(dc, dz):
        zz = z
        if dz & 1:
            zz = zz + 1 - 2 * zl
        if dz & 2:
            zz = zz + 2 - 4 * zh
        return (d + 1 - 2 * k if dc else d, zz)

    sib, zp, swap = col(1, 0), col(0, 1), col(1, 2)
    count = [0]
    sends = []

    def sem():
        count[0] += 1
        return count[0] - 1

    def rcopy(src, dst, dev, keep=False):
        i = sem()
        cp = pltpu.make_async_remote_copy(
            src, dst, ssem.at[i], rsem.at[i], device_id=dev, device_id_type=MESH
        )
        cp.start()
        if keep:
            sends.append(cp.wait_send)
        return cp

    peers = [col(dc, dz) for dc in range(2) for dz in range(4) if dc or dz]
    peers += [(flip(d, bit + 1), z) for bit in range(chip_bits)]
    barrier = pltpu.get_barrier_semaphore()
    for dev in peers:
        pl.semaphore_signal(barrier, inc=1, device_id=dev, device_id_type=MESH)
    pl.semaphore_wait(barrier, len(peers))

    def swap_rows(src, dst_own, dst_other):
        i = sem()
        keep = pltpu.make_async_copy(src, dst_own, rsem.at[i])
        move = pltpu.make_async_remote_copy(
            src, dst_other, ssem.at[i], rsem.at[i], device_id=swap, device_id_type=MESH
        )

        @pl.when(k == zh)
        def _():
            keep.start()

        pl.when(k != zh)(move.start)

        def finish_send():
            @pl.when(k != zh)
            def _():
                move.wait_send()

        sends.append(finish_send)
        return keep.wait

    def many(start, size):
        return pl.ds(pl.multiple_of(start, size), size)

    def block(b):
        return many(b * BLK, BLK)

    def half(h):
        return pl.ds(h * HALF, HALF)

    def spot(b, h):
        return many(h * 4 * HALF + b * HALF, HALF)

    def chunk(c):
        return many(c * BLK, BLK)

    def plain_rows(c):
        at = (c % 2) * 2 * BLK + (c // 2) * HALF
        return many(at, HALF), many(at + BLK, HALF)

    def plain(ref, c):
        one, two = plain_rows(c)
        return jnp.concatenate([ref[one, :], ref[two, :]], axis=0)

    def plain_store(ref, c, value):
        one, two = plain_rows(c)
        ref[one, :] = value[0:HALF]
        ref[two, :] = value[HALF:BLK]

    own_rows = pl.ds(pl.multiple_of(d * R, R), R)
    chip_rows = pl.ds(pl.multiple_of(j * (2 * R), 2 * R), 2 * R)
    slots = (0, 1 + zl, 2 - zl, 3 + zl, 4 - zl, 5, 6, 7)
    sources = {
        0: [(qkvw.at[0, n], n * 256, 256) for n in range(3)] + [(outT.at[0], 768, 256)],
        1: [(finw.at[0], 0, D)],
        3: [(foutT.at[0], 0, D)],
        5: [(qkvw.at[1, n], n * 256, 256) for n in range(3)] + [(outT.at[1], 768, 256)],
        6: [(finw.at[1], 0, D)],
        7: [(foutT.at[1], 0, D)],
    }

    holder = 2 * j + zh
    home = k == zh

    def near(item):
        arrived = p0r.at[item]
        i = sem()
        for src, at, width in sources[item]:
            dst = W.at[slots[item], own_rows, pl.ds(at, width)]

            @pl.when(home)
            def _(src=src, dst=dst):
                pltpu.make_async_copy(src, dst, arrived).start()

            @pl.when(jnp.logical_not(home))
            def _(src=src, dst=dst):
                pltpu.make_async_remote_copy(
                    src, dst, ssem.at[i], arrived, device_id=(holder, z), device_id_type=MESH
                ).start()

        slab = W.at[slots[item], own_rows, :]

        def finish():
            @pl.when(jnp.logical_not(home))
            def _():
                pltpu.make_async_copy(slab, slab, ssem.at[i]).wait()

        sends.append(finish)

    def far(item):
        i = sem()
        for src, at, width in sources[item]:
            dst = W.at[slots[item], own_rows, pl.ds(at, width)]
            pltpu.make_async_remote_copy(
                src, dst, ssem.at[i], p0r.at[item], device_id=(holder, swap[1]), device_id_type=MESH
            ).start()
        slab = W.at[slots[item], own_rows, :]
        sends.append(pltpu.make_async_copy(slab, slab, ssem.at[i]).wait)

    pass_sem = {1: sem(), 3: sem()}

    def passing(item):
        slab = W.at[slots[item], chip_rows, :]
        i = pass_sem[item]
        return pltpu.make_async_remote_copy(
            slab, slab, ssem.at[i], rsem.at[i], device_id=zp, device_id_type=MESH
        )

    def pass_on(item):
        passing(item).start()

    for item in pass_sem:
        sends.append(passing(item).wait_send)

    def arrive(item):
        if item in (2, 4):
            passing(item - 1).wait_recv()
            return
        slab = W.at[slots[item], chip_rows, :]
        pltpu.make_async_copy(slab, slab, p0r.at[item]).wait()

    half_cols = (pl.ds(0, D // 2), pl.ds(D // 2, D // 2))
    order = (tuple(range(chip_bits)), tuple(reversed(range(chip_bits))))
    stage_sem = {
        (item, stage): (sem(), sem()) for item in range(PIECES) for stage in range(chip_bits)
    }

    def stage_slabs(item, stage):
        for cols, i in zip(half_cols, stage_sem[item, stage]):
            yield W.at[slots[item], pl.ds(0, (1 << stage) * 2 * R), cols], i

    for item, stage in stage_sem:
        for slab, i in stage_slabs(item, stage):
            sends.append(pltpu.make_async_copy(slab, slab, ssem.at[i]).wait)

    def start_stage(item, stage):
        for cols, bits, i in zip(half_cols, order, stage_sem[item, stage]):
            dev = (flip(d, bits[stage] + 1), z)

            def send(m, carry=0, bits=bits, cols=cols, dev=dev, i=i):
                chip = j
                for n, bit in enumerate(bits[:stage]):
                    chip = chip + ((m // (1 << n)) % 2) * (flip(j, bit) - j)
                ref = W.at[slots[item], pl.ds(pl.multiple_of(chip * (2 * R), 2 * R), 2 * R), cols]
                pltpu.make_async_remote_copy(
                    ref, ref, ssem.at[i], rsem.at[i], device_id=dev, device_id_type=MESH
                ).start()
                return carry

            if stage <= 1:
                for m in range(1 << stage):
                    send(m)
            else:
                lax.fori_loop(0, 1 << stage, send, 0)

    def wait_stage(item, stage):
        for slab, i in stage_slabs(item, stage):
            pltpu.make_async_copy(slab, slab, rsem.at[i]).wait()

    def first(*items):
        for item in items:
            arrive(item)
            start_stage(item, 0)

    def later(*items):
        for item in items:
            for stage in range(1, chip_bits):
                wait_stage(item, stage - 1)
                start_stage(item, stage)

    def ready(item):
        wait_stage(item, chip_bits - 1)

    def at_home(f):
        pl.when(home)(f)

    def away(f):
        pl.when(jnp.logical_not(home))(f)

    def share_heads():
        i = sem()
        mine = smp.at[zl]
        copies = [
            pltpu.make_async_remote_copy(
                small_mp, mine, ssem.at[i], rsem.at[i], device_id=col(0, r), device_id_type=MESH
            )
            for r in (1, 2, 3)
        ]
        slab = W.at[0, pl.ds(0, 3 * 32), :]

        @at_home
        def _():
            for cp in copies:
                cp.start()
            pltpu.make_async_copy(small_mp, mine, rsem.at[i]).start()

        def finish():
            at_home(pltpu.make_async_copy(slab, slab, ssem.at[i]).wait)

        sends.append(finish)
        return pltpu.make_async_copy(smp, smp, rsem.at[i]).wait

    def share_small():
        sdp[d] = small_dp[...]
        bits = tuple(range(1, chip_bits + 1)) + (0,)
        for stage, bit in enumerate(bits):
            i = sem()

            def send(m, carry=0, i=i, bit=bit, stage=stage):
                slot = d
                for n, b in enumerate(bits[:stage]):
                    slot = slot + ((m // (1 << n)) % 2) * (flip(d, b) - d)
                pltpu.make_async_remote_copy(
                    sdp.at[slot], sdp.at[slot], ssem.at[i], rsem.at[i],
                    device_id=(flip(d, bit), z), device_id_type=MESH,
                ).start()
                return carry

            if stage <= 2:
                for m in range(1 << stage):
                    send(m)
            else:
                lax.fori_loop(0, 1 << stage, send, 0)
            slab = sdp.at[pl.ds(0, 1 << stage)]
            pltpu.make_async_copy(slab, slab, rsem.at[i]).wait()
            sends.append(pltpu.make_async_copy(slab, slab, ssem.at[i]).wait)
        for n in range(ndp):
            vecs[:, n * R : (n + 1) * R] = sdp[n].astype(F32)[:, 0:R]

    def unpack_small():
        keep = lax.broadcasted_iota(jnp.int32, (16, 768), 0) < 8
        for layer in range(LAYERS):
            tile = smp[zl, 16 * layer : 16 * layer + 16, :].astype(F32)
            bpad[layer] = jnp.zeros((128, 768), BF)
            bpad[layer, 0:16, :] = jnp.where(keep, tile[:, 0:768], 0.0).astype(BF)
            bqkv[layer] = tile[8:9, 0:768]
            for s in range(2):
                b1[layer, s] = smp[s, 16 * layer : 16 * layer + 16, :].astype(F32)[9:10, :]

    def vec(layer, n):
        return vecs[layer * 6 + n : layer * 6 + n + 1, :]

    class Gather:
        def __init__(self, buf, h):
            mine = buf.at[spot(qi, h)]
            self.other = buf.at[spot(2 * k + 1 - zl, h)]
            self.to_z = rcopy(mine, mine, zp)
            self.to_s = rcopy(mine, mine, sib)

        def forward(self):
            self.to_z.wait_recv()
            self.fwd = rcopy(self.other, self.other, sib)

        def chip(self):
            self.to_s.wait_recv()

        def finish(self, chip=True):
            if chip:
                self.chip()
            self.fwd.wait_recv()
            for cp in (self.to_z, self.to_s, self.fwd):
                cp.wait_send()

    first_sums = (part, rs1, rs2s, rs2r)
    late_sums = (party, rs1y, rs2ys, rs2yr)

    class Scatter:
        def __init__(self, partial, h, buffers, dst, base=None):
            p, r1, r2s, r2r = buffers
            self.h, self.dst, self.r2r = h, dst, r2r
            p[h] = partial(2 * h + 1 - k).astype(BF)
            self.first = rcopy(p.at[h], r1.at[h], sib)
            own2[...] = partial(2 * h + k)
            self.first.wait_recv()
            away, here = many((1 - zl) * HALF, HALF), many(zl * HALF, HALF)
            r2s[h] = (own2[away, :] + r1[h, away, :].astype(F32)).astype(BF)
            self.second = rcopy(r2s.at[h], r2r.at[h], zp)
            total = own2[here, :] + r1[h, here, :].astype(F32)
            dst[half(h), :] = total if base is None else total + base(half(h))

        def finish(self):
            self.second.wait_recv()
            self.dst[half(self.h), :] += self.r2r[self.h].astype(F32)
            self.first.wait_send()
            self.second.wait_send()

    class Late:
        def __init__(self, first, second, dst, r2r, h):
            self.first, self.second, self.dst, self.r2r, self.h = first, second, dst, r2r, h

        def finish(self):
            self.second.wait_recv()
            self.dst[half(self.h), :] += self.r2r[self.h].astype(F32)
            self.first.wait_send()
            self.second.wait_send()

    def add_up(partial, buffers, dst):
        p, r1, r2s, r2r = buffers
        away, here = many((1 - zl) * HALF, HALF), many(zl * HALF, HALF)
        first, out = [], []
        for h in range(2):
            p[h] = partial(2 * h + 1 - k).astype(BF)
            first.append(rcopy(p.at[h], r1.at[h], sib))
        for h in range(2):
            own2[...] = partial(2 * h + k)
            first[h].wait_recv()
            r2s[h] = (own2[away, :] + r1[h, away, :].astype(F32)).astype(BF)
            second = rcopy(r2s.at[h], r2r.at[h], zp)
            dst[half(h), :] = own2[here, :] + r1[h, here, :].astype(F32)
            out.append(Late(first[h], second, dst, r2r, h))
        return out

    class Output:
        def begin(self):
            self.first = []
            for h in range(2):
                party[h] = nt(act[2 * h + 1 - k], W[7]).astype(BF)
                self.first.append(rcopy(party.at[h], rs1y.at[h], sib))
            for h in range(2):
                heldy[h] = nt(act[2 * h + k], W[7]).astype(BF)

        def middle(self):
            away, here = many((1 - zl) * HALF, HALF), many(zl * HALF, HALF)
            self.second = []
            for h in range(2):
                self.first[h].wait_recv()
                rs2ys[h] = (heldy[h, away, :].astype(F32) + rs1y[h, away, :].astype(F32)).astype(BF)
                self.second.append(rcopy(rs2ys.at[h], rs2yr.at[h], zp))
                m1[1, half(h), :] += (
                    vec(1, 5) + heldy[h, here, :].astype(F32) + rs1y[h, here, :].astype(F32)
                )

        def finish(self):
            for h in range(2):
                self.second[h].wait_recv()
                self.first[h].wait_send()
                self.second[h].wait_send()
                party[0, half(h), :] = (m1[1, half(h), :] + rs2yr[h].astype(F32)).astype(BF)

    def by_rows(h, f):
        def body(c, carry):
            f(many(h * HALF + c * 64, 64), c * 64)
            return carry

        lax.fori_loop(0, HALF // 64, body, 0)

    def norm_into(src, h, layer, which, dst, start):
        gain, shift = vec(layer, 2 * which), vec(layer, 2 * which + 1)

        def f(rows, at):
            xhat, _ = normed(src[rows, :].astype(F32))
            dst[many(start + at, 64), :] = (xhat * gain + shift).astype(BF)

        by_rows(h, f)

    def spot_start(h):
        return h * 4 * HALF + qi * HALF

    tri = lax.broadcasted_iota(jnp.int32, (BLK, BLK), 0) <= lax.broadcasted_iota(
        jnp.int32, (BLK, BLK), 1
    )
    lane_head = lax.broadcasted_iota(jnp.int32, (1, BLK), 1) // HD

    def project(layer, h):
        w = W.at[ATTENTION[layer]]

        def body(core, carry):
            c = 2 * h + core
            n = n1[layer, chunk(c), :]
            t = nn(n, apad[layer]).astype(BF)
            low[layer, chunk(c), :] = t
            pr = nn(n, w[:, 0:768]) + bqkv[layer] + nn(t, bpad[layer])
            pr = pr.astype(BF)
            plain_store(q_ref.at[layer], c, pr[:, 0:256])
            plain_store(k_ref.at[layer], c, pr[:, 256:512])
            v = pr[:, 512:768]
            plain_store(v_ref.at[layer], c, v)
            vt = v.astype(F32).T.astype(BF)
            one, two = plain_rows(c)
            tr[:, one] = vt[:, 0:HALF]
            tr[:, two] = vt[:, HALF:BLK]
            return carry

        lax.fori_loop(0, 2, body, 0)

    def attend(layer, i):
        lo = i * BLK
        kk, qq = k_ref.at[layer], q_ref.at[layer]

        def pair(hp, carry):
            for s in range(2):
                h = hp * 2 + s
                qm = qq[lo : lo + BLK, :] * jnp.where(lane_head == h, 0.125, 0.0).astype(BF)
                head = pl.ds(pl.multiple_of(h * HD, HD), HD)
                sd = jnp.where(tri, nt(kk[lo : lo + BLK, :], qm), NEG)
                top = jnp.max(sd, axis=0, keepdims=True)
                if i:
                    sa = nt(kk[0:lo, :], qm)
                    top = jnp.maximum(top, jnp.max(sa, axis=0, keepdims=True))
                ed = jnp.exp(sd - top)
                total = jnp.sum(ed, axis=0, keepdims=True)
                o = nn(tr[head, lo : lo + BLK], ed.astype(BF))
                if i:
                    ea = jnp.exp(sa - top)
                    total = total + jnp.sum(ea, axis=0, keepdims=True)
                    o = o + nn(tr[head, 0:lo], ea.astype(BF))
                ctxT[head, :] = o / total
                lse[layer, pl.ds(h, 1), lo : lo + BLK] = top + jnp.log(total)
            return carry

        lax.fori_loop(0, 2, pair, 0)
        ctx[lo : lo + BLK, :] = ctxT[...].T.astype(BF)

    def attend_back(layer, i):
        lo = i * BLK
        kk, qq, vv = k_ref.at[layer], q_ref.at[layer], v_ref.at[layer]

        def pair(hp, carry):
            for s in range(2):
                h = hp * 2 + s
                on = lane_head == h
                qm = qq[lo : lo + BLK, :] * jnp.where(on, 0.125, 0.0).astype(BF)
                gm = gctx[lo : lo + BLK, :] * jnp.where(on, 1.0, 0.0).astype(BF)
                head = pl.ds(pl.multiple_of(h * HD, HD), HD)
                ls = lse[layer, pl.ds(h, 1), lo : lo + BLK]
                spans = [(lo, lo + BLK)] + ([(0, lo)] if i else [])
                ps, ts = [], []
                for a, b in spans:
                    p = jnp.exp(nt(kk[a:b, :], qm) - ls)
                    if a == lo:
                        p = jnp.where(tri, p, 0.0)
                    ps.append(p)
                    ts.append(p * nt(vv[a:b, :], gm))
                dsum = sum(jnp.sum(t, axis=0, keepdims=True) for t in ts)
                o = None
                for (a, b), p, t in zip(spans, ps, ts):
                    gs = (t - p * dsum).astype(BF)
                    dv = nn(p.astype(BF), gm)
                    dk = nn(gs, qm)
                    for c in range(a // BLK, b // BLK):
                        at = pl.ds(c * BLK, BLK)
                        gv[:, at] += dv[c * BLK - a : (c + 1) * BLK - a]
                        gk[:, at] += dk[c * BLK - a : (c + 1) * BLK - a]
                    dq = nn(tr[head, a:b], gs)
                    o = dq if o is None else o + dq
                ctxT[head, :] = o * 0.125
            return carry

        lax.fori_loop(0, 2, pair, 0)
        gqkv[lo : lo + BLK, 0:256] = ctxT[...].T.astype(BF)

    def out_partial(layer):
        w = W.at[ATTENTION[layer]]
        return lambda c: nt(plain(ctx, c), w[:, 768:1024])

    heads_here = share_heads()
    x_moves = [swap_rows(x_in.at[half(h)], x0.at[half(h)], x0.at[half(h)]) for h in range(2)]
    outT[0] = outw[0].astype(F32).T.astype(BF)
    near(0)
    far(0)
    share_small()
    foutT[0] = foutw[0].astype(F32).T.astype(BF)
    near(1)
    near(3)
    at_home(lambda: first(0, 1, 3))
    outT[1] = outw[1].astype(F32).T.astype(BF)
    foutT[1] = foutw[1].astype(F32).T.astype(BF)
    near(5)
    near(6)
    near(7)
    heads_here()
    unpack_small()
    ag = []
    for h in range(2):
        x_moves[h]()
        norm_into(x0, h, 0, 0, n1.at[0], spot_start(h))
        ag.append(Gather(n1.at[0], h))
    far(1)
    at_home(lambda: later(0, 1))
    away(lambda: first(0))
    at_home(lambda: later(3))
    ag[0].forward()
    at_home(lambda: first(5))

    @away
    def _():
        later(0)
        first(1)
        pass_on(1)

    ag[1].forward()
    at_home(lambda: pass_on(1))
    far(3)
    at_home(lambda: later(5))
    ag[0].finish()
    ag[1].finish()
    away(lambda: later(1))
    at_home(lambda: pass_on(3))
    ready(0)
    project(0, 0)
    project(0, 1)
    attend(0, 0)
    attend(0, 1)
    at_home(lambda: first(2))

    @away
    def _():
        first(3)
        pass_on(3)

    attend(0, 2)
    attend(0, 3)
    at_home(lambda: later(2))
    away(lambda: later(3))
    sums = add_up(out_partial(0), first_sums, acc)
    at_home(lambda: first(4))
    away(lambda: first(2))
    nx = []
    for h in range(2):
        sums[h].finish()
        m1[0, half(h), :] = x0[half(h), :].astype(F32) + acc[half(h), :] + vec(0, 4)
        norm_into(m1.at[0], h, 0, 1, nx0.at[h], k * HALF)
        mine = nx0.at[h, many(k * HALF, HALF)]
        nx.append(rcopy(mine, mine, sib))
        if h == 0:
            at_home(lambda: later(4))

            @away
            def _():
                later(2)
                first(4)

    far(5)
    far(6)

    @away
    def _():
        later(4)
        first(5)

    cot_here = [
        swap_rows(
            cot_in.at[half(h)], gmx.at[spot(qi, h)], gmx.at[spot(2 * (1 - k) + zl, h)]
        )
        for h in range(2)
    ]
    for cp in nx:
        cp.wait_recv()

    def hidden0(s):
        def body(c, carry):
            h, hc = c // 2, c % 2
            cols = many(hc * 512, 512)
            u = nn(nx0[h], W[1 + s, :, cols]) + b1[0, s, :, cols]
            u0[h, s, :, cols] = u.astype(BF)
            act[2 * h + s, :, cols] = gelu(u).astype(BF)
            return carry

        lax.fori_loop(0, 4, body, 0)

    ready(1)
    hidden0(zl)
    ready(2)
    hidden0(1 - zl)
    for cp in nx:
        cp.wait_send()
    ready(3)
    ready(4)

    def share0(h, value):
        own2[...] = value
        sy[h] = own2[many((1 - k) * HALF, HALF), :].astype(BF)
        cp = rcopy(sy.at[h], syr.at[h], sib)
        acc[half(h), :] = own2[many(k * HALF, HALF), :]

        def finish():
            cp.wait_recv()
            acc[half(h), :] += syr[h].astype(F32)
            cp.wait_send()

        return finish

    ag = []
    ends = [share0(h, nt(act[2 * h], W[3]) + nt(act[2 * h + 1], W[4])) for h in range(2)]
    away(lambda: later(5))
    for h in range(2):
        ends[h]()
        x1[half(h), :] = m1[0, half(h), :] + acc[half(h), :] + vec(0, 5)
        norm_into(x1, h, 1, 0, n1.at[1], spot_start(h))
        ag.append(Gather(n1.at[1], h))
    first(6)
    ag[0].forward()
    ag[0].finish()
    ready(5)
    project(1, 0)
    ag[1].forward()
    ag[1].finish()
    later(6)
    project(1, 1)
    for h in range(2):
        cot_here[h]()
    far(7)
    gm = [Gather(gmx, h) for h in range(2)]
    attend(1, 0)
    attend(1, 1)
    attend(1, 2)
    attend(1, 3)
    sums = add_up(out_partial(1), first_sums, acc)
    gm[0].forward()
    gm[1].forward()
    first(7)
    ag = []
    for h in range(2):
        sums[h].finish()
        m1[1, half(h), :] = x1[half(h), :] + acc[half(h), :] + vec(1, 4)
        norm_into(m1.at[1], h, 1, 1, ga, spot_start(h))
        ag.append(Gather(ga, h))
        if h == 0:
            later(7)
    gm[0].finish()
    gm[1].finish()
    ready(6)

    def hidden1(h):
        def body(i, carry):
            c, hc = 2 * h + i // 2, i % 2
            cols = many(hc * 512, 512)
            u = nn(ga[chunk(c), :], W[6, :, cols]) + b1[1, zl, :, cols]
            u1[c, :, cols] = u.astype(BF)
            act[c, :, cols] = gelu(u).astype(BF)
            return carry

        lax.fori_loop(0, 4, body, 0)

    def feed_back1(c):
        gh = nn(gmx[chunk(c), :], W[7])
        gu = (gh * gelu_slope(u1[c].astype(F32))).astype(BF)
        return nt(gu, W[6])

    sums = []
    for h in range(2):
        ag[h].forward()
        ag[h].finish()
        hidden1(h)
        if h == 0:
            ready(7)
        sums.append(Scatter(feed_back1, h, first_sums, acc))

    def mid_back(layer, h, g_rows):
        gain = vec(layer, 2)

        def f(rows, at):
            v = g_rows(rows, at) + norm_back(m1[layer, rows, :], acc[rows, :], gain)
            gmid[rows, :] = v
            ga[many(spot_start(h) + at, 64), :] = v.astype(BF)

        by_rows(h, f)

    hops = [(flip(d, b), z) for b in range(1, chip_bits + 1)] + [sib, zp, col(0, 2)]

    def reduce_all(layer):
        flight = []

        def hop():
            n = len(flight)
            if n:
                if n > len(hops):
                    return
                flight[-1].wait_recv()
                total = gsend[layer, n - 1] + grecv[layer, n - 1]
                if n == len(hops):
                    G[16 * layer : 16 * layer + 16, :] = total
                    flight.append(None)
                    return
                gsend[layer, n] = total
            flight.append(rcopy(gsend.at[layer, n], grecv.at[layer, n], hops[n], keep=True))

        return hop

    def turn(layer):
        def body(c, carry):
            tr[:, block(c)] = k_ref[layer, block(c), :].astype(F32).T.astype(BF)
            return carry

        lax.fori_loop(0, 4, body, 0)

    def attention_back(layer, ag, extra, hop):
        w = W.at[ATTENTION[layer]]

        def down(b):
            rows = jnp.concatenate([ga[spot(b, 0), :], ga[spot(b, 1), :]], axis=0)
            gctx[block(b), :] = nn(rows, w[:, 768:1024]).astype(BF)

        def back(mine, upper):
            for zz in range(2):
                i = 2 * upper + (zz if mine else 1 - zz)

                @pl.when(zl == zz)
                def _(i=i):
                    attend_back(layer, i)

        gk[...] = jnp.zeros_like(gk)
        gv[...] = jnp.zeros_like(gv)
        ag[0].chip()
        ag[1].chip()
        down(zl)
        down(2 + zl)
        back(True, 1)
        ag[0].forward()
        back(True, 0)
        hop()
        ag[1].forward()
        ag[0].finish(False)
        ag[1].finish(False)
        extra()
        down(1 - zl)
        down(3 - zl)
        back(False, 1)
        back(False, 0)
        hop()

        def lows(c, carry):
            gqkv[block(c), 256:512] = gk[:, block(c)].astype(BF)
            gqkv[block(c), 512:768] = gv[:, block(c)].astype(BF)
            gt_ref[block(c), :] = nt(gqkv[block(c), :], bpad[layer]).astype(BF)
            return carry

        lax.fori_loop(0, 4, lows, 0)
        sums = add_up(
            lambda c: nt(plain(gqkv, c), w[:, 0:768]) + nt(plain(gt_ref, c), apad[layer]),
            first_sums, acc,
        )

        def grads(c, carry):
            ga_sum, gb_sum = carry
            gtt = plain(gt_ref, c).astype(F32).T[0:16, :].astype(BF)
            tt = low[layer, chunk(c), :].astype(F32).T[0:16, :].astype(BF)
            return (
                ga_sum + nn(gtt, n1[layer, chunk(c), :]),
                gb_sum + nn(tt, plain(gqkv, c)),
            )

        ga_sum, gb_sum = lax.fori_loop(
            0, 4, grads, (jnp.zeros((16, D), F32), jnp.zeros((16, 768), F32))
        )
        gb = ADAPTER_SCALE * jnp.where(
            lax.broadcasted_iota(jnp.int32, (8, 256), 0) < 4, gb_sum[0:8, 0:256], gb_sum[0:8, 512:768]
        )
        gsend[layer, 0, 0:8, :] = ga_sum[0:8, :]
        gsend[layer, 0, 8:16, :] = jnp.zeros((8, D), F32)
        gsend[layer, 0, 8:16, many(qi * 256, 256)] = gb
        step = reduce_all(layer)
        step()
        return sums, step

    def step_back(layer, h, src):
        gain = vec(layer, 0)

        def f(rows, at):
            g_ref[rows, :] = gmid[rows, :] + norm_back(src[rows, :].astype(F32), acc[rows, :], gain)

        by_rows(h, f)

    output = Output()
    output.begin()
    turn(1)
    ag = []
    for h in range(2):
        sums[h].finish()
        mid_back(
            1, h, lambda rows, at, h=h: gmx[many(spot_start(h) + at, 64), :].astype(F32)
        )
        ag.append(Gather(ga, h))
    sums, hop1 = attention_back(1, ag, output.middle, lambda: None)

    def feed_back0(h):
        total = None
        for s in range(2):
            gh = nn(nx0[h], W[3 + s])
            gu = (gh * gelu_slope(u0[h, s].astype(F32))).astype(BF)
            y = nt(gu, W[1 + s])
            total = y if total is None else total + y
        return total

    def next_rows(h):
        sums[h].finish()
        step_back(1, h, x1)
        nx0[h, many(k * HALF, HALF), :] = g_ref[half(h), :].astype(BF)
        mine = nx0.at[h, many(k * HALF, HALF)]
        return rcopy(mine, mine, sib)

    def after(h):
        ends[h]()
        mid_back(0, h, lambda rows, at: g_ref[rows, :])
        ag.append(Gather(ga, h))

    ag, ends = [], []
    nx = [next_rows(0)]
    turn(0)
    hop1()
    nx[0].wait_recv()
    ends.append(share0(0, feed_back0(0)))
    nx.append(next_rows(1))
    after(0)
    nx[1].wait_recv()
    ends.append(share0(1, feed_back0(1)))
    after(1)
    hop1()
    for cp in nx:
        cp.wait_send()
    out_here = []

    def give_output():
        output.finish()
        for h in range(2):
            out_here.append(
                swap_rows(party.at[0, half(h)], out_ref.at[half(h)], out_ref.at[half(h)])
            )

    sums, hop0 = attention_back(0, ag, give_output, hop1)
    gin_here = []
    for _ in range(len(hops) - 3):
        hop0()
    for h in range(2):
        sums[h].finish()
        step_back(0, h, x0)
        party[1, half(h), :] = g_ref[half(h), :].astype(BF)
        hop0()
        gin_here.append(swap_rows(party.at[1, half(h)], gin_ref.at[half(h)], gin_ref.at[half(h)]))
    for _ in range(len(hops)):
        hop1()
        hop0()
    for h in range(2):
        out_here[h]()
        gin_here[h]()
    for w in sends:
        w()


def shards(
    inputs, qkv_w, qkv_b, out_w, out_b, fin_w, fin_b, fout_w, fout_b, gains, shifts, first, second,
    cotangent,
):
    ndp = lax.axis_size("dp")
    R = qkv_w.shape[1]
    hops = ndp.bit_length() - 1 + 2
    small_dp = jnp.stack(
        [gains[:, 0], shifts[:, 0], gains[:, 1], shifts[:, 1], out_b, fout_b], axis=1
    ).reshape(LAYERS * 6, R)
    small_dp = jnp.pad(small_dp, ((0, 16 - LAYERS * 6), (0, 128 - R)))
    up = second * jnp.asarray(ADAPTER_SCALE, BF)
    small_mp = jnp.concatenate(
        [
            jnp.pad(up[:, 0], ((0, 0), (0, 0), (0, 768))),
            jnp.pad(up[:, 1], ((0, 0), (0, 0), (512, 256))),
            jnp.pad(qkv_b.reshape(LAYERS, 1, 768), ((0, 0), (0, 0), (0, 256))),
            jnp.pad(fin_b[:, None], ((0, 0), (0, 6), (0, 0))),
        ],
        axis=1,
    ).reshape(LAYERS * 16, D)
    apad = jnp.concatenate(
        [first[:, 0], first[:, 1], jnp.zeros((LAYERS, D, 120), BF)], axis=2
    )
    anyspec = pl.BlockSpec(memory_space=pl.ANY)
    vm = pl.BlockSpec(memory_space=pltpu.VMEM)
    V = pltpu.VMEM
    scratch = [
        V((PIECES, D, D), BF),
        V((LAYERS, D, D), BF),
        V((D, D), BF),
        V((D, D), BF),
        V((LAYERS, D, 256), BF),
        V((LAYERS, D, 256), BF),
        V((LAYERS, D, 256), BF),
        V((256, D), BF),
        V((LAYERS, D, 128), BF),
        V((BLK, D), BF),
        V((BLK, D), F32),
        V((LAYERS, BLK, D), F32),
        V((2, 2, BLK, D), BF),
        V((4, BLK, D), BF),
        V((4, BLK, D), BF),
        V((D, 256), BF),
        V((D, 256), BF),
        V((256, 256), F32),
        V((2, BLK, D), BF),
        V((2, BLK, D), BF),
        V((2, BLK, D), BF),
        V((2, HALF, D), BF),
        V((2, HALF, D), BF),
        V((2, BLK, D), BF),
        V((2, BLK, D), BF),
        V((2, HALF, D), BF),
        V((2, HALF, D), BF),
        V((2, BLK, D), BF),
        V((2, HALF, D), BF),
        V((2, HALF, D), BF),
        V((D, 768), BF),
        V((D, 128), BF),
        V((BLK, D), F32),
        V((BLK, D), F32),
        V((BLK, D), F32),
        V((BLK, D), F32),
        V((LAYERS, hops, 16, D), F32),
        V((LAYERS, hops, 16, D), F32),
        V((LAYERS, 8, D), F32),
        V((LAYERS, R, 256), BF),
        V((LAYERS, R, D), BF),
        V((ndp, 16, 128), BF),
        V((2, 32, D), BF),
        V((16, D), F32),
        V((LAYERS, 128, 768), BF),
        V((LAYERS, 1, 768), F32),
        V((LAYERS, 2, 1, D), F32),
        pltpu.SemaphoreType.DMA((200,)),
        pltpu.SemaphoreType.DMA((200,)),
        pltpu.SemaphoreType.DMA((PIECES,)),
    ]
    out, gin, G = pl.pallas_call(
        functools.partial(kernel, ndp),
        out_shape=(
            jax.ShapeDtypeStruct((BLK, D), BF),
            jax.ShapeDtypeStruct((BLK, D), BF),
            jax.ShapeDtypeStruct((32, D), F32),
        ),
        in_specs=[anyspec, anyspec, anyspec, anyspec, vm, vm, vm, vm, vm],
        out_specs=(anyspec, anyspec, vm),
        scratch_shapes=scratch,
        compiler_params=pltpu.CompilerParams(
            collective_id=0, has_side_effects=True, vmem_limit_bytes=63 * 2**20
        ),
        name="two_blocks",
    )(inputs, cotangent, jnp.swapaxes(qkv_w, 1, 2), fin_w, out_w, fout_w, apad, small_dp, small_mp)
    G = G.reshape(LAYERS, 16, D)
    grad_a = jnp.swapaxes(G[:, 0:8].reshape(LAYERS, 2, 4, D), 2, 3)
    grad_b = G[:, 8:16].reshape(LAYERS, 2, 4, D)
    return (out, gin, grad_a, grad_b)


def solution(mesh):
    placed = (
        P(("dp", "mp"), None),
        P(None, "dp", None, "mp"),
        P(None, None, "mp"),
        P(None, "mp", "dp"),
        P(None, "dp"),
        P(None, "dp", "mp"),
        P(None, "mp"),
        P(None, "mp", "dp"),
        P(None, "dp"),
        P(None, None, "dp"),
        P(None, None, "dp"),
        P(),
        P(None, None, None, "mp"),
        P(("dp", "mp"), None),
    )
    return jax.shard_map(
        shards,
        mesh=mesh,
        in_specs=placed,
        out_specs=(P(("dp", "mp"), None), P(("dp", "mp"), None), P(), P()),
        check_vma=False,
    )
```

```python
import functools

import jax
import jax.numpy as jnp
from jax import lax
from jax.experimental import pallas as pl
from jax.experimental.pallas import tpu as pltpu
from jax.sharding import PartitionSpec as P

MESH = pl.DeviceIdType.MESH
F32 = jnp.float32
BF = jnp.bfloat16
D = 1024
BLK = 256
HALF = 128
HD = 64
LAYERS = 2
NORM_EPS = 1e-05
ADAPTER_SCALE = 8.0
C0 = 0.7978845608
C1 = 0.044715
NEG = -1e30

ATTENTION = (0, 5)
PIECES = 8


def nt(a, b):
    return lax.dot_general(a, b, (((1,), (1,)), ((), ())), preferred_element_type=F32)


def nn(a, b):
    return lax.dot_general(a, b, (((1,), (0,)), ((), ())), preferred_element_type=F32)


def flip(value, bit):
    return value + (1 << bit) * (1 - 2 * ((value // (1 << bit)) % 2))


def gelu(u):
    return 0.5 * u * (1.0 + jnp.tanh(C0 * (u + C1 * u * u * u)))


def gelu_slope(u):
    square = u * u
    th = jnp.tanh(C0 * u * (1.0 + C1 * square))
    return 0.5 * (1.0 + th) + 0.5 * u * (1.0 - th * th) * (C0 * (1.0 + 3.0 * C1 * square))


def normed(x):
    c = x - jnp.mean(x, axis=-1, keepdims=True)
    rstd = lax.rsqrt(jnp.mean(c * c, axis=-1, keepdims=True) + NORM_EPS)
    return c * rstd, rstd


def norm_back(x, grad, gain):
    xhat, rstd = normed(x)
    gx = grad * gain
    return rstd * (
        gx
        - jnp.mean(gx, axis=-1, keepdims=True)
        - xhat * jnp.mean(gx * xhat, axis=-1, keepdims=True)
    )


def kernel(
    ndp,
    x_in, cot_in, qkvw, finw, outw, foutw, gains, shifts, outb, foutb, qkvb, finb, first_w, second_w,
    out_ref, gin_ref, grad_a, grad_b,
    W, n1, ga, gmx, q_ref, k_ref, v_ref, tr, low, x0, x1, m1, u0, u1, act, ctx, gctx, ctxT,
    part, heldy, rs1, rs2s, rs2r, party, rs1y, rs2ys, rs2yr, nx0, sy, syr, gqkv, gt_ref,
    acc, g_ref, gmid, own2, gsend, grecv, lse, outT, foutT, sdp, smp, vecs, bpad, bqkv, b1, packed, small_mp, aT,
    ssem, rsem, p0r,
):
    R = finw.shape[1]
    gk, gv = acc, g_ref
    d = lax.axis_index("dp")
    z = lax.axis_index("mp")
    k = d % 2
    j = d // 2
    zl = z % 2
    zh = z // 2
    qi = 2 * k + zl
    chip_bits = (ndp // 2).bit_length() - 1

    def col(dc, dz):
        zz = z
        if dz & 1:
            zz = zz + 1 - 2 * zl
        if dz & 2:
            zz = zz + 2 - 4 * zh
        return (d + 1 - 2 * k if dc else d, zz)

    sib, zp, swap = col(1, 0), col(0, 1), col(1, 2)
    count = [0]
    sends = []

    def sem():
        count[0] += 1
        return count[0] - 1

    def rcopy(src, dst, dev, keep=False):
        i = sem()
        cp = pltpu.make_async_remote_copy(
            src, dst, ssem.at[i], rsem.at[i], device_id=dev, device_id_type=MESH
        )
        cp.start()
        if keep:
            sends.append(cp.wait_send)
        return cp

    peers = [col(dc, dz) for dc in range(2) for dz in range(4) if dc or dz]
    peers += [(flip(d, bit + 1), z) for bit in range(chip_bits)]
    barrier = pltpu.get_barrier_semaphore()
    for dev in peers:
        pl.semaphore_signal(barrier, inc=1, device_id=dev, device_id_type=MESH)
    pl.semaphore_wait(barrier, len(peers))

    def swap_rows(src, dst_own, dst_other):
        i = sem()
        keep = pltpu.make_async_copy(src, dst_own, rsem.at[i])
        move = pltpu.make_async_remote_copy(
            src, dst_other, ssem.at[i], rsem.at[i], device_id=swap, device_id_type=MESH
        )

        @pl.when(k == zh)
        def _():
            keep.start()

        pl.when(k != zh)(move.start)

        def finish_send():
            @pl.when(k != zh)
            def _():
                move.wait_send()

        sends.append(finish_send)
        return keep.wait

    def many(start, size):
        return pl.ds(pl.multiple_of(start, size), size)

    def block(b):
        return many(b * BLK, BLK)

    def half(h):
        return pl.ds(h * HALF, HALF)

    def spot(b, h):
        return many(h * 4 * HALF + b * HALF, HALF)

    def chunk(c):
        return many(c * BLK, BLK)

    def plain_rows(c):
        at = (c % 2) * 2 * BLK + (c // 2) * HALF
        return many(at, HALF), many(at + BLK, HALF)

    def plain(ref, c):
        one, two = plain_rows(c)
        return jnp.concatenate([ref[one, :], ref[two, :]], axis=0)

    def plain_store(ref, c, value):
        one, two = plain_rows(c)
        ref[one, :] = value[0:HALF]
        ref[two, :] = value[HALF:BLK]

    own_rows = pl.ds(pl.multiple_of(d * R, R), R)
    chip_rows = pl.ds(pl.multiple_of(j * (2 * R), 2 * R), 2 * R)
    slots = (0, 1 + zl, 2 - zl, 3 + zl, 4 - zl, 5, 6, 7)
    sources = {
        0: [(qkvw.at[0, n], n * 256, 256) for n in range(3)] + [(outT.at[0], 768, 256)],
        1: [(finw.at[0], 0, D)],
        3: [(foutT.at[0], 0, D)],
        5: [(qkvw.at[1, n], n * 256, 256) for n in range(3)] + [(outT.at[1], 768, 256)],
        6: [(finw.at[1], 0, D)],
        7: [(foutT.at[1], 0, D)],
    }

    holder = 2 * j + zh
    home = k == zh

    def near(item):
        arrived = p0r.at[item]
        i = sem()
        for src, at, width in sources[item]:
            dst = W.at[slots[item], own_rows, pl.ds(at, width)]

            @pl.when(home)
            def _(src=src, dst=dst):
                pltpu.make_async_copy(src, dst, arrived).start()

            @pl.when(jnp.logical_not(home))
            def _(src=src, dst=dst):
                pltpu.make_async_remote_copy(
                    src, dst, ssem.at[i], arrived, device_id=(holder, z), device_id_type=MESH
                ).start()

        slab = W.at[slots[item], own_rows, :]

        def finish():
            @pl.when(jnp.logical_not(home))
            def _():
                pltpu.make_async_copy(slab, slab, ssem.at[i]).wait()

        sends.append(finish)

    far_sem = {item: sem() for item in sources}

    def far(item):
        i = far_sem[item]
        for src, at, width in sources[item]:
            dst = W.at[slots[item], own_rows, pl.ds(at, width)]
            pltpu.make_async_remote_copy(
                src, dst, ssem.at[i], p0r.at[item], device_id=(holder, swap[1]), device_id_type=MESH
            ).start()

    for item in sources:
        slab = W.at[slots[item], own_rows, :]
        sends.append(pltpu.make_async_copy(slab, slab, ssem.at[far_sem[item]]).wait)

    pass_sem = {1: sem(), 3: sem()}

    def passing(item):
        slab = W.at[slots[item], chip_rows, :]
        i = pass_sem[item]
        return pltpu.make_async_remote_copy(
            slab, slab, ssem.at[i], rsem.at[i], device_id=zp, device_id_type=MESH
        )

    def pass_on(item):
        passing(item).start()

    for item in pass_sem:
        sends.append(passing(item).wait_send)

    def arrive(item):
        if item in (2, 4):
            passing(item - 1).wait_recv()
            return
        slab = W.at[slots[item], chip_rows, :]
        pltpu.make_async_copy(slab, slab, p0r.at[item]).wait()

    half_cols = (pl.ds(0, D // 2), pl.ds(D // 2, D // 2))
    order = (tuple(range(chip_bits)), tuple(reversed(range(chip_bits))))
    stage_sem = {
        (item, stage): (sem(), sem()) for item in range(PIECES) for stage in range(chip_bits)
    }

    def stage_slabs(item, stage):
        for cols, i in zip(half_cols, stage_sem[item, stage]):
            yield W.at[slots[item], pl.ds(0, (1 << stage) * 2 * R), cols], i

    for item, stage in stage_sem:
        for slab, i in stage_slabs(item, stage):
            sends.append(pltpu.make_async_copy(slab, slab, ssem.at[i]).wait)

    def start_stage(item, stage):
        for cols, bits, i in zip(half_cols, order, stage_sem[item, stage]):
            dev = (flip(d, bits[stage] + 1), z)

            def send(m, carry=0, bits=bits, cols=cols, dev=dev, i=i):
                chip = j
                for n, bit in enumerate(bits[:stage]):
                    chip = chip + ((m // (1 << n)) % 2) * (flip(j, bit) - j)
                ref = W.at[slots[item], pl.ds(pl.multiple_of(chip * (2 * R), 2 * R), 2 * R), cols]
                pltpu.make_async_remote_copy(
                    ref, ref, ssem.at[i], rsem.at[i], device_id=dev, device_id_type=MESH
                ).start()
                return carry

            if stage <= 1:
                for m in range(1 << stage):
                    send(m)
            else:
                lax.fori_loop(0, 1 << stage, send, 0)

    def wait_stage(item, stage):
        for slab, i in stage_slabs(item, stage):
            pltpu.make_async_copy(slab, slab, rsem.at[i]).wait()

    def first(*items):
        for item in items:
            arrive(item)
            start_stage(item, 0)

    def later(*items):
        for item in items:
            for stage in range(1, chip_bits):
                wait_stage(item, stage - 1)
                start_stage(item, stage)

    def ready(item):
        wait_stage(item, chip_bits - 1)

    def at_home(f):
        pl.when(home)(f)

    def away(f):
        pl.when(jnp.logical_not(home))(f)

    def share_heads():
        packed[...] = jnp.zeros_like(packed)
        up = ADAPTER_SCALE * second_w[...].astype(F32)
        heads = qkvb[...].astype(F32)
        hidden = finb[...].astype(F32)
        down = first_w[...].astype(F32)
        for layer in range(LAYERS):
            at = 16 * layer
            packed[at : at + 4, 0:256] = up[layer, 0]
            packed[at + 4 : at + 8, 512:768] = up[layer, 1]
            for n in range(3):
                packed[at + 8 : at + 9, n * 256 : (n + 1) * 256] = heads[layer, n : n + 1]
            packed[at + 9 : at + 10, :] = hidden[layer : layer + 1]
        small_mp[...] = packed[...].astype(BF)
        i = sem()
        mine = smp.at[zl]
        copies = [
            pltpu.make_async_remote_copy(
                small_mp, mine, ssem.at[i], rsem.at[i], device_id=col(0, r), device_id_type=MESH
            )
            for r in (1, 2, 3)
        ]
        slab = W.at[0, pl.ds(0, 3 * 32), :]

        @at_home
        def _():
            for cp in copies:
                cp.start()
            pltpu.make_async_copy(small_mp, mine, rsem.at[i]).start()

        def finish():
            at_home(pltpu.make_async_copy(slab, slab, ssem.at[i]).wait)

        sends.append(finish)
        packed[...] = jnp.zeros_like(packed)
        for layer in range(LAYERS):
            at = 16 * layer
            packed[at : at + 4, :] = down[layer, 0]
            packed[at + 4 : at + 8, :] = down[layer, 1]
            aT[layer] = jnp.zeros((128, D), BF)
            aT[layer, 0:16, :] = packed[at : at + 16, :].astype(BF)
        return pltpu.make_async_copy(smp, smp, rsem.at[i]).wait

    def share_small():
        sdp[d] = jnp.zeros((16, 128), F32)
        norm = [gains[...].astype(F32), shifts[...].astype(F32)]
        bias = [outb[...].astype(F32), foutb[...].astype(F32)]
        for layer in range(LAYERS):
            for which in range(2):
                for n in range(2):
                    at = layer * 6 + 2 * which + n
                    sdp[d, at : at + 1, 0:R] = norm[n][layer, which : which + 1]
            for n in range(2):
                at = layer * 6 + 4 + n
                sdp[d, at : at + 1, 0:R] = bias[n][layer : layer + 1]
        bits = tuple(range(1, chip_bits + 1)) + (0,)
        for stage, bit in enumerate(bits):
            i = sem()

            def send(m, carry=0, i=i, bit=bit, stage=stage):
                slot = d
                for n, b in enumerate(bits[:stage]):
                    slot = slot + ((m // (1 << n)) % 2) * (flip(d, b) - d)
                pltpu.make_async_remote_copy(
                    sdp.at[slot], sdp.at[slot], ssem.at[i], rsem.at[i],
                    device_id=(flip(d, bit), z), device_id_type=MESH,
                ).start()
                return carry

            if stage <= 2:
                for m in range(1 << stage):
                    send(m)
            else:
                lax.fori_loop(0, 1 << stage, send, 0)
            slab = sdp.at[pl.ds(0, 1 << stage)]
            pltpu.make_async_copy(slab, slab, rsem.at[i]).wait()
            sends.append(pltpu.make_async_copy(slab, slab, ssem.at[i]).wait)
        for n in range(ndp):
            vecs[:, n * R : (n + 1) * R] = sdp[n, :, 0:R]

    def unpack_small():
        keep = lax.broadcasted_iota(jnp.int32, (16, 768), 0) < 8
        for layer in range(LAYERS):
            tile = smp[zl, 16 * layer : 16 * layer + 16, :].astype(F32)
            bpad[layer] = jnp.zeros((128, 768), BF)
            bpad[layer, 0:16, :] = jnp.where(keep, tile[:, 0:768], 0.0).astype(BF)
            bqkv[layer] = tile[8:9, 0:768]
            for s in range(2):
                b1[layer, s] = smp[s, 16 * layer : 16 * layer + 16, :].astype(F32)[9:10, :]

    def vec(layer, n):
        return vecs[layer * 6 + n : layer * 6 + n + 1, :]

    class Gather:
        def __init__(self, buf, h):
            mine = buf.at[spot(qi, h)]
            self.other = buf.at[spot(2 * k + 1 - zl, h)]
            self.to_z = rcopy(mine, mine, zp)
            self.to_s = rcopy(mine, mine, sib)

        def forward(self):
            self.to_z.wait_recv()
            self.fwd = rcopy(self.other, self.other, sib)

        def chip(self):
            self.to_s.wait_recv()

        def finish(self, chip=True):
            if chip:
                self.chip()
            self.fwd.wait_recv()
            for cp in (self.to_z, self.to_s, self.fwd):
                cp.wait_send()

    first_sums = (part, rs1, rs2s, rs2r)
    late_sums = (party, rs1y, rs2ys, rs2yr)

    class Scatter:
        def __init__(self, partial, h, buffers, dst, base=None):
            p, r1, r2s, r2r = buffers
            self.h, self.dst, self.r2r = h, dst, r2r
            p[h] = partial(2 * h + 1 - k).astype(BF)
            self.first = rcopy(p.at[h], r1.at[h], sib)
            own2[...] = partial(2 * h + k)
            self.first.wait_recv()
            away, here = many((1 - zl) * HALF, HALF), many(zl * HALF, HALF)
            r2s[h] = (own2[away, :] + r1[h, away, :].astype(F32)).astype(BF)
            self.second = rcopy(r2s.at[h], r2r.at[h], zp)
            total = own2[here, :] + r1[h, here, :].astype(F32)
            dst[half(h), :] = total if base is None else total + base(half(h))

        def finish(self):
            self.second.wait_recv()
            self.dst[half(self.h), :] += self.r2r[self.h].astype(F32)
            self.first.wait_send()
            self.second.wait_send()

    class Late:
        def __init__(self, first, second, dst, r2r, h):
            self.first, self.second, self.dst, self.r2r, self.h = first, second, dst, r2r, h

        def finish(self):
            self.second.wait_recv()
            self.dst[half(self.h), :] += self.r2r[self.h].astype(F32)
            self.first.wait_send()
            self.second.wait_send()

    def add_up(partial, buffers, dst):
        p, r1, r2s, r2r = buffers
        away, here = many((1 - zl) * HALF, HALF), many(zl * HALF, HALF)
        first, out = [], []
        for h in range(2):
            p[h] = partial(2 * h + 1 - k).astype(BF)
            first.append(rcopy(p.at[h], r1.at[h], sib))
        for h in range(2):
            own2[...] = partial(2 * h + k)
            first[h].wait_recv()
            r2s[h] = (own2[away, :] + r1[h, away, :].astype(F32)).astype(BF)
            second = rcopy(r2s.at[h], r2r.at[h], zp)
            dst[half(h), :] = own2[here, :] + r1[h, here, :].astype(F32)
            out.append(Late(first[h], second, dst, r2r, h))
        return out

    class Output:
        def begin(self):
            self.first = []
            for h in range(2):
                party[h] = nt(act[2 * h + 1 - k], W[7]).astype(BF)
                self.first.append(rcopy(party.at[h], rs1y.at[h], sib))
            for h in range(2):
                heldy[h] = nt(act[2 * h + k], W[7]).astype(BF)

        def middle(self):
            away, here = many((1 - zl) * HALF, HALF), many(zl * HALF, HALF)
            self.second = []
            for h in range(2):
                self.first[h].wait_recv()
                rs2ys[h] = (heldy[h, away, :].astype(F32) + rs1y[h, away, :].astype(F32)).astype(BF)
                self.second.append(rcopy(rs2ys.at[h], rs2yr.at[h], zp))
                m1[1, half(h), :] += (
                    vec(1, 5) + heldy[h, here, :].astype(F32) + rs1y[h, here, :].astype(F32)
                )

        def finish(self):
            for h in range(2):
                self.second[h].wait_recv()
                self.first[h].wait_send()
                self.second[h].wait_send()
                party[0, half(h), :] = (m1[1, half(h), :] + rs2yr[h].astype(F32)).astype(BF)

    def by_rows(h, f):
        def body(c, carry):
            f(many(h * HALF + c * 64, 64), c * 64)
            return carry

        lax.fori_loop(0, HALF // 64, body, 0)

    def norm_into(src, h, layer, which, dst, start):
        gain, shift = vec(layer, 2 * which), vec(layer, 2 * which + 1)

        def f(rows, at):
            xhat, _ = normed(src[rows, :].astype(F32))
            dst[many(start + at, 64), :] = (xhat * gain + shift).astype(BF)

        by_rows(h, f)

    def spot_start(h):
        return h * 4 * HALF + qi * HALF

    tri = lax.broadcasted_iota(jnp.int32, (BLK, BLK), 0) <= lax.broadcasted_iota(
        jnp.int32, (BLK, BLK), 1
    )
    lane_head = lax.broadcasted_iota(jnp.int32, (1, BLK), 1) // HD

    def project(layer, h):
        w = W.at[ATTENTION[layer]]

        def body(core, carry):
            c = 2 * h + core
            n = n1[layer, chunk(c), :]
            t = nt(n, aT[layer]).astype(BF)
            low[layer, chunk(c), :] = t
            pr = nn(n, w[:, 0:768]) + bqkv[layer] + nn(t, bpad[layer])
            pr = pr.astype(BF)
            plain_store(q_ref.at[layer], c, pr[:, 0:256])
            plain_store(k_ref.at[layer], c, pr[:, 256:512])
            v = pr[:, 512:768]
            plain_store(v_ref.at[layer], c, v)
            vt = v.astype(F32).T.astype(BF)
            one, two = plain_rows(c)
            tr[:, one] = vt[:, 0:HALF]
            tr[:, two] = vt[:, HALF:BLK]
            return carry

        lax.fori_loop(0, 2, body, 0)

    def attend(layer, i):
        lo = i * BLK
        kk, qq = k_ref.at[layer], q_ref.at[layer]

        def pair(hp, carry):
            for s in range(2):
                h = hp * 2 + s
                qm = qq[lo : lo + BLK, :] * jnp.where(lane_head == h, 0.125, 0.0).astype(BF)
                head = pl.ds(pl.multiple_of(h * HD, HD), HD)
                sd = jnp.where(tri, nt(kk[lo : lo + BLK, :], qm), NEG)
                top = jnp.max(sd, axis=0, keepdims=True)
                if i:
                    sa = nt(kk[0:lo, :], qm)
                    top = jnp.maximum(top, jnp.max(sa, axis=0, keepdims=True))
                ed = jnp.exp(sd - top)
                total = jnp.sum(ed, axis=0, keepdims=True)
                o = nn(tr[head, lo : lo + BLK], ed.astype(BF))
                if i:
                    ea = jnp.exp(sa - top)
                    total = total + jnp.sum(ea, axis=0, keepdims=True)
                    o = o + nn(tr[head, 0:lo], ea.astype(BF))
                ctxT[head, :] = o / total
                lse[layer, pl.ds(h, 1), lo : lo + BLK] = top + jnp.log(total)
            return carry

        lax.fori_loop(0, 2, pair, 0)
        ctx[lo : lo + BLK, :] = ctxT[...].T.astype(BF)

    def attend_back(layer, i):
        lo = i * BLK
        kk, qq, vv = k_ref.at[layer], q_ref.at[layer], v_ref.at[layer]

        def pair(hp, carry):
            for s in range(2):
                h = hp * 2 + s
                on = lane_head == h
                qm = qq[lo : lo + BLK, :] * jnp.where(on, 0.125, 0.0).astype(BF)
                gm = gctx[lo : lo + BLK, :] * jnp.where(on, 1.0, 0.0).astype(BF)
                head = pl.ds(pl.multiple_of(h * HD, HD), HD)
                ls = lse[layer, pl.ds(h, 1), lo : lo + BLK]
                spans = [(lo, lo + BLK)] + ([(0, lo)] if i else [])
                ps, ts = [], []
                for a, b in spans:
                    p = jnp.exp(nt(kk[a:b, :], qm) - ls)
                    if a == lo:
                        p = jnp.where(tri, p, 0.0)
                    ps.append(p)
                    ts.append(p * nt(vv[a:b, :], gm))
                dsum = sum(jnp.sum(t, axis=0, keepdims=True) for t in ts)
                o = None
                for (a, b), p, t in zip(spans, ps, ts):
                    gs = (t - p * dsum).astype(BF)
                    dv = nn(p.astype(BF), gm)
                    dk = nn(gs, qm)
                    for c in range(a // BLK, b // BLK):
                        at = pl.ds(c * BLK, BLK)
                        gv[:, at] += dv[c * BLK - a : (c + 1) * BLK - a]
                        gk[:, at] += dk[c * BLK - a : (c + 1) * BLK - a]
                    dq = nn(tr[head, a:b], gs)
                    o = dq if o is None else o + dq
                ctxT[head, :] = o * 0.125
            return carry

        lax.fori_loop(0, 2, pair, 0)
        gqkv[lo : lo + BLK, 0:256] = ctxT[...].T.astype(BF)

    def out_partial(layer):
        w = W.at[ATTENTION[layer]]
        return lambda c: nt(plain(ctx, c), w[:, 768:1024])

    heads_here = share_heads()
    x_moves = [swap_rows(x_in.at[half(h)], x0.at[half(h)], x0.at[half(h)]) for h in range(2)]
    outT[0] = outw[0].astype(F32).T.astype(BF)
    near(0)
    far(0)
    share_small()
    foutT[0] = foutw[0].astype(F32).T.astype(BF)
    near(1)
    near(3)
    at_home(lambda: first(0, 1, 3))
    outT[1] = outw[1].astype(F32).T.astype(BF)
    foutT[1] = foutw[1].astype(F32).T.astype(BF)
    near(5)
    near(6)
    near(7)
    heads_here()
    unpack_small()
    ag = []
    for h in range(2):
        x_moves[h]()
        norm_into(x0, h, 0, 0, n1.at[0], spot_start(h))
        ag.append(Gather(n1.at[0], h))
    away(lambda: far(1))
    at_home(lambda: later(0, 1))
    away(lambda: first(0))
    at_home(lambda: later(3))
    ag[0].forward()
    at_home(lambda: far(1))
    at_home(lambda: first(5))

    @away
    def _():
        later(0)
        first(1)
        pass_on(1)

    ag[1].forward()
    at_home(lambda: pass_on(1))
    far(3)
    at_home(lambda: later(5))
    ag[0].finish()
    ag[1].finish()
    away(lambda: later(1))
    at_home(lambda: pass_on(3))
    ready(0)
    project(0, 0)
    project(0, 1)
    attend(0, 0)
    attend(0, 1)
    at_home(lambda: first(2))

    @away
    def _():
        first(3)
        pass_on(3)

    attend(0, 2)
    attend(0, 3)
    at_home(lambda: later(2))
    away(lambda: later(3))
    sums = add_up(out_partial(0), first_sums, acc)
    at_home(lambda: first(4))

    @away
    def _():
        first(2, 4)
        later(2, 4)

    nx = []
    for h in range(2):
        sums[h].finish()
        m1[0, half(h), :] = x0[half(h), :].astype(F32) + acc[half(h), :] + vec(0, 4)
        norm_into(m1.at[0], h, 0, 1, nx0.at[h], k * HALF)
        mine = nx0.at[h, many(k * HALF, HALF)]
        nx.append(rcopy(mine, mine, sib))
        if h == 0:
            at_home(lambda: later(4))
    far(5)
    far(6)

    away(lambda: first(5))
    cot_here = [
        swap_rows(
            cot_in.at[half(h)], gmx.at[spot(qi, h)], gmx.at[spot(2 * (1 - k) + zl, h)]
        )
        for h in range(2)
    ]
    for cp in nx:
        cp.wait_recv()

    def hidden0(s):
        def body(c, carry):
            h, hc = c // 2, c % 2
            cols = many(hc * 512, 512)
            u = nn(nx0[h], W[1 + s, :, cols]) + b1[0, s, :, cols]
            u0[h, s, :, cols] = u.astype(BF)
            act[2 * h + s, :, cols] = gelu(u).astype(BF)
            return carry

        lax.fori_loop(0, 4, body, 0)

    ready(1)
    hidden0(zl)
    ready(2)
    hidden0(1 - zl)
    for cp in nx:
        cp.wait_send()
    ready(3)
    ready(4)

    def share0(h, value):
        own2[...] = value
        sy[h] = own2[many((1 - k) * HALF, HALF), :].astype(BF)
        cp = rcopy(sy.at[h], syr.at[h], sib)
        acc[half(h), :] = own2[many(k * HALF, HALF), :]

        def finish():
            cp.wait_recv()
            acc[half(h), :] += syr[h].astype(F32)
            cp.wait_send()

        return finish

    ag = []
    ends = [share0(h, nt(act[2 * h], W[3]) + nt(act[2 * h + 1], W[4])) for h in range(2)]
    away(lambda: later(5))
    for h in range(2):
        ends[h]()
        x1[half(h), :] = m1[0, half(h), :] + acc[half(h), :] + vec(0, 5)
        norm_into(x1, h, 1, 0, n1.at[1], spot_start(h))
        ag.append(Gather(n1.at[1], h))
    first(6)
    ag[0].forward()
    ag[0].finish()
    ready(5)
    project(1, 0)
    ag[1].forward()
    ag[1].finish()
    later(6)
    project(1, 1)
    for h in range(2):
        cot_here[h]()
    far(7)
    gm = [Gather(gmx, h) for h in range(2)]
    attend(1, 0)
    attend(1, 1)
    attend(1, 2)
    attend(1, 3)
    sums = add_up(out_partial(1), first_sums, acc)
    first(7)
    ag = []
    for h in range(2):
        sums[h].finish()
        m1[1, half(h), :] = x1[half(h), :] + acc[half(h), :] + vec(1, 4)
        norm_into(m1.at[1], h, 1, 1, ga, spot_start(h))
        ag.append(Gather(ga, h))
        if h == 0:
            later(7)
    gm[0].forward()
    gm[1].forward()
    ready(6)

    def hidden1(h):
        def body(i, carry):
            c, hc = 2 * h + i // 2, i % 2
            cols = many(hc * 512, 512)
            u = nn(ga[chunk(c), :], W[6, :, cols]) + b1[1, zl, :, cols]
            u1[c, :, cols] = u.astype(BF)
            act[c, :, cols] = gelu(u).astype(BF)
            return carry

        lax.fori_loop(0, 4, body, 0)

    def feed_back1(c):
        gh = nn(gmx[chunk(c), :], W[7])
        gu = (gh * gelu_slope(u1[c].astype(F32))).astype(BF)
        return nt(gu, W[6])

    sums = []
    for h in range(2):
        ag[h].forward()
        ag[h].finish()
        hidden1(h)
        if h == 0:
            ready(7)
            gm[0].finish()
            gm[1].finish()
        sums.append(Scatter(feed_back1, h, first_sums, acc))

    def mid_back(layer, h, g_rows):
        gain = vec(layer, 2)

        def f(rows, at):
            v = g_rows(rows, at) + norm_back(m1[layer, rows, :], acc[rows, :], gain)
            gmid[rows, :] = v
            ga[many(spot_start(h) + at, 64), :] = v.astype(BF)

        by_rows(h, f)

    hops = [(flip(d, b), z) for b in range(1, chip_bits + 1)] + [sib, zp, col(0, 2)]

    def reduce_all(layer):
        flight = []

        def hop():
            n = len(flight)
            if n:
                if n > len(hops):
                    return
                flight[-1].wait_recv()
                total = gsend[layer, n - 1] + grecv[layer, n - 1]
                if n == len(hops):
                    for n in range(2):
                        grad_a[layer, n] = total[4 * n : 4 * n + 4]
                        grad_b[layer, n] = total[8 + 4 * n : 12 + 4 * n]
                    flight.append(None)
                    return
                gsend[layer, n] = total
            flight.append(rcopy(gsend.at[layer, n], grecv.at[layer, n], hops[n], keep=True))

        return hop

    def turn(layer):
        def body(c, carry):
            tr[:, block(c)] = k_ref[layer, block(c), :].astype(F32).T.astype(BF)
            return carry

        lax.fori_loop(0, 4, body, 0)

    def attention_back(layer, ag, extra, hop):
        w = W.at[ATTENTION[layer]]

        def down(b):
            rows = jnp.concatenate([ga[spot(b, 0), :], ga[spot(b, 1), :]], axis=0)
            gctx[block(b), :] = nn(rows, w[:, 768:1024]).astype(BF)

        def back(mine, upper):
            for zz in range(2):
                i = 2 * upper + (zz if mine else 1 - zz)

                @pl.when(zl == zz)
                def _(i=i):
                    attend_back(layer, i)

        gk[...] = jnp.zeros_like(gk)
        gv[...] = jnp.zeros_like(gv)
        ag[0].chip()
        ag[1].chip()
        down(zl)
        down(2 + zl)
        back(True, 1)
        ag[0].forward()
        back(True, 0)
        hop()
        ag[1].forward()
        ag[0].finish(False)
        ag[1].finish(False)
        extra()
        down(1 - zl)
        down(3 - zl)
        back(False, 1)
        back(False, 0)
        hop()

        def lows(c, carry):
            gqkv[block(c), 256:512] = gk[:, block(c)].astype(BF)
            gqkv[block(c), 512:768] = gv[:, block(c)].astype(BF)
            gt_ref[block(c), :] = nt(gqkv[block(c), :], bpad[layer]).astype(BF)
            return carry

        lax.fori_loop(0, 4, lows, 0)
        sums = add_up(
            lambda c: nt(plain(gqkv, c), w[:, 0:768]) + nn(plain(gt_ref, c), aT[layer]),
            first_sums, acc,
        )

        def grads(c, carry):
            ga_sum, gb_sum = carry
            gtt = plain(gt_ref, c).astype(F32).T[0:16, :].astype(BF)
            tt = low[layer, chunk(c), :].astype(F32).T[0:16, :].astype(BF)
            return (
                ga_sum + nn(gtt, n1[layer, chunk(c), :]),
                gb_sum + nn(tt, plain(gqkv, c)),
            )

        ga_sum, gb_sum = lax.fori_loop(
            0, 4, grads, (jnp.zeros((16, D), F32), jnp.zeros((16, 768), F32))
        )
        gb = ADAPTER_SCALE * jnp.where(
            lax.broadcasted_iota(jnp.int32, (8, 256), 0) < 4, gb_sum[0:8, 0:256], gb_sum[0:8, 512:768]
        )
        gsend[layer, 0, 0:8, :] = ga_sum[0:8, :]
        gsend[layer, 0, 8:16, :] = jnp.zeros((8, D), F32)
        gsend[layer, 0, 8:16, many(qi * 256, 256)] = gb
        step = reduce_all(layer)
        step()
        return sums, step

    def step_back(layer, h, src):
        gain = vec(layer, 0)

        def f(rows, at):
            g_ref[rows, :] = gmid[rows, :] + norm_back(src[rows, :].astype(F32), acc[rows, :], gain)

        by_rows(h, f)

    output = Output()
    output.begin()
    turn(1)
    ag = []
    for h in range(2):
        sums[h].finish()
        mid_back(
            1, h, lambda rows, at, h=h: gmx[many(spot_start(h) + at, 64), :].astype(F32)
        )
        ag.append(Gather(ga, h))
    sums, hop1 = attention_back(1, ag, output.middle, lambda: None)

    def feed_back0(h):
        total = None
        for s in range(2):
            gh = nn(nx0[h], W[3 + s])
            gu = (gh * gelu_slope(u0[h, s].astype(F32))).astype(BF)
            y = nt(gu, W[1 + s])
            total = y if total is None else total + y
        return total

    def next_rows(h):
        sums[h].finish()
        step_back(1, h, x1)
        nx0[h, many(k * HALF, HALF), :] = g_ref[half(h), :].astype(BF)
        mine = nx0.at[h, many(k * HALF, HALF)]
        return rcopy(mine, mine, sib)

    def after(h):
        ends[h]()
        mid_back(0, h, lambda rows, at: g_ref[rows, :])
        ag.append(Gather(ga, h))

    ag, ends = [], []
    nx = [next_rows(0)]
    turn(0)
    hop1()
    nx[0].wait_recv()
    ends.append(share0(0, feed_back0(0)))
    nx.append(next_rows(1))
    after(0)
    nx[1].wait_recv()
    ends.append(share0(1, feed_back0(1)))
    after(1)
    hop1()
    for cp in nx:
        cp.wait_send()
    out_here = []

    def give_output():
        output.finish()
        for h in range(2):
            out_here.append(
                swap_rows(party.at[0, half(h)], out_ref.at[half(h)], out_ref.at[half(h)])
            )

    sums, hop0 = attention_back(0, ag, give_output, hop1)
    gin_here = []
    for _ in range(len(hops) - 3):
        hop0()
    for h in range(2):
        sums[h].finish()
        step_back(0, h, x0)
        party[1, half(h), :] = g_ref[half(h), :].astype(BF)
        hop0()
        gin_here.append(swap_rows(party.at[1, half(h)], gin_ref.at[half(h)], gin_ref.at[half(h)]))
    for _ in range(len(hops)):
        hop1()
        hop0()
    for h in range(2):
        out_here[h]()
        gin_here[h]()
    for w in sends:
        w()


def shards(
    inputs, qkv_w, qkv_b, out_w, out_b, fin_w, fin_b, fout_w, fout_b, gains, shifts, first, second,
    cotangent,
):
    ndp = lax.axis_size("dp")
    R = qkv_w.shape[1]
    hops = ndp.bit_length() - 1 + 2
    anyspec = pl.BlockSpec(memory_space=pl.ANY)
    vm = pl.BlockSpec(memory_space=pltpu.VMEM)
    V = pltpu.VMEM
    scratch = [
        V((PIECES, D, D), BF),
        V((LAYERS, D, D), BF),
        V((D, D), BF),
        V((D, D), BF),
        V((LAYERS, D, 256), BF),
        V((LAYERS, D, 256), BF),
        V((LAYERS, D, 256), BF),
        V((256, D), BF),
        V((LAYERS, D, 128), BF),
        V((BLK, D), BF),
        V((BLK, D), F32),
        V((LAYERS, BLK, D), F32),
        V((2, 2, BLK, D), BF),
        V((4, BLK, D), BF),
        V((4, BLK, D), BF),
        V((D, 256), BF),
        V((D, 256), BF),
        V((256, 256), F32),
        V((2, BLK, D), BF),
        V((2, BLK, D), BF),
        V((2, BLK, D), BF),
        V((2, HALF, D), BF),
        V((2, HALF, D), BF),
        V((2, BLK, D), BF),
        V((2, BLK, D), BF),
        V((2, HALF, D), BF),
        V((2, HALF, D), BF),
        V((2, BLK, D), BF),
        V((2, HALF, D), BF),
        V((2, HALF, D), BF),
        V((D, 768), BF),
        V((D, 128), BF),
        V((BLK, D), F32),
        V((BLK, D), F32),
        V((BLK, D), F32),
        V((BLK, D), F32),
        V((LAYERS, hops, 16, D), F32),
        V((LAYERS, hops, 16, D), F32),
        V((LAYERS, 8, D), F32),
        V((LAYERS, R, 256), BF),
        V((LAYERS, R, D), BF),
        V((ndp, 16, 128), F32),
        V((2, 32, D), BF),
        V((16, D), F32),
        V((LAYERS, 128, 768), BF),
        V((LAYERS, 1, 768), F32),
        V((LAYERS, 2, 1, D), F32),
        V((LAYERS * 16, D), F32),
        V((LAYERS * 16, D), BF),
        V((LAYERS, 128, D), BF),
        pltpu.SemaphoreType.DMA((200,)),
        pltpu.SemaphoreType.DMA((200,)),
        pltpu.SemaphoreType.DMA((PIECES,)),
    ]
    out, gin, grad_a, grad_b = pl.pallas_call(
        functools.partial(kernel, ndp),
        out_shape=(
            jax.ShapeDtypeStruct((BLK, D), BF),
            jax.ShapeDtypeStruct((BLK, D), BF),
            jax.ShapeDtypeStruct((LAYERS, 2, 4, D), F32),
            jax.ShapeDtypeStruct((LAYERS, 2, 4, D), F32),
        ),
        in_specs=[anyspec] * 4 + [vm] * 10,
        out_specs=(anyspec, anyspec, vm, vm),
        scratch_shapes=scratch,
        compiler_params=pltpu.CompilerParams(
            collective_id=0, has_side_effects=True, vmem_limit_bytes=63 * 2**20
        ),
        name="two_blocks",
    )(
        inputs, cotangent, jnp.swapaxes(qkv_w, 1, 2), fin_w, out_w, fout_w,
        gains, shifts, out_b, fout_b, qkv_b, fin_b, jnp.swapaxes(first, 2, 3), second,
    )
    return (out, gin, jnp.swapaxes(grad_a, 2, 3), grad_b)


def solution(mesh):
    placed = (
        P(("dp", "mp"), None),
        P(None, "dp", None, "mp"),
        P(None, None, "mp"),
        P(None, "mp", "dp"),
        P(None, "dp"),
        P(None, "dp", "mp"),
        P(None, "mp"),
        P(None, "mp", "dp"),
        P(None, "dp"),
        P(None, None, "dp"),
        P(None, None, "dp"),
        P(),
        P(None, None, None, "mp"),
        P(("dp", "mp"), None),
    )
    return jax.shard_map(
        shards,
        mesh=mesh,
        in_specs=placed,
        out_specs=(P(("dp", "mp"), None), P(("dp", "mp"), None), P(), P()),
        check_vma=False,
    )
```

```python
import functools

import jax
import jax.numpy as jnp
from jax import lax
from jax.experimental import pallas as pl
from jax.experimental.pallas import tpu as pltpu
from jax.sharding import PartitionSpec as P

MESH = pl.DeviceIdType.MESH
F32 = jnp.float32
BF = jnp.bfloat16
D = 1024
BLK = 256
HALF = 128
HD = 64
STEP = HD + 16
LAYERS = 2
NORM_EPS = 1e-05
ADAPTER_SCALE = 8.0
C0 = 0.7978845608
C1 = 0.044715
NEG = -1e30

ATTENTION = (0, 5)
PIECES = 8


def nt(a, b):
    return lax.dot_general(a, b, (((1,), (1,)), ((), ())), preferred_element_type=F32)


def nn(a, b):
    return lax.dot_general(a, b, (((1,), (0,)), ((), ())), preferred_element_type=F32)


def flip(value, bit):
    return value + (1 << bit) * (1 - 2 * ((value // (1 << bit)) % 2))


def gelu(u):
    return 0.5 * u * (1.0 + jnp.tanh(C0 * (u + C1 * u * u * u)))


def gelu_slope(u):
    square = u * u
    th = jnp.tanh(C0 * u * (1.0 + C1 * square))
    return 0.5 * (1.0 + th) + 0.5 * u * (1.0 - th * th) * (C0 * (1.0 + 3.0 * C1 * square))


def normed(x):
    c = x - jnp.mean(x, axis=-1, keepdims=True)
    rstd = lax.rsqrt(jnp.mean(c * c, axis=-1, keepdims=True) + NORM_EPS)
    return c * rstd, rstd


def norm_back(x, grad, gain):
    xhat, rstd = normed(x)
    gx = grad * gain
    return rstd * (
        gx
        - jnp.mean(gx, axis=-1, keepdims=True)
        - xhat * jnp.mean(gx * xhat, axis=-1, keepdims=True)
    )


def kernel(
    ndp,
    x_in, cot_in, qkvw, finw, outw, foutw, gains, shifts, outb, foutb, qkvb, finb, first_w, second_w,
    out_ref, gin_ref, grad_a, grad_b,
    W, n1, ga, gmx, q_ref, k_ref, v_ref, tr, low, x0, x1, m1, u0, u1, act, ctx, gctx, ctxT,
    part, rs1, rs2s, rs2r, party, rs1y, rs2ys, rs2yr, nx0, sy, syr, gqkv, gt_ref,
    acc, g_ref, gmid, own2, gsend, grecv, lse, outT, foutT, sdp, smp, vecs, bpad, bqkv, b1, packed, small_mp, aT,
    ssem, rsem, p0r,
):
    R = finw.shape[1]
    gk, gv = acc, g_ref
    d = lax.axis_index("dp")
    z = lax.axis_index("mp")
    k = d % 2
    j = d // 2
    zl = z % 2
    zh = z // 2
    qi = 2 * k + zl
    chip_bits = (ndp // 2).bit_length() - 1

    def col(dc, dz):
        zz = z
        if dz & 1:
            zz = zz + 1 - 2 * zl
        if dz & 2:
            zz = zz + 2 - 4 * zh
        return (d + 1 - 2 * k if dc else d, zz)

    sib, zp, swap = col(1, 0), col(0, 1), col(1, 2)
    count = [0]
    sends = []

    def sem():
        count[0] += 1
        return count[0] - 1

    def rcopy(src, dst, dev, keep=False):
        i = sem()
        cp = pltpu.make_async_remote_copy(
            src, dst, ssem.at[i], rsem.at[i], device_id=dev, device_id_type=MESH
        )
        cp.start()
        if keep:
            sends.append(cp.wait_send)
        return cp

    peers = [col(dc, dz) for dc in range(2) for dz in range(4) if dc or dz]
    peers += [(flip(d, bit + 1), z) for bit in range(chip_bits)]
    barrier = pltpu.get_barrier_semaphore()
    for dev in peers:
        pl.semaphore_signal(barrier, inc=1, device_id=dev, device_id_type=MESH)
    pl.semaphore_wait(barrier, len(peers))

    def swap_rows(src, dst_own, dst_other):
        i = sem()
        keep = pltpu.make_async_copy(src, dst_own, rsem.at[i])
        move = pltpu.make_async_remote_copy(
            src, dst_other, ssem.at[i], rsem.at[i], device_id=swap, device_id_type=MESH
        )

        @pl.when(k == zh)
        def _():
            keep.start()

        pl.when(k != zh)(move.start)

        def finish_send():
            @pl.when(k != zh)
            def _():
                move.wait_send()

        sends.append(finish_send)
        return keep.wait

    def many(start, size):
        return pl.ds(pl.multiple_of(start, size), size)

    def block(b):
        return many(b * BLK, BLK)

    def half(h):
        return pl.ds(h * HALF, HALF)

    def spot(b, h):
        return many(h * 4 * HALF + b * HALF, HALF)

    def chunk(c):
        return many(c * BLK, BLK)

    def plain_rows(c):
        at = (c % 2) * 2 * BLK + (c // 2) * HALF
        return many(at, HALF), many(at + BLK, HALF)

    def plain(ref, c):
        one, two = plain_rows(c)
        return jnp.concatenate([ref[one, :], ref[two, :]], axis=0)

    def plain_store(ref, c, value):
        one, two = plain_rows(c)
        ref[one, :] = value[0:HALF]
        ref[two, :] = value[HALF:BLK]

    own_rows = pl.ds(pl.multiple_of(d * R, R), R)
    chip_rows = pl.ds(pl.multiple_of(j * (2 * R), 2 * R), 2 * R)
    slots = (0, 1 + zl, 2 - zl, 3 + zl, 4 - zl, 5, 6, 7)
    sources = {
        0: [(qkvw.at[0, n], n * 256, 256) for n in range(3)] + [(outT.at[0], 768, 256)],
        1: [(finw.at[0], 0, D)],
        3: [(foutT.at[0], 0, D)],
        5: [(qkvw.at[1, n], n * 256, 256) for n in range(3)] + [(outT.at[1], 768, 256)],
        6: [(finw.at[1], 0, D)],
        7: [(foutT.at[1], 0, D)],
    }

    holder = 2 * j + zh
    home = k == zh

    def near(item):
        arrived = p0r.at[item]
        i = sem()
        for src, at, width in sources[item]:
            dst = W.at[slots[item], own_rows, pl.ds(at, width)]

            @pl.when(home)
            def _(src=src, dst=dst):
                pltpu.make_async_copy(src, dst, arrived).start()

            @pl.when(jnp.logical_not(home))
            def _(src=src, dst=dst):
                pltpu.make_async_remote_copy(
                    src, dst, ssem.at[i], arrived, device_id=(holder, z), device_id_type=MESH
                ).start()

        slab = W.at[slots[item], own_rows, :]

        def finish():
            @pl.when(jnp.logical_not(home))
            def _():
                pltpu.make_async_copy(slab, slab, ssem.at[i]).wait()

        sends.append(finish)

    far_sem = {item: sem() for item in sources}

    def far(item):
        i = far_sem[item]
        for src, at, width in sources[item]:
            dst = W.at[slots[item], own_rows, pl.ds(at, width)]
            pltpu.make_async_remote_copy(
                src, dst, ssem.at[i], p0r.at[item], device_id=(holder, swap[1]), device_id_type=MESH
            ).start()

    for item in sources:
        slab = W.at[slots[item], own_rows, :]
        sends.append(pltpu.make_async_copy(slab, slab, ssem.at[far_sem[item]]).wait)

    pass_sem = {1: sem(), 3: sem()}

    def passing(item):
        slab = W.at[slots[item], chip_rows, :]
        i = pass_sem[item]
        return pltpu.make_async_remote_copy(
            slab, slab, ssem.at[i], rsem.at[i], device_id=zp, device_id_type=MESH
        )

    def pass_on(item):
        passing(item).start()

    for item in pass_sem:
        sends.append(passing(item).wait_send)

    def arrive(item):
        if item in (2, 4):
            passing(item - 1).wait_recv()
            return
        slab = W.at[slots[item], chip_rows, :]
        pltpu.make_async_copy(slab, slab, p0r.at[item]).wait()

    half_cols = (pl.ds(0, D // 2), pl.ds(D // 2, D // 2))
    order = (tuple(range(chip_bits)), tuple(reversed(range(chip_bits))))
    stage_sem = {
        (item, stage): (sem(), sem()) for item in range(PIECES) for stage in range(chip_bits)
    }

    def stage_slabs(item, stage):
        for cols, i in zip(half_cols, stage_sem[item, stage]):
            yield W.at[slots[item], pl.ds(0, (1 << stage) * 2 * R), cols], i

    for item, stage in stage_sem:
        for slab, i in stage_slabs(item, stage):
            sends.append(pltpu.make_async_copy(slab, slab, ssem.at[i]).wait)

    def start_stage(item, stage):
        for cols, bits, i in zip(half_cols, order, stage_sem[item, stage]):
            dev = (flip(d, bits[stage] + 1), z)

            def send(m, carry=0, bits=bits, cols=cols, dev=dev, i=i):
                chip = j
                for n, bit in enumerate(bits[:stage]):
                    chip = chip + ((m // (1 << n)) % 2) * (flip(j, bit) - j)
                ref = W.at[slots[item], pl.ds(pl.multiple_of(chip * (2 * R), 2 * R), 2 * R), cols]
                pltpu.make_async_remote_copy(
                    ref, ref, ssem.at[i], rsem.at[i], device_id=dev, device_id_type=MESH
                ).start()
                return carry

            if stage <= 1:
                for m in range(1 << stage):
                    send(m)
            else:
                lax.fori_loop(0, 1 << stage, send, 0)

    def wait_stage(item, stage):
        for slab, i in stage_slabs(item, stage):
            pltpu.make_async_copy(slab, slab, rsem.at[i]).wait()

    def first(*items):
        for item in items:
            arrive(item)
            start_stage(item, 0)

    def later(*items):
        for item in items:
            for stage in range(1, chip_bits):
                wait_stage(item, stage - 1)
                start_stage(item, stage)

    def ready(item):
        wait_stage(item, chip_bits - 1)

    def at_home(f):
        pl.when(home)(f)

    def away(f):
        pl.when(jnp.logical_not(home))(f)

    def share_heads():
        packed[...] = jnp.zeros_like(packed)
        up = ADAPTER_SCALE * second_w[...].astype(F32)
        heads = qkvb[...].astype(F32)
        hidden = finb[...].astype(F32)
        down = first_w[...].astype(F32)
        for layer in range(LAYERS):
            at = 16 * layer
            packed[at : at + 4, 0:256] = up[layer, 0]
            packed[at + 4 : at + 8, 512:768] = up[layer, 1]
            for n in range(3):
                packed[at + 8 : at + 9, n * 256 : (n + 1) * 256] = heads[layer, n : n + 1]
            packed[at + 9 : at + 10, :] = hidden[layer : layer + 1]
        small_mp[...] = packed[...].astype(BF)
        i = sem()
        mine = smp.at[zl]
        copies = [
            pltpu.make_async_remote_copy(
                small_mp, mine, ssem.at[i], rsem.at[i], device_id=col(0, r), device_id_type=MESH
            )
            for r in (1, 2, 3)
        ]
        slab = W.at[0, pl.ds(0, 3 * 32), :]

        @at_home
        def _():
            for cp in copies:
                cp.start()
            pltpu.make_async_copy(small_mp, mine, rsem.at[i]).start()

        def finish():
            at_home(pltpu.make_async_copy(slab, slab, ssem.at[i]).wait)

        sends.append(finish)
        packed[...] = jnp.zeros_like(packed)
        for layer in range(LAYERS):
            at = 16 * layer
            packed[at : at + 4, :] = down[layer, 0]
            packed[at + 4 : at + 8, :] = down[layer, 1]
            aT[layer] = jnp.zeros((128, D), BF)
            aT[layer, 0:16, :] = packed[at : at + 16, :].astype(BF)
        return pltpu.make_async_copy(smp, smp, rsem.at[i]).wait

    def share_small():
        sdp[d] = jnp.zeros((16, 128), F32)
        norm = [gains[...].astype(F32), shifts[...].astype(F32)]
        bias = [outb[...].astype(F32), foutb[...].astype(F32)]
        for layer in range(LAYERS):
            for which in range(2):
                for n in range(2):
                    at = layer * 6 + 2 * which + n
                    sdp[d, at : at + 1, 0:R] = norm[n][layer, which : which + 1]
            for n in range(2):
                at = layer * 6 + 4 + n
                sdp[d, at : at + 1, 0:R] = bias[n][layer : layer + 1]
        bits = tuple(range(1, chip_bits + 1)) + (0,)
        for stage, bit in enumerate(bits):
            i = sem()

            def send(m, carry=0, i=i, bit=bit, stage=stage):
                slot = d
                for n, b in enumerate(bits[:stage]):
                    slot = slot + ((m // (1 << n)) % 2) * (flip(d, b) - d)
                pltpu.make_async_remote_copy(
                    sdp.at[slot], sdp.at[slot], ssem.at[i], rsem.at[i],
                    device_id=(flip(d, bit), z), device_id_type=MESH,
                ).start()
                return carry

            if stage <= 2:
                for m in range(1 << stage):
                    send(m)
            else:
                lax.fori_loop(0, 1 << stage, send, 0)
            slab = sdp.at[pl.ds(0, 1 << stage)]
            pltpu.make_async_copy(slab, slab, rsem.at[i]).wait()
            sends.append(pltpu.make_async_copy(slab, slab, ssem.at[i]).wait)
        for n in range(ndp):
            vecs[:, n * R : (n + 1) * R] = sdp[n, :, 0:R]

    def unpack_small():
        keep = lax.broadcasted_iota(jnp.int32, (16, 768), 0) < 8
        for layer in range(LAYERS):
            tile = smp[zl, 16 * layer : 16 * layer + 16, :].astype(F32)
            bpad[layer] = jnp.zeros((128, 768), BF)
            bpad[layer, 0:16, :] = jnp.where(keep, tile[:, 0:768], 0.0).astype(BF)
            bqkv[layer] = tile[8:9, 0:768]
            for s in range(2):
                b1[layer, s] = smp[s, 16 * layer : 16 * layer + 16, :].astype(F32)[9:10, :]

    def vec(layer, n):
        return vecs[layer * 6 + n : layer * 6 + n + 1, :]

    class Gather:
        def __init__(self, buf, h):
            mine = buf.at[spot(qi, h)]
            self.other = buf.at[spot(2 * k + 1 - zl, h)]
            self.to_z = rcopy(mine, mine, zp)
            self.to_s = rcopy(mine, mine, sib)

        def forward(self):
            self.to_z.wait_recv()
            self.fwd = rcopy(self.other, self.other, sib)

        def chip(self):
            self.to_s.wait_recv()

        def finish(self, chip=True):
            if chip:
                self.chip()
            self.fwd.wait_recv()
            for cp in (self.to_z, self.to_s, self.fwd):
                cp.wait_send()

    first_sums = (part, rs1, rs2s, rs2r)
    late_sums = (party, rs1y, rs2ys, rs2yr)

    class Scatter:
        def __init__(self, partial, h, buffers, dst, base=None):
            p, r1, r2s, r2r = buffers
            self.h, self.dst, self.r2r = h, dst, r2r
            p[h] = partial(2 * h + 1 - k).astype(BF)
            self.first = rcopy(p.at[h], r1.at[h], sib)
            own2[...] = partial(2 * h + k)
            self.first.wait_recv()
            away, here = many((1 - zl) * HALF, HALF), many(zl * HALF, HALF)
            r2s[h] = (own2[away, :] + r1[h, away, :].astype(F32)).astype(BF)
            self.second = rcopy(r2s.at[h], r2r.at[h], zp)
            total = own2[here, :] + r1[h, here, :].astype(F32)
            dst[half(h), :] = total if base is None else total + base(half(h))

        def finish(self):
            self.second.wait_recv()
            self.dst[half(self.h), :] += self.r2r[self.h].astype(F32)
            self.first.wait_send()
            self.second.wait_send()

    class Late:
        def __init__(self, first, second, dst, r2r, h):
            self.first, self.second, self.dst, self.r2r, self.h = first, second, dst, r2r, h

        def finish(self):
            self.second.wait_recv()
            self.dst[half(self.h), :] += self.r2r[self.h].astype(F32)
            self.first.wait_send()
            self.second.wait_send()

    def add_up(partial, buffers, dst):
        p, r1, r2s, r2r = buffers
        away, here = many((1 - zl) * HALF, HALF), many(zl * HALF, HALF)
        first, out = [], []
        for h in range(2):
            p[h] = partial(2 * h + 1 - k).astype(BF)
            first.append(rcopy(p.at[h], r1.at[h], sib))
        for h in range(2):
            own2[...] = partial(2 * h + k)
            first[h].wait_recv()
            r2s[h] = (own2[away, :] + r1[h, away, :].astype(F32)).astype(BF)
            second = rcopy(r2s.at[h], r2r.at[h], zp)
            dst[half(h), :] = own2[here, :] + r1[h, here, :].astype(F32)
            out.append(Late(first[h], second, dst, r2r, h))
        return out

    class Output:
        def begin(self):
            self.first = []
            for h in range(2):
                party[h] = nt(act[2 * h + 1 - k], W[7]).astype(BF)
                self.first.append(rcopy(party.at[h], rs1y.at[h], sib))
            for h in range(2):
                nx0[h] = nt(act[2 * h + k], W[7]).astype(BF)

        def middle(self):
            away, here = many((1 - zl) * HALF, HALF), many(zl * HALF, HALF)
            self.second = []
            for h in range(2):
                self.first[h].wait_recv()
                rs2ys[h] = (nx0[h, away, :].astype(F32) + rs1y[h, away, :].astype(F32)).astype(BF)
                self.second.append(rcopy(rs2ys.at[h], rs2yr.at[h], zp))
                m1[1, half(h), :] += (
                    vec(1, 5) + nx0[h, here, :].astype(F32) + rs1y[h, here, :].astype(F32)
                )

        def finish(self):
            for h in range(2):
                self.second[h].wait_recv()
                self.first[h].wait_send()
                self.second[h].wait_send()
                party[0, half(h), :] = (m1[1, half(h), :] + rs2yr[h].astype(F32)).astype(BF)

    def by_rows(h, f):
        def body(c, carry):
            f(many(h * HALF + c * 64, 64), c * 64)
            return carry

        lax.fori_loop(0, HALF // 64, body, 0)

    def norm_into(src, h, layer, which, dst, start):
        gain, shift = vec(layer, 2 * which), vec(layer, 2 * which + 1)

        def f(rows, at):
            xhat, _ = normed(src[rows, :].astype(F32))
            dst[many(start + at, 64), :] = (xhat * gain + shift).astype(BF)

        by_rows(h, f)

    def spot_start(h):
        return h * 4 * HALF + qi * HALF

    tri = lax.broadcasted_iota(jnp.int32, (BLK, BLK), 0) <= lax.broadcasted_iota(
        jnp.int32, (BLK, BLK), 1
    )
    lane_head = lax.broadcasted_iota(jnp.int32, (1, BLK), 1) // HD
    head_rows = (
        lax.broadcasted_iota(jnp.int32, (8, BLK), 1) // HD
        == lax.broadcasted_iota(jnp.int32, (8, BLK), 0)
    ).astype(BF)

    def project(layer, h):
        w = W.at[ATTENTION[layer]]

        def body(core, carry):
            c = 2 * h + core
            rows = n1[layer, chunk(c), :]
            t = nt(rows, aT[layer]).astype(BF)
            low[layer, chunk(c), :] = t
            pr = nn(rows, w[:, 0:768]) + bqkv[layer] + nn(t, bpad[layer])
            pr = pr.astype(BF)
            plain_store(q_ref.at[layer], c, pr[:, 0:256])
            plain_store(k_ref.at[layer], c, pr[:, 256:512])
            v = pr[:, 512:768]
            plain_store(v_ref.at[layer], c, v)
            vt = v.astype(F32).T.astype(BF)
            one, two = plain_rows(c)
            for n in range(4):
                tr[STEP * n : STEP * n + HD, one] = vt[n * HD : (n + 1) * HD, 0:HALF]
                tr[STEP * n : STEP * n + HD, two] = vt[n * HD : (n + 1) * HD, HALF:BLK]
            return carry

        lax.fori_loop(0, 2, body, 0)

    def attend(layer, i):
        lo = i * BLK
        kk, qq = k_ref.at[layer], q_ref.at[layer]
        for h in range(4):
            qm = qq[lo : lo + BLK, :] * jnp.where(lane_head == h, 0.125, 0.0).astype(BF)
            rows = pl.ds(STEP * h, STEP)
            sd = jnp.where(tri, nt(kk[lo : lo + BLK, :], qm), NEG)
            top = jnp.max(sd, axis=0, keepdims=True)
            if i:
                sa = nt(kk[0:lo, :], qm)
                top = jnp.maximum(top, jnp.max(sa, axis=0, keepdims=True))
            o = nn(tr[rows, lo : lo + BLK], jnp.exp(sd - top).astype(BF))
            if i:
                o = o + nn(tr[rows, 0:lo], jnp.exp(sa - top).astype(BF))
            total = o[HD : HD + 1]
            ctxT[h * HD : (h + 1) * HD, :] = o[0:HD] * (1.0 / total)
            lse[layer, h : h + 1, lo : lo + BLK] = top + jnp.log(total)
        ctx[layer, lo : lo + BLK, :] = ctxT[...].T.astype(BF)

    def attend_back(layer, i):
        lo = i * BLK
        kk, qq, vv = k_ref.at[layer], q_ref.at[layer], v_ref.at[layer]
        grad = gctx[lo : lo + BLK, :]
        product = grad.astype(F32) * ctx[layer, lo : lo + BLK, :].astype(F32)
        high = product.astype(BF)
        sums = nt(head_rows, high) + nt(head_rows, (product - high.astype(F32)).astype(BF))
        spans = [(lo, lo + BLK)] + ([(0, lo)] if i else [])
        for pair in range(2):
            queries, grads, parts = [], [], [([], []) for _ in spans]
            for h in (2 * pair, 2 * pair + 1):
                on = lane_head == h
                qm = qq[lo : lo + BLK, :] * jnp.where(on, 0.125, 0.0).astype(BF)
                gm = grad * jnp.where(on, 1.0, 0.0).astype(BF)
                ls = lse[layer, h : h + 1, lo : lo + BLK]
                dq = None
                for (a, b), (ps, gss) in zip(spans, parts):
                    p = jnp.exp(nt(kk[a:b, :], qm) - ls)
                    if a == lo:
                        p = jnp.where(tri, p, 0.0)
                    gs = (p * (nt(vv[a:b, :], gm) - sums[h : h + 1])).astype(BF)
                    y = nn(tr[STEP * h : STEP * h + HD, a:b], gs)
                    dq = y if dq is None else dq + y
                    ps.append(p.astype(BF))
                    gss.append(gs)
                ctxT[h * HD : (h + 1) * HD, :] = dq * 0.125
                queries.append(qm)
                grads.append(gm)
            queries, grads = jnp.concatenate(queries, axis=0), jnp.concatenate(grads, axis=0)
            for (a, b), (ps, gss) in zip(spans, parts):
                dv = nn(jnp.concatenate(ps, axis=1), grads)
                dk = nn(jnp.concatenate(gss, axis=1), queries)
                for c in range(a // BLK, b // BLK):
                    at = pl.ds(c * BLK, BLK)
                    gv[:, at] += dv[c * BLK - a : (c + 1) * BLK - a]
                    gk[:, at] += dk[c * BLK - a : (c + 1) * BLK - a]
        gqkv[lo : lo + BLK, 0:256] = ctxT[...].T.astype(BF)

    def out_partial(layer):
        w = W.at[ATTENTION[layer]]
        return lambda c: nt(plain(ctx.at[layer], c), w[:, 768:1024])

    heads_here = share_heads()
    for h in range(4):
        tr[STEP * h + HD : STEP * (h + 1), :] = jnp.ones((STEP - HD, D), BF)
    x_moves = [swap_rows(x_in.at[half(h)], x0.at[half(h)], x0.at[half(h)]) for h in range(2)]
    outT[0] = outw[0].astype(F32).T.astype(BF)
    near(0)
    far(0)
    share_small()
    foutT[0] = foutw[0].astype(F32).T.astype(BF)
    near(1)
    near(3)
    at_home(lambda: first(0, 1, 3))
    outT[1] = outw[1].astype(F32).T.astype(BF)
    foutT[1] = foutw[1].astype(F32).T.astype(BF)
    near(5)
    near(6)
    near(7)
    heads_here()
    unpack_small()
    ag = []
    for h in range(2):
        x_moves[h]()
        norm_into(x0, h, 0, 0, n1.at[0], spot_start(h))
        ag.append(Gather(n1.at[0], h))
    away(lambda: far(1))
    at_home(lambda: later(0, 1))
    away(lambda: first(0))
    at_home(lambda: later(3))
    ag[0].forward()
    at_home(lambda: far(1))
    at_home(lambda: first(5))

    @away
    def _():
        later(0)
        first(1)
        pass_on(1)

    ag[1].forward()
    at_home(lambda: pass_on(1))
    far(3)
    at_home(lambda: later(5))
    ag[0].finish()
    ag[1].finish()
    away(lambda: later(1))
    at_home(lambda: pass_on(3))
    ready(0)
    project(0, 0)
    project(0, 1)
    attend(0, 0)
    attend(0, 1)
    cot_here = [
        swap_rows(
            cot_in.at[half(h)], gmx.at[spot(qi, h)], gmx.at[spot(2 * (1 - k) + zl, h)]
        )
        for h in range(2)
    ]
    at_home(lambda: first(2))

    @away
    def _():
        first(3)
        pass_on(3)

    attend(0, 2)
    attend(0, 3)
    at_home(lambda: later(2))
    away(lambda: later(3))
    sums = add_up(out_partial(0), first_sums, acc)
    far(5)
    at_home(lambda: first(4))

    @away
    def _():
        first(2, 4)
        later(2, 4)

    nx = []
    for h in range(2):
        sums[h].finish()
        m1[0, half(h), :] = x0[half(h), :].astype(F32) + acc[half(h), :] + vec(0, 4)
        norm_into(m1.at[0], h, 0, 1, nx0.at[h], k * HALF)
        mine = nx0.at[h, many(k * HALF, HALF)]
        nx.append(rcopy(mine, mine, sib))
        if h == 0:
            at_home(lambda: later(4))
    far(6)
    for cp in nx:
        cp.wait_recv()

    def hidden0(s):
        def body(h, carry):
            for hc in range(2):
                cols = pl.ds(hc * 512, 512)
                u = nn(nx0[h], W[1 + s, :, cols]) + b1[0, s, :, cols]
                u0[h, s, :, cols] = u.astype(BF)
                act[2 * h + s, :, cols] = gelu(u).astype(BF)
            return carry

        lax.fori_loop(0, 2, body, 0)

    ready(1)
    hidden0(zl)
    ready(2)
    hidden0(1 - zl)
    away(lambda: first(5))
    for cp in nx:
        cp.wait_send()
    ready(3)
    ready(4)

    def share0(h, value):
        own2[...] = value
        sy[h] = own2[many((1 - k) * HALF, HALF), :].astype(BF)
        cp = rcopy(sy.at[h], syr.at[h], sib)
        acc[half(h), :] = own2[many(k * HALF, HALF), :]

        def finish():
            cp.wait_recv()
            acc[half(h), :] += syr[h].astype(F32)
            cp.wait_send()

        return finish

    ag = []
    ends = [share0(h, nt(act[2 * h], W[3]) + nt(act[2 * h + 1], W[4])) for h in range(2)]
    away(lambda: later(5))
    for h in range(2):
        ends[h]()
        x1[half(h), :] = m1[0, half(h), :] + acc[half(h), :] + vec(0, 5)
        norm_into(x1, h, 1, 0, n1.at[1], spot_start(h))
        ag.append(Gather(n1.at[1], h))
    first(6)
    ag[0].forward()
    ag[0].finish()
    ready(5)
    project(1, 0)
    ag[1].forward()
    ag[1].finish()
    later(6)
    project(1, 1)
    for h in range(2):
        cot_here[h]()
    far(7)
    gm = [Gather(gmx, h) for h in range(2)]
    attend(1, 0)
    attend(1, 1)
    attend(1, 2)
    attend(1, 3)
    sums = add_up(out_partial(1), first_sums, acc)
    first(7)
    later(7)
    ag = []
    for h in range(2):
        sums[h].finish()
        m1[1, half(h), :] = x1[half(h), :] + acc[half(h), :] + vec(1, 4)
        norm_into(m1.at[1], h, 1, 1, ga, spot_start(h))
        ag.append(Gather(ga, h))
    gm[0].forward()
    gm[1].forward()
    ready(6)

    def hidden1(h):
        def body(core, carry):
            c = 2 * h + core
            for hc in range(2):
                cols = pl.ds(hc * 512, 512)
                u = nn(ga[chunk(c), :], W[6, :, cols]) + b1[1, zl, :, cols]
                u1[c, :, cols] = u.astype(BF)
                act[c, :, cols] = gelu(u).astype(BF)
            return carry

        lax.fori_loop(0, 2, body, 0)

    def feed_back1(c):
        gh = nn(gmx[chunk(c), :], W[7])
        gu = (gh * gelu_slope(u1[c].astype(F32))).astype(BF)
        return nt(gu, W[6])

    sums = []
    for h in range(2):
        ag[h].forward()
        ag[h].finish()
        hidden1(h)
        if h == 0:
            ready(7)
            gm[0].finish()
            gm[1].finish()
        sums.append(Scatter(feed_back1, h, first_sums, acc))

    def mid_back(layer, h, g_rows):
        gain = vec(layer, 2)

        def f(rows, at):
            v = g_rows(rows, at) + norm_back(m1[layer, rows, :], acc[rows, :], gain)
            gmid[rows, :] = v
            ga[many(spot_start(h) + at, 64), :] = v.astype(BF)

        by_rows(h, f)

    hops = [(flip(d, b), z) for b in range(1, chip_bits + 1)] + [sib, zp, col(0, 2)]

    def reduce_all(layer):
        flight = []

        def hop():
            n = len(flight)
            if n:
                if n > len(hops):
                    return
                flight[-1].wait_recv()
                total = gsend[layer, (n - 1) % 2] + grecv[layer, n - 1]
                if n == len(hops):
                    for cp in flight[-2:]:
                        cp.wait_send()
                    for n in range(2):
                        grad_a[layer, n] = total[4 * n : 4 * n + 4]
                        grad_b[layer, n] = total[8 + 4 * n : 12 + 4 * n]
                    flight.append(None)
                    return
                if n > 1:
                    flight[n - 2].wait_send()
                gsend[layer, n % 2] = total
            flight.append(rcopy(gsend.at[layer, n % 2], grecv.at[layer, n], hops[n]))

        return hop

    def turn(layer):
        def body(c, carry):
            kt = k_ref[layer, block(c), :].astype(F32).T.astype(BF)
            for n in range(4):
                tr[STEP * n : STEP * n + HD, block(c)] = kt[n * HD : (n + 1) * HD]
            return carry

        lax.fori_loop(0, 4, body, 0)

    def attention_back(layer, ag, extra, hop):
        w = W.at[ATTENTION[layer]]

        def down(b):
            rows = jnp.concatenate([ga[spot(b, 0), :], ga[spot(b, 1), :]], axis=0)
            gctx[block(b), :] = nn(rows, w[:, 768:1024]).astype(BF)

        gk[...] = jnp.zeros_like(gk)
        gv[...] = jnp.zeros_like(gv)
        ag[0].chip()
        ag[1].chip()

        def back(mine, upper):
            for zz in range(2):
                i = 2 * upper + (zz if mine else 1 - zz)

                @pl.when(zl == zz)
                def _(i=i):
                    attend_back(layer, i)

        down(zl)
        down(2 + zl)
        back(True, 1)
        ag[0].forward()
        back(True, 0)
        ag[1].forward()
        ag[0].finish(False)
        ag[1].finish(False)
        extra()
        down(1 - zl)
        down(3 - zl)
        back(False, 1)
        back(False, 0)
        hop()

        def lows(c, carry):
            gqkv[block(c), 256:512] = gk[:, block(c)].astype(BF)
            gqkv[block(c), 512:768] = gv[:, block(c)].astype(BF)
            gt_ref[block(c), :] = nt(gqkv[block(c), :], bpad[layer]).astype(BF)
            return carry

        lax.fori_loop(0, 4, lows, 0)
        step = reduce_all(layer)

        def adapters():
            def grads(c, carry):
                ga_sum, gb_sum = carry
                gtt = plain(gt_ref, c).astype(F32).T[0:16, :].astype(BF)
                tt = low[layer, chunk(c), :].astype(F32).T[0:16, :].astype(BF)
                return (
                    ga_sum + nn(gtt, n1[layer, chunk(c), :]),
                    gb_sum + nn(tt, plain(gqkv, c)),
                )

            ga_sum, gb_sum = lax.fori_loop(
                0, 4, grads, (jnp.zeros((16, D), F32), jnp.zeros((16, 768), F32))
            )
            gb = ADAPTER_SCALE * jnp.where(
                lax.broadcasted_iota(jnp.int32, (8, 256), 0) < 4, gb_sum[0:8, 0:256], gb_sum[0:8, 512:768]
            )
            gsend[layer, 0, 0:8, :] = ga_sum[0:8, :]
            gsend[layer, 0, 8:16, :] = jnp.zeros((8, D), F32)
            gsend[layer, 0, 8:16, many(qi * 256, 256)] = gb
            step()

        if layer == 0:
            adapters()
        sums = add_up(
            lambda c: nt(plain(gqkv, c), w[:, 0:768]) + nn(plain(gt_ref, c), aT[layer]),
            first_sums, acc,
        )
        if layer == 1:
            adapters()
        return sums, step

    def step_back(layer, h, src):
        gain = vec(layer, 0)

        def f(rows, at):
            g_ref[rows, :] = gmid[rows, :] + norm_back(src[rows, :].astype(F32), acc[rows, :], gain)

        by_rows(h, f)

    output = Output()
    output.begin()
    turn(1)
    ag = []
    for h in range(2):
        sums[h].finish()
        mid_back(
            1, h, lambda rows, at, h=h: gmx[many(spot_start(h) + at, 64), :].astype(F32)
        )
        ag.append(Gather(ga, h))
    sums, hop1 = attention_back(1, ag, output.middle, lambda: None)

    def feed_back0(h):
        total = None
        for s in range(2):
            gh = nn(nx0[h], W[3 + s])
            gu = (gh * gelu_slope(u0[h, s].astype(F32))).astype(BF)
            y = nt(gu, W[1 + s])
            total = y if total is None else total + y
        return total

    def next_rows(h):
        sums[h].finish()
        step_back(1, h, x1)
        nx0[h, many(k * HALF, HALF), :] = g_ref[half(h), :].astype(BF)
        mine = nx0.at[h, many(k * HALF, HALF)]
        return rcopy(mine, mine, sib)

    def after(h):
        ends[h]()
        mid_back(0, h, lambda rows, at: g_ref[rows, :])
        ag.append(Gather(ga, h))

    ag, ends = [], []
    nx = [next_rows(0)]
    turn(0)
    hop1()
    nx[0].wait_recv()
    ends.append(share0(0, feed_back0(0)))
    hop1()
    nx.append(next_rows(1))
    after(0)
    nx[1].wait_recv()
    ends.append(share0(1, feed_back0(1)))
    after(1)
    hop1()
    for cp in nx:
        cp.wait_send()
    out_here = []

    def give_output():
        output.finish()
        for h in range(2):
            out_here.append(
                swap_rows(party.at[0, half(h)], out_ref.at[half(h)], out_ref.at[half(h)])
            )

    sums, hop0 = attention_back(0, ag, lambda: (hop1(), give_output()), lambda: None)
    gin_here = []
    for _ in range(len(hops) - 3):
        hop0()
    for h in range(2):
        sums[h].finish()
        step_back(0, h, x0)
        party[1, half(h), :] = g_ref[half(h), :].astype(BF)
        gin_here.append(swap_rows(party.at[1, half(h)], gin_ref.at[half(h)], gin_ref.at[half(h)]))
        hop0()
    for _ in hops:
        hop0()
    for _ in hops:
        hop1()
    for h in range(2):
        out_here[h]()
        gin_here[h]()
    for w in sends:
        w()


def shards(
    inputs, qkv_w, qkv_b, out_w, out_b, fin_w, fin_b, fout_w, fout_b, gains, shifts, first, second,
    cotangent,
):
    ndp = lax.axis_size("dp")
    R = qkv_w.shape[1]
    hops = ndp.bit_length() - 1 + 2
    anyspec = pl.BlockSpec(memory_space=pl.ANY)
    vm = pl.BlockSpec(memory_space=pltpu.VMEM)
    V = pltpu.VMEM
    scratch = [
        V((PIECES, D, D), BF),
        V((LAYERS, D, D), BF),
        V((D, D), BF),
        V((D, D), BF),
        V((LAYERS, D, 256), BF),
        V((LAYERS, D, 256), BF),
        V((LAYERS, D, 256), BF),
        V((4 * STEP, D), BF),
        V((LAYERS, D, 128), BF),
        V((BLK, D), BF),
        V((BLK, D), F32),
        V((LAYERS, BLK, D), F32),
        V((2, 2, BLK, D), BF),
        V((4, BLK, D), BF),
        V((4, BLK, D), BF),
        V((LAYERS, D, 256), BF),
        V((D, 256), BF),
        V((256, 256), F32),
        V((2, BLK, D), BF),
        V((2, BLK, D), BF),
        V((2, HALF, D), BF),
        V((2, HALF, D), BF),
        V((2, BLK, D), BF),
        V((2, BLK, D), BF),
        V((2, HALF, D), BF),
        V((2, HALF, D), BF),
        V((2, BLK, D), BF),
        V((2, HALF, D), BF),
        V((2, HALF, D), BF),
        V((D, 768), BF),
        V((D, 128), BF),
        V((BLK, D), F32),
        V((BLK, D), F32),
        V((BLK, D), F32),
        V((BLK, D), F32),
        V((LAYERS, 2, 16, D), F32),
        V((LAYERS, hops, 16, D), F32),
        V((LAYERS, 8, D), F32),
        V((LAYERS, R, 256), BF),
        V((LAYERS, R, D), BF),
        V((ndp, 16, 128), F32),
        V((2, 32, D), BF),
        V((16, D), F32),
        V((LAYERS, 128, 768), BF),
        V((LAYERS, 1, 768), F32),
        V((LAYERS, 2, 1, D), F32),
        V((LAYERS * 16, D), F32),
        V((LAYERS * 16, D), BF),
        V((LAYERS, 128, D), BF),
        pltpu.SemaphoreType.DMA((200,)),
        pltpu.SemaphoreType.DMA((200,)),
        pltpu.SemaphoreType.DMA((PIECES,)),
    ]
    out, gin, grad_a, grad_b = pl.pallas_call(
        functools.partial(kernel, ndp),
        out_shape=(
            jax.ShapeDtypeStruct((BLK, D), BF),
            jax.ShapeDtypeStruct((BLK, D), BF),
            jax.ShapeDtypeStruct((LAYERS, 2, 4, D), F32),
            jax.ShapeDtypeStruct((LAYERS, 2, 4, D), F32),
        ),
        in_specs=[anyspec] * 4 + [vm] * 10,
        out_specs=(anyspec, anyspec, vm, vm),
        scratch_shapes=scratch,
        compiler_params=pltpu.CompilerParams(
            collective_id=0, has_side_effects=True, vmem_limit_bytes=63 * 2**20
        ),
        name="two_blocks",
    )(
        inputs, cotangent, jnp.swapaxes(qkv_w, 1, 2), fin_w, out_w, fout_w,
        gains, shifts, out_b, fout_b, qkv_b, fin_b, jnp.swapaxes(first, 2, 3), second,
    )
    return (out, gin, jnp.swapaxes(grad_a, 2, 3), grad_b)


def solution(mesh):
    placed = (
        P(("dp", "mp"), None),
        P(None, "dp", None, "mp"),
        P(None, None, "mp"),
        P(None, "mp", "dp"),
        P(None, "dp"),
        P(None, "dp", "mp"),
        P(None, "mp"),
        P(None, "mp", "dp"),
        P(None, "dp"),
        P(None, None, "dp"),
        P(None, None, "dp"),
        P(),
        P(None, None, None, "mp"),
        P(("dp", "mp"), None),
    )
    return jax.shard_map(
        shards,
        mesh=mesh,
        in_specs=placed,
        out_specs=(P(("dp", "mp"), None), P(("dp", "mp"), None), P(), P()),
        check_vma=False,
    )
```

```python
import functools

import jax
import jax.numpy as jnp
from jax import lax
from jax.experimental import pallas as pl
from jax.experimental.pallas import tpu as pltpu
from jax.sharding import PartitionSpec as P

MESH = pl.DeviceIdType.MESH
F32 = jnp.float32
BF = jnp.bfloat16
D = 1024
BLK = 256
HALF = 128
HD = 64
STEP = HD + 16
LAYERS = 2
NORM_EPS = 1e-05
ADAPTER_SCALE = 8.0
C0 = 0.7978845608
C1 = 0.044715
NEG = -1e30

ATTENTION = (0, 5)
PIECES = 8


def nt(a, b):
    return lax.dot_general(a, b, (((1,), (1,)), ((), ())), preferred_element_type=F32)


def nn(a, b):
    return lax.dot_general(a, b, (((1,), (0,)), ((), ())), preferred_element_type=F32)


def flip(value, bit):
    return value + (1 << bit) * (1 - 2 * ((value // (1 << bit)) % 2))


def gelu(u):
    return 0.5 * u * (1.0 + jnp.tanh(C0 * (u + C1 * u * u * u)))


def gelu_slope(u):
    square = u * u
    th = jnp.tanh(C0 * u * (1.0 + C1 * square))
    return 0.5 * (1.0 + th) + 0.5 * u * (1.0 - th * th) * (C0 * (1.0 + 3.0 * C1 * square))


def normed(x):
    c = x - jnp.mean(x, axis=-1, keepdims=True)
    rstd = lax.rsqrt(jnp.mean(c * c, axis=-1, keepdims=True) + NORM_EPS)
    return c * rstd, rstd


def norm_back(x, grad, gain):
    xhat, rstd = normed(x)
    gx = grad * gain
    return rstd * (
        gx
        - jnp.mean(gx, axis=-1, keepdims=True)
        - xhat * jnp.mean(gx * xhat, axis=-1, keepdims=True)
    )


def kernel(
    ndp,
    x_in, cot_in, qkvw, finw, outw, foutw, gains, shifts, outb, foutb, qkvb, finb, first_w, second_w,
    out_ref, gin_ref, grad_a, grad_b,
    W, n1, ga, gmx, q_ref, k_ref, v_ref, tr, low, x0, x1, m1, u0, u1, act, ctx, gctx, ctxT,
    part, rs1, rs2s, rs2r, party, rs1y, rs2ys, rs2yr, nx0, sy, syr, gqkv, gt_ref,
    acc, g_ref, gmid, own2, gsend, grecv, lse, outT, foutT, sdp, smp, vecs, bpad, bqkv, b1, packed, small_mp, aT,
    ssem, rsem, p0r,
):
    R = finw.shape[1]
    gk, gv = acc, g_ref
    d = lax.axis_index("dp")
    z = lax.axis_index("mp")
    k = d % 2
    j = d // 2
    zl = z % 2
    zh = z // 2
    qi = 2 * k + zl
    chip_bits = (ndp // 2).bit_length() - 1

    def col(dc, dz):
        zz = z
        if dz & 1:
            zz = zz + 1 - 2 * zl
        if dz & 2:
            zz = zz + 2 - 4 * zh
        return (d + 1 - 2 * k if dc else d, zz)

    sib, zp, swap = col(1, 0), col(0, 1), col(1, 2)
    count = [0]
    sends = []

    def sem():
        count[0] += 1
        return count[0] - 1

    def rcopy(src, dst, dev, keep=False):
        i = sem()
        cp = pltpu.make_async_remote_copy(
            src, dst, ssem.at[i], rsem.at[i], device_id=dev, device_id_type=MESH
        )
        cp.start()
        if keep:
            sends.append(cp.wait_send)
        return cp

    peers = [col(dc, dz) for dc in range(2) for dz in range(4) if dc or dz]
    peers += [(flip(d, bit + 1), z) for bit in range(chip_bits)]
    barrier = pltpu.get_barrier_semaphore()
    for dev in peers:
        pl.semaphore_signal(barrier, inc=1, device_id=dev, device_id_type=MESH)
    pl.semaphore_wait(barrier, len(peers))

    def swap_rows(src, dst_own, dst_other):
        i = sem()
        keep = pltpu.make_async_copy(src, dst_own, rsem.at[i])
        move = pltpu.make_async_remote_copy(
            src, dst_other, ssem.at[i], rsem.at[i], device_id=swap, device_id_type=MESH
        )

        @pl.when(k == zh)
        def _():
            keep.start()

        pl.when(k != zh)(move.start)

        def finish_send():
            @pl.when(k != zh)
            def _():
                move.wait_send()

        sends.append(finish_send)
        return keep.wait

    def many(start, size):
        return pl.ds(pl.multiple_of(start, size), size)

    def block(b):
        return many(b * BLK, BLK)

    def half(h):
        return pl.ds(h * HALF, HALF)

    def spot(b, h):
        return many(h * 4 * HALF + b * HALF, HALF)

    def chunk(c):
        return many(c * BLK, BLK)

    def plain_rows(c):
        at = (c % 2) * 2 * BLK + (c // 2) * HALF
        return many(at, HALF), many(at + BLK, HALF)

    def plain(ref, c):
        one, two = plain_rows(c)
        return jnp.concatenate([ref[one, :], ref[two, :]], axis=0)

    def plain_store(ref, c, value):
        one, two = plain_rows(c)
        ref[one, :] = value[0:HALF]
        ref[two, :] = value[HALF:BLK]

    own_rows = pl.ds(pl.multiple_of(d * R, R), R)
    chip_rows = pl.ds(pl.multiple_of(j * (2 * R), 2 * R), 2 * R)
    slots = (0, 1 + zl, 2 - zl, 3 + zl, 4 - zl, 5, 6, 7)
    sources = {
        0: [(qkvw.at[0, n], n * 256, 256) for n in range(3)] + [(outT.at[0], 768, 256)],
        1: [(finw.at[0], 0, D)],
        3: [(foutT.at[0], 0, D)],
        5: [(qkvw.at[1, n], n * 256, 256) for n in range(3)] + [(outT.at[1], 768, 256)],
        6: [(finw.at[1], 0, D)],
        7: [(foutT.at[1], 0, D)],
    }

    holder = 2 * j + zh
    home = k == zh

    def near(item):
        arrived = p0r.at[item]
        i = sem()
        for src, at, width in sources[item]:
            dst = W.at[slots[item], own_rows, pl.ds(at, width)]

            @pl.when(home)
            def _(src=src, dst=dst):
                pltpu.make_async_copy(src, dst, arrived).start()

            @pl.when(jnp.logical_not(home))
            def _(src=src, dst=dst):
                pltpu.make_async_remote_copy(
                    src, dst, ssem.at[i], arrived, device_id=(holder, z), device_id_type=MESH
                ).start()

        slab = W.at[slots[item], own_rows, :]

        def finish():
            @pl.when(jnp.logical_not(home))
            def _():
                pltpu.make_async_copy(slab, slab, ssem.at[i]).wait()

        sends.append(finish)

    far_sem = {item: sem() for item in sources}

    def far(item):
        i = far_sem[item]
        for src, at, width in sources[item]:
            dst = W.at[slots[item], own_rows, pl.ds(at, width)]
            pltpu.make_async_remote_copy(
                src, dst, ssem.at[i], p0r.at[item], device_id=(holder, swap[1]), device_id_type=MESH
            ).start()

    for item in sources:
        slab = W.at[slots[item], own_rows, :]
        sends.append(pltpu.make_async_copy(slab, slab, ssem.at[far_sem[item]]).wait)

    pass_sem = {1: sem(), 3: sem()}

    def passing(item):
        slab = W.at[slots[item], chip_rows, :]
        i = pass_sem[item]
        return pltpu.make_async_remote_copy(
            slab, slab, ssem.at[i], rsem.at[i], device_id=zp, device_id_type=MESH
        )

    def pass_on(item):
        passing(item).start()

    for item in pass_sem:
        sends.append(passing(item).wait_send)

    def arrive(item):
        if item in (2, 4):
            passing(item - 1).wait_recv()
            return
        slab = W.at[slots[item], chip_rows, :]
        pltpu.make_async_copy(slab, slab, p0r.at[item]).wait()

    half_cols = (pl.ds(0, D // 2), pl.ds(D // 2, D // 2))
    order = (tuple(range(chip_bits)), tuple(reversed(range(chip_bits))))
    stage_sem = {
        (item, stage): (sem(), sem()) for item in range(PIECES) for stage in range(chip_bits)
    }

    def stage_slabs(item, stage):
        for cols, i in zip(half_cols, stage_sem[item, stage]):
            yield W.at[slots[item], pl.ds(0, (1 << stage) * 2 * R), cols], i

    for item, stage in stage_sem:
        for slab, i in stage_slabs(item, stage):
            sends.append(pltpu.make_async_copy(slab, slab, ssem.at[i]).wait)

    def start_stage(item, stage):
        for cols, bits, i in zip(half_cols, order, stage_sem[item, stage]):
            dev = (flip(d, bits[stage] + 1), z)

            def send(m, carry=0, bits=bits, cols=cols, dev=dev, i=i):
                chip = j
                for n, bit in enumerate(bits[:stage]):
                    chip = chip + ((m // (1 << n)) % 2) * (flip(j, bit) - j)
                ref = W.at[slots[item], pl.ds(pl.multiple_of(chip * (2 * R), 2 * R), 2 * R), cols]
                pltpu.make_async_remote_copy(
                    ref, ref, ssem.at[i], rsem.at[i], device_id=dev, device_id_type=MESH
                ).start()
                return carry

            if stage <= 1:
                for m in range(1 << stage):
                    send(m)
            else:
                lax.fori_loop(0, 1 << stage, send, 0)

    def wait_stage(item, stage):
        for slab, i in stage_slabs(item, stage):
            pltpu.make_async_copy(slab, slab, rsem.at[i]).wait()

    def first(*items):
        for item in items:
            arrive(item)
            start_stage(item, 0)

    def later(*items):
        for item in items:
            for stage in range(1, chip_bits):
                wait_stage(item, stage - 1)
                start_stage(item, stage)

    def ready(item):
        wait_stage(item, chip_bits - 1)

    def at_home(f):
        pl.when(home)(f)

    def away(f):
        pl.when(jnp.logical_not(home))(f)

    def share_heads():
        packed[...] = jnp.zeros_like(packed)
        up = ADAPTER_SCALE * second_w[...].astype(F32)
        heads = qkvb[...].astype(F32)
        hidden = finb[...].astype(F32)
        down = first_w[...].astype(F32)
        for layer in range(LAYERS):
            at = 16 * layer
            packed[at : at + 4, 0:256] = up[layer, 0]
            packed[at + 4 : at + 8, 512:768] = up[layer, 1]
            for n in range(3):
                packed[at + 8 : at + 9, n * 256 : (n + 1) * 256] = heads[n, layer : layer + 1]
            packed[at + 9 : at + 10, :] = hidden[layer : layer + 1]
        small_mp[...] = packed[...].astype(BF)
        i = sem()
        mine = smp.at[zl]
        copies = [
            pltpu.make_async_remote_copy(
                small_mp, mine, ssem.at[i], rsem.at[i], device_id=col(0, r), device_id_type=MESH
            )
            for r in (1, 2, 3)
        ]
        slab = W.at[0, pl.ds(0, 3 * 32), :]

        @at_home
        def _():
            for cp in copies:
                cp.start()
            pltpu.make_async_copy(small_mp, mine, rsem.at[i]).start()

        def finish():
            at_home(pltpu.make_async_copy(slab, slab, ssem.at[i]).wait)

        sends.append(finish)
        packed[...] = jnp.zeros_like(packed)
        for layer in range(LAYERS):
            at = 16 * layer
            packed[at : at + 4, :] = down[layer, 0]
            packed[at + 4 : at + 8, :] = down[layer, 1]
            aT[layer] = jnp.zeros((128, D), BF)
            aT[layer, 0:16, :] = packed[at : at + 16, :].astype(BF)
        return pltpu.make_async_copy(smp, smp, rsem.at[i]).wait

    def share_small():
        sdp[d] = jnp.zeros((16, 128), F32)
        norm = [gains[...].astype(F32), shifts[...].astype(F32)]
        bias = [outb[...].astype(F32), foutb[...].astype(F32)]
        for layer in range(LAYERS):
            for which in range(2):
                for n in range(2):
                    at = layer * 6 + 2 * which + n
                    sdp[d, at : at + 1, 0:R] = norm[n][layer, which : which + 1]
            for n in range(2):
                at = layer * 6 + 4 + n
                sdp[d, at : at + 1, 0:R] = bias[n][layer : layer + 1]
        bits = tuple(range(1, chip_bits + 1)) + (0,)
        for stage, bit in enumerate(bits):
            i = sem()

            def send(m, carry=0, i=i, bit=bit, stage=stage):
                slot = d
                for n, b in enumerate(bits[:stage]):
                    slot = slot + ((m // (1 << n)) % 2) * (flip(d, b) - d)
                pltpu.make_async_remote_copy(
                    sdp.at[slot], sdp.at[slot], ssem.at[i], rsem.at[i],
                    device_id=(flip(d, bit), z), device_id_type=MESH,
                ).start()
                return carry

            if stage <= 2:
                for m in range(1 << stage):
                    send(m)
            else:
                lax.fori_loop(0, 1 << stage, send, 0)
            slab = sdp.at[pl.ds(0, 1 << stage)]
            pltpu.make_async_copy(slab, slab, rsem.at[i]).wait()
            sends.append(pltpu.make_async_copy(slab, slab, ssem.at[i]).wait)
        for n in range(ndp):
            vecs[:, n * R : (n + 1) * R] = sdp[n, :, 0:R]

    def unpack_small():
        keep = lax.broadcasted_iota(jnp.int32, (16, 768), 0) < 8
        for layer in range(LAYERS):
            tile = smp[zl, 16 * layer : 16 * layer + 16, :].astype(F32)
            bpad[layer] = jnp.zeros((128, 768), BF)
            bpad[layer, 0:16, :] = jnp.where(keep, tile[:, 0:768], 0.0).astype(BF)
            bqkv[layer] = tile[8:9, 0:768]
            for s in range(2):
                b1[layer, s] = smp[s, 16 * layer : 16 * layer + 16, :].astype(F32)[9:10, :]

    def vec(layer, n):
        return vecs[layer * 6 + n : layer * 6 + n + 1, :]

    class Gather:
        def __init__(self, buf, h):
            mine = buf.at[spot(qi, h)]
            self.other = buf.at[spot(2 * k + 1 - zl, h)]
            self.to_z = rcopy(mine, mine, zp)
            self.to_s = rcopy(mine, mine, sib)

        def forward(self):
            self.to_z.wait_recv()
            self.fwd = rcopy(self.other, self.other, sib)

        def chip(self):
            self.to_s.wait_recv()

        def finish(self, chip=True):
            if chip:
                self.chip()
            self.fwd.wait_recv()
            for cp in (self.to_z, self.to_s, self.fwd):
                cp.wait_send()

    first_sums = (part, rs1, rs2s, rs2r)
    late_sums = (party, rs1y, rs2ys, rs2yr)

    class Scatter:
        def __init__(self, partial, h, buffers, dst, base=None):
            p, r1, r2s, r2r = buffers
            self.h, self.dst, self.r2r = h, dst, r2r
            p[h] = partial(2 * h + 1 - k).astype(BF)
            self.first = rcopy(p.at[h], r1.at[h], sib)
            own2[...] = partial(2 * h + k)
            self.first.wait_recv()
            away, here = many((1 - zl) * HALF, HALF), many(zl * HALF, HALF)
            r2s[h] = (own2[away, :] + r1[h, away, :].astype(F32)).astype(BF)
            self.second = rcopy(r2s.at[h], r2r.at[h], zp)
            total = own2[here, :] + r1[h, here, :].astype(F32)
            dst[half(h), :] = total if base is None else total + base(half(h))

        def finish(self):
            self.second.wait_recv()
            self.dst[half(self.h), :] += self.r2r[self.h].astype(F32)
            self.first.wait_send()
            self.second.wait_send()

    class Late:
        def __init__(self, first, second, dst, r2r, h):
            self.first, self.second, self.dst, self.r2r, self.h = first, second, dst, r2r, h

        def finish(self):
            self.second.wait_recv()
            self.dst[half(self.h), :] += self.r2r[self.h].astype(F32)
            self.first.wait_send()
            self.second.wait_send()

    def add_up(partial, buffers, dst):
        p, r1, r2s, r2r = buffers
        away, here = many((1 - zl) * HALF, HALF), many(zl * HALF, HALF)
        first, out = [], []
        for h in range(2):
            p[h] = partial(2 * h + 1 - k).astype(BF)
            first.append(rcopy(p.at[h], r1.at[h], sib))
        for h in range(2):
            own2[...] = partial(2 * h + k)
            first[h].wait_recv()
            r2s[h] = (own2[away, :] + r1[h, away, :].astype(F32)).astype(BF)
            second = rcopy(r2s.at[h], r2r.at[h], zp)
            dst[half(h), :] = own2[here, :] + r1[h, here, :].astype(F32)
            out.append(Late(first[h], second, dst, r2r, h))
        return out

    class Output:
        def begin(self):
            self.first = []
            for h in range(2):
                party[h] = nt(act[2 * h + 1 - k], W[7]).astype(BF)
                self.first.append(rcopy(party.at[h], rs1y.at[h], sib))
            for h in range(2):
                nx0[h] = nt(act[2 * h + k], W[7]).astype(BF)

        def middle(self):
            away, here = many((1 - zl) * HALF, HALF), many(zl * HALF, HALF)
            self.second = []
            for h in range(2):
                self.first[h].wait_recv()
                rs2ys[h] = (nx0[h, away, :].astype(F32) + rs1y[h, away, :].astype(F32)).astype(BF)
                self.second.append(rcopy(rs2ys.at[h], rs2yr.at[h], zp))
                m1[1, half(h), :] += (
                    vec(1, 5) + nx0[h, here, :].astype(F32) + rs1y[h, here, :].astype(F32)
                )

        def finish(self):
            for h in range(2):
                self.second[h].wait_recv()
                self.first[h].wait_send()
                self.second[h].wait_send()
                party[0, half(h), :] = (m1[1, half(h), :] + rs2yr[h].astype(F32)).astype(BF)

    def by_rows(h, f):
        def body(c, carry):
            f(many(h * HALF + c * 64, 64), c * 64)
            return carry

        lax.fori_loop(0, HALF // 64, body, 0)

    def norm_into(src, h, layer, which, dst, start):
        gain, shift = vec(layer, 2 * which), vec(layer, 2 * which + 1)

        def f(rows, at):
            xhat, _ = normed(src[rows, :].astype(F32))
            dst[many(start + at, 64), :] = (xhat * gain + shift).astype(BF)

        by_rows(h, f)

    def spot_start(h):
        return h * 4 * HALF + qi * HALF

    tri = lax.broadcasted_iota(jnp.int32, (BLK, BLK), 0) <= lax.broadcasted_iota(
        jnp.int32, (BLK, BLK), 1
    )
    lane_head = lax.broadcasted_iota(jnp.int32, (1, BLK), 1) // HD
    head_rows = (
        lax.broadcasted_iota(jnp.int32, (8, BLK), 1) // HD
        == lax.broadcasted_iota(jnp.int32, (8, BLK), 0)
    ).astype(BF)

    def project(layer, h):
        w = W.at[ATTENTION[layer]]

        def body(core, carry):
            c = 2 * h + core
            rows = n1[layer, chunk(c), :]
            t = nt(rows, aT[layer]).astype(BF)
            low[layer, chunk(c), :] = t
            pr = nn(rows, w[:, 0:768]) + bqkv[layer] + nn(t, bpad[layer])
            pr = pr.astype(BF)
            plain_store(q_ref.at[layer], c, pr[:, 0:256])
            plain_store(k_ref.at[layer], c, pr[:, 256:512])
            v = pr[:, 512:768]
            plain_store(v_ref.at[layer], c, v)
            vt = v.astype(F32).T.astype(BF)
            one, two = plain_rows(c)
            for n in range(4):
                tr[STEP * n : STEP * n + HD, one] = vt[n * HD : (n + 1) * HD, 0:HALF]
                tr[STEP * n : STEP * n + HD, two] = vt[n * HD : (n + 1) * HD, HALF:BLK]
            return carry

        lax.fori_loop(0, 2, body, 0)

    def attend(layer, i):
        lo = i * BLK
        kk, qq = k_ref.at[layer], q_ref.at[layer]
        for h in range(4):
            qm = qq[lo : lo + BLK, :] * jnp.where(lane_head == h, 0.125, 0.0).astype(BF)
            rows = pl.ds(STEP * h, STEP)
            sd = jnp.where(tri, nt(kk[lo : lo + BLK, :], qm), NEG)
            top = jnp.max(sd, axis=0, keepdims=True)
            if i:
                sa = nt(kk[0:lo, :], qm)
                top = jnp.maximum(top, jnp.max(sa, axis=0, keepdims=True))
            o = nn(tr[rows, lo : lo + BLK], jnp.exp(sd - top).astype(BF))
            if i:
                o = o + nn(tr[rows, 0:lo], jnp.exp(sa - top).astype(BF))
            total = o[HD : HD + 1]
            ctxT[h * HD : (h + 1) * HD, :] = o[0:HD] * (1.0 / total)
            lse[layer, h : h + 1, lo : lo + BLK] = top + jnp.log(total)
        ctx[layer, lo : lo + BLK, :] = ctxT[...].T.astype(BF)

    def attend_back(layer, i):
        lo = i * BLK
        kk, qq, vv = k_ref.at[layer], q_ref.at[layer], v_ref.at[layer]
        grad = gctx[lo : lo + BLK, :]
        product = grad.astype(F32) * ctx[layer, lo : lo + BLK, :].astype(F32)
        high = product.astype(BF)
        sums = nt(head_rows, high) + nt(head_rows, (product - high.astype(F32)).astype(BF))
        spans = [(lo, lo + BLK)] + ([(0, lo)] if i else [])
        for pair in range(2):
            queries, grads, parts = [], [], [([], []) for _ in spans]
            for h in (2 * pair, 2 * pair + 1):
                on = lane_head == h
                qm = qq[lo : lo + BLK, :] * jnp.where(on, 0.125, 0.0).astype(BF)
                gm = grad * jnp.where(on, 1.0, 0.0).astype(BF)
                ls = lse[layer, h : h + 1, lo : lo + BLK]
                dq = None
                for (a, b), (ps, gss) in zip(spans, parts):
                    p = jnp.exp(nt(kk[a:b, :], qm) - ls)
                    if a == lo:
                        p = jnp.where(tri, p, 0.0)
                    gs = (p * (nt(vv[a:b, :], gm) - sums[h : h + 1])).astype(BF)
                    y = nn(tr[STEP * h : STEP * h + HD, a:b], gs)
                    dq = y if dq is None else dq + y
                    ps.append(p.astype(BF))
                    gss.append(gs)
                ctxT[h * HD : (h + 1) * HD, :] = dq * 0.125
                queries.append(qm)
                grads.append(gm)
            queries, grads = jnp.concatenate(queries, axis=0), jnp.concatenate(grads, axis=0)
            for (a, b), (ps, gss) in zip(spans, parts):
                dv = nn(jnp.concatenate(ps, axis=1), grads)
                dk = nn(jnp.concatenate(gss, axis=1), queries)
                for c in range(a // BLK, b // BLK):
                    at = pl.ds(c * BLK, BLK)
                    gv[:, at] += dv[c * BLK - a : (c + 1) * BLK - a]
                    gk[:, at] += dk[c * BLK - a : (c + 1) * BLK - a]
        gqkv[lo : lo + BLK, 0:256] = ctxT[...].T.astype(BF)

    def out_partial(layer):
        w = W.at[ATTENTION[layer]]
        return lambda c: nt(plain(ctx.at[layer], c), w[:, 768:1024])

    x_moves = [swap_rows(x_in.at[half(h)], x0.at[half(h)], x0.at[half(h)]) for h in range(2)]
    outT[0] = outw[0].astype(F32).T.astype(BF)
    near(0)
    far(0)
    heads_here = share_heads()
    share_small()
    foutT[0] = foutw[0].astype(F32).T.astype(BF)
    near(1)
    near(3)
    at_home(lambda: first(0, 1, 3))
    for h in range(4):
        tr[STEP * h + HD : STEP * (h + 1), :] = jnp.ones((STEP - HD, D), BF)
    outT[1] = outw[1].astype(F32).T.astype(BF)
    foutT[1] = foutw[1].astype(F32).T.astype(BF)
    near(5)
    near(6)
    near(7)
    heads_here()
    unpack_small()
    ag = []
    for h in range(2):
        x_moves[h]()
        norm_into(x0, h, 0, 0, n1.at[0], spot_start(h))
        ag.append(Gather(n1.at[0], h))
    away(lambda: far(1))
    at_home(lambda: later(0, 1))
    away(lambda: first(0))
    at_home(lambda: later(3))
    ag[0].forward()
    at_home(lambda: far(1))
    at_home(lambda: first(5))

    @away
    def _():
        later(0)
        first(1)
        pass_on(1)

    ag[1].forward()
    at_home(lambda: pass_on(1))
    far(3)
    at_home(lambda: later(5))
    ag[0].finish()
    ag[1].finish()
    away(lambda: later(1))
    at_home(lambda: pass_on(3))
    ready(0)
    project(0, 0)
    project(0, 1)
    attend(0, 0)
    attend(0, 1)
    cot_here = [
        swap_rows(
            cot_in.at[half(h)], gmx.at[spot(qi, h)], gmx.at[spot(2 * (1 - k) + zl, h)]
        )
        for h in range(2)
    ]
    at_home(lambda: first(2))

    @away
    def _():
        first(3)
        pass_on(3)

    attend(0, 2)
    attend(0, 3)
    at_home(lambda: later(2))
    away(lambda: later(3))
    sums = add_up(out_partial(0), first_sums, acc)
    far(5)
    at_home(lambda: first(4))

    @away
    def _():
        first(2, 4)
        later(2, 4)

    nx = []
    for h in range(2):
        sums[h].finish()
        m1[0, half(h), :] = x0[half(h), :].astype(F32) + acc[half(h), :] + vec(0, 4)
        norm_into(m1.at[0], h, 0, 1, nx0.at[h], k * HALF)
        mine = nx0.at[h, many(k * HALF, HALF)]
        nx.append(rcopy(mine, mine, sib))
        if h == 0:
            at_home(lambda: later(4))
    for h in range(2):
        cot_here[h]()
    gm = [Gather(gmx, h) for h in range(2)]
    far(6)
    for cp in nx:
        cp.wait_recv()

    def hidden0(s):
        def body(h, carry):
            for hc in range(2):
                cols = pl.ds(hc * 512, 512)
                u = nn(nx0[h], W[1 + s, :, cols]) + b1[0, s, :, cols]
                u0[h, s, :, cols] = u.astype(BF)
                act[2 * h + s, :, cols] = gelu(u).astype(BF)
            return carry

        lax.fori_loop(0, 2, body, 0)

    ready(1)
    hidden0(zl)
    ready(2)
    hidden0(1 - zl)
    away(lambda: first(5))
    for cp in nx:
        cp.wait_send()
    ready(3)
    ready(4)

    def share0(h, value):
        own2[...] = value
        sy[h] = own2[many((1 - k) * HALF, HALF), :].astype(BF)
        cp = rcopy(sy.at[h], syr.at[h], sib)
        acc[half(h), :] = own2[many(k * HALF, HALF), :]

        def finish():
            cp.wait_recv()
            acc[half(h), :] += syr[h].astype(F32)
            cp.wait_send()

        return finish

    ag = []
    ends = [share0(h, nt(act[2 * h], W[3]) + nt(act[2 * h + 1], W[4])) for h in range(2)]
    away(lambda: later(5))
    for h in range(2):
        ends[h]()
        x1[half(h), :] = m1[0, half(h), :] + acc[half(h), :] + vec(0, 5)
        norm_into(x1, h, 1, 0, n1.at[1], spot_start(h))
        ag.append(Gather(n1.at[1], h))
    first(6)
    ag[0].forward()
    ag[0].finish()
    ready(5)
    project(1, 0)
    ag[1].forward()
    ag[1].finish()
    later(6)
    project(1, 1)
    far(7)
    attend(1, 0)
    attend(1, 1)
    gm[0].forward()
    gm[1].forward()
    attend(1, 2)
    attend(1, 3)
    sums = add_up(out_partial(1), first_sums, acc)
    first(7)
    ag = []
    for h in range(2):
        sums[h].finish()
        m1[1, half(h), :] = x1[half(h), :] + acc[half(h), :] + vec(1, 4)
        norm_into(m1.at[1], h, 1, 1, ga, spot_start(h))
        ag.append(Gather(ga, h))
        if h == 0:
            later(7)
    ready(6)

    def hidden1(h):
        def body(core, carry):
            c = 2 * h + core
            for hc in range(2):
                cols = pl.ds(hc * 512, 512)
                u = nn(ga[chunk(c), :], W[6, :, cols]) + b1[1, zl, :, cols]
                u1[c, :, cols] = u.astype(BF)
                act[c, :, cols] = gelu(u).astype(BF)
            return carry

        lax.fori_loop(0, 2, body, 0)

    def feed_back1(c):
        gh = nn(gmx[chunk(c), :], W[7])
        gu = (gh * gelu_slope(u1[c].astype(F32))).astype(BF)
        return nt(gu, W[6])

    sums = []
    for h in range(2):
        ag[h].forward()
        ag[h].finish()
        hidden1(h)
        if h == 0:
            ready(7)
            gm[0].finish()
            gm[1].finish()
        sums.append(Scatter(feed_back1, h, first_sums, acc))

    def mid_back(layer, h, g_rows):
        gain = vec(layer, 2)

        def f(rows, at):
            v = g_rows(rows, at) + norm_back(m1[layer, rows, :], acc[rows, :], gain)
            gmid[rows, :] = v
            ga[many(spot_start(h) + at, 64), :] = v.astype(BF)

        by_rows(h, f)

    hops = [(flip(d, b), z) for b in range(1, chip_bits + 1)] + [sib, zp, col(0, 2)]

    def reduce_all(layer):
        flight = []

        def hop():
            n = len(flight)
            if n:
                if n > len(hops):
                    return
                flight[-1].wait_recv()
                total = gsend[layer, (n - 1) % 2] + grecv[layer, n - 1]
                if n == len(hops):
                    for cp in flight[-2:]:
                        cp.wait_send()
                    for n in range(2):
                        grad_a[layer, n] = total[4 * n : 4 * n + 4]
                        grad_b[layer, n] = total[8 + 4 * n : 12 + 4 * n]
                    flight.append(None)
                    return
                if n > 1:
                    flight[n - 2].wait_send()
                gsend[layer, n % 2] = total
            flight.append(rcopy(gsend.at[layer, n % 2], grecv.at[layer, n], hops[n]))

        return hop

    def turn(layer):
        def body(c, carry):
            kt = k_ref[layer, block(c), :].astype(F32).T.astype(BF)
            for n in range(4):
                tr[STEP * n : STEP * n + HD, block(c)] = kt[n * HD : (n + 1) * HD]
            return carry

        lax.fori_loop(0, 4, body, 0)

    def attention_back(layer, ag, extra, hop):
        w = W.at[ATTENTION[layer]]

        def down(b):
            rows = jnp.concatenate([ga[spot(b, 0), :], ga[spot(b, 1), :]], axis=0)
            gctx[block(b), :] = nn(rows, w[:, 768:1024]).astype(BF)

        gk[...] = jnp.zeros_like(gk)
        gv[...] = jnp.zeros_like(gv)
        ag[0].chip()
        ag[1].chip()

        def back(mine, upper):
            for zz in range(2):
                i = 2 * upper + (zz if mine else 1 - zz)

                @pl.when(zl == zz)
                def _(i=i):
                    attend_back(layer, i)

        down(zl)
        down(2 + zl)
        back(True, 1)
        ag[0].forward()
        back(True, 0)
        ag[1].forward()
        ag[0].finish(False)
        ag[1].finish(False)
        extra()
        down(1 - zl)
        down(3 - zl)
        back(False, 1)
        back(False, 0)
        hop()

        def lows(c, carry):
            gqkv[block(c), 256:512] = gk[:, block(c)].astype(BF)
            gqkv[block(c), 512:768] = gv[:, block(c)].astype(BF)
            gt_ref[block(c), :] = nt(gqkv[block(c), :], bpad[layer]).astype(BF)
            return carry

        lax.fori_loop(0, 4, lows, 0)
        step = reduce_all(layer)

        def adapters():
            def grads(c, carry):
                ga_sum, gb_sum = carry
                gtt = plain(gt_ref, c).astype(F32).T[0:16, :].astype(BF)
                tt = low[layer, chunk(c), :].astype(F32).T[0:16, :].astype(BF)
                return (
                    ga_sum + nn(gtt, n1[layer, chunk(c), :]),
                    gb_sum + nn(tt, plain(gqkv, c)),
                )

            ga_sum, gb_sum = lax.fori_loop(
                0, 4, grads, (jnp.zeros((16, D), F32), jnp.zeros((16, 768), F32))
            )
            gb = ADAPTER_SCALE * jnp.where(
                lax.broadcasted_iota(jnp.int32, (8, 256), 0) < 4, gb_sum[0:8, 0:256], gb_sum[0:8, 512:768]
            )
            gsend[layer, 0, 0:8, :] = ga_sum[0:8, :]
            gsend[layer, 0, 8:16, :] = jnp.zeros((8, D), F32)
            gsend[layer, 0, 8:16, many(qi * 256, 256)] = gb
            step()

        if layer == 0:
            adapters()
        sums = add_up(
            lambda c: nt(plain(gqkv, c), w[:, 0:768]) + nn(plain(gt_ref, c), aT[layer]),
            first_sums, acc,
        )
        if layer == 1:
            adapters()
        return sums, step

    def step_back(layer, h, src):
        gain = vec(layer, 0)

        def f(rows, at):
            g_ref[rows, :] = gmid[rows, :] + norm_back(src[rows, :].astype(F32), acc[rows, :], gain)

        by_rows(h, f)

    output = Output()
    output.begin()
    turn(1)
    ag = []
    for h in range(2):
        sums[h].finish()
        mid_back(
            1, h, lambda rows, at, h=h: gmx[many(spot_start(h) + at, 64), :].astype(F32)
        )
        ag.append(Gather(ga, h))
    sums, hop1 = attention_back(1, ag, output.middle, lambda: None)

    def feed_back0(h):
        total = None
        for s in range(2):
            gh = nn(nx0[h], W[3 + s])
            gu = (gh * gelu_slope(u0[h, s].astype(F32))).astype(BF)
            y = nt(gu, W[1 + s])
            total = y if total is None else total + y
        return total

    def next_rows(h):
        sums[h].finish()
        step_back(1, h, x1)
        nx0[h, many(k * HALF, HALF), :] = g_ref[half(h), :].astype(BF)
        mine = nx0.at[h, many(k * HALF, HALF)]
        return rcopy(mine, mine, sib)

    def after(h):
        ends[h]()
        mid_back(0, h, lambda rows, at: g_ref[rows, :])
        ag.append(Gather(ga, h))

    ag, ends = [], []
    nx = [next_rows(0)]
    turn(0)
    hop1()
    nx[0].wait_recv()
    ends.append(share0(0, feed_back0(0)))
    hop1()
    nx.append(next_rows(1))
    after(0)
    nx[1].wait_recv()
    ends.append(share0(1, feed_back0(1)))
    after(1)
    hop1()
    for cp in nx:
        cp.wait_send()
    out_here = []

    def give_output():
        output.finish()
        for h in range(2):
            out_here.append(
                swap_rows(party.at[0, half(h)], out_ref.at[half(h)], out_ref.at[half(h)])
            )

    sums, hop0 = attention_back(0, ag, lambda: (hop1(), give_output()), lambda: None)
    gin_here = []
    for _ in range(len(hops) - 3):
        hop0()
    for h in range(2):
        sums[h].finish()
        step_back(0, h, x0)
        party[1, half(h), :] = g_ref[half(h), :].astype(BF)
        gin_here.append(swap_rows(party.at[1, half(h)], gin_ref.at[half(h)], gin_ref.at[half(h)]))
        hop0()
    for _ in hops:
        hop0()
    for _ in hops:
        hop1()
    for h in range(2):
        out_here[h]()
        gin_here[h]()
    for w in sends:
        w()


def shards(
    inputs, qkv_w, qkv_b, out_w, out_b, fin_w, fin_b, fout_w, fout_b, gains, shifts, first, second,
    cotangent,
):
    ndp = lax.axis_size("dp")
    R = qkv_w.shape[1]
    hops = ndp.bit_length() - 1 + 2
    anyspec = pl.BlockSpec(memory_space=pl.ANY)
    vm = pl.BlockSpec(memory_space=pltpu.VMEM)
    V = pltpu.VMEM
    scratch = [
        V((PIECES, D, D), BF),
        V((LAYERS, D, D), BF),
        V((D, D), BF),
        V((D, D), BF),
        V((LAYERS, D, 256), BF),
        V((LAYERS, D, 256), BF),
        V((LAYERS, D, 256), BF),
        V((4 * STEP, D), BF),
        V((LAYERS, D, 128), BF),
        V((BLK, D), BF),
        V((BLK, D), F32),
        V((LAYERS, BLK, D), F32),
        V((2, 2, BLK, D), BF),
        V((4, BLK, D), BF),
        V((4, BLK, D), BF),
        V((LAYERS, D, 256), BF),
        V((D, 256), BF),
        V((256, 256), F32),
        V((2, BLK, D), BF),
        V((2, BLK, D), BF),
        V((2, HALF, D), BF),
        V((2, HALF, D), BF),
        V((2, BLK, D), BF),
        V((2, BLK, D), BF),
        V((2, HALF, D), BF),
        V((2, HALF, D), BF),
        V((2, BLK, D), BF),
        V((2, HALF, D), BF),
        V((2, HALF, D), BF),
        V((D, 768), BF),
        V((D, 128), BF),
        V((BLK, D), F32),
        V((BLK, D), F32),
        V((BLK, D), F32),
        V((BLK, D), F32),
        V((LAYERS, 2, 16, D), F32),
        V((LAYERS, hops, 16, D), F32),
        V((LAYERS, 8, D), F32),
        V((LAYERS, R, 256), BF),
        V((LAYERS, R, D), BF),
        V((ndp, 16, 128), F32),
        V((2, 32, D), BF),
        V((16, D), F32),
        V((LAYERS, 128, 768), BF),
        V((LAYERS, 1, 768), F32),
        V((LAYERS, 2, 1, D), F32),
        V((LAYERS * 16, D), F32),
        V((LAYERS * 16, D), BF),
        V((LAYERS, 128, D), BF),
        pltpu.SemaphoreType.DMA((200,)),
        pltpu.SemaphoreType.DMA((200,)),
        pltpu.SemaphoreType.DMA((PIECES,)),
    ]
    out, gin, grad_a, grad_b = pl.pallas_call(
        functools.partial(kernel, ndp),
        out_shape=(
            jax.ShapeDtypeStruct((BLK, D), BF),
            jax.ShapeDtypeStruct((BLK, D), BF),
            jax.ShapeDtypeStruct((LAYERS, 2, 4, D), F32),
            jax.ShapeDtypeStruct((LAYERS, 2, 4, D), F32),
        ),
        in_specs=[anyspec] * 4 + [vm] * 10,
        out_specs=(anyspec, anyspec, vm, vm),
        scratch_shapes=scratch,
        compiler_params=pltpu.CompilerParams(
            collective_id=0, has_side_effects=True, vmem_limit_bytes=63 * 2**20
        ),
        name="two_blocks",
    )(
        inputs, cotangent, jnp.swapaxes(qkv_w, 1, 2), fin_w, out_w, fout_w,
        gains, shifts, out_b, fout_b, jnp.swapaxes(qkv_b, 0, 1), fin_b, jnp.swapaxes(first, 2, 3), second,
    )
    return (out, gin, jnp.swapaxes(grad_a, 2, 3), grad_b)


def solution(mesh):
    placed = (
        P(("dp", "mp"), None),
        P(None, "dp", None, "mp"),
        P(None, None, "mp"),
        P(None, "mp", "dp"),
        P(None, "dp"),
        P(None, "dp", "mp"),
        P(None, "mp"),
        P(None, "mp", "dp"),
        P(None, "dp"),
        P(None, None, "dp"),
        P(None, None, "dp"),
        P(),
        P(None, None, None, "mp"),
        P(("dp", "mp"), None),
    )
    return jax.shard_map(
        shards,
        mesh=mesh,
        in_specs=placed,
        out_specs=(P(("dp", "mp"), None), P(("dp", "mp"), None), P(), P()),
        check_vma=False,
    )
```

```python
import functools

import jax
import jax.numpy as jnp
from jax import lax
from jax.experimental import pallas as pl
from jax.experimental.pallas import tpu as pltpu
from jax.sharding import PartitionSpec as P

MESH = pl.DeviceIdType.MESH
F32 = jnp.float32
BF = jnp.bfloat16
D = 1024
BLK = 256
HALF = 128
HD = 64
STEP = HD + 16
LAYERS = 2
NORM_EPS = 1e-05
ADAPTER_SCALE = 8.0
C0 = 0.7978845608
C1 = 0.044715
NEG = -1e30

ATTENTION = (0, 5)
PIECES = 8


def nt(a, b):
    return lax.dot_general(a, b, (((1,), (1,)), ((), ())), preferred_element_type=F32)


def nn(a, b):
    return lax.dot_general(a, b, (((1,), (0,)), ((), ())), preferred_element_type=F32)


def flip(value, bit):
    return value + (1 << bit) * (1 - 2 * ((value // (1 << bit)) % 2))


def gelu(u):
    return 0.5 * u * (1.0 + jnp.tanh(C0 * (u + C1 * u * u * u)))


def gelu_slope(u):
    square = u * u
    th = jnp.tanh(C0 * u * (1.0 + C1 * square))
    return 0.5 * (1.0 + th) + 0.5 * u * (1.0 - th * th) * (C0 * (1.0 + 3.0 * C1 * square))


def normed(x):
    c = x - jnp.mean(x, axis=-1, keepdims=True)
    rstd = lax.rsqrt(jnp.mean(c * c, axis=-1, keepdims=True) + NORM_EPS)
    return c * rstd, rstd


def norm_back(x, grad, gain):
    xhat, rstd = normed(x)
    gx = grad * gain
    return rstd * (
        gx
        - jnp.mean(gx, axis=-1, keepdims=True)
        - xhat * jnp.mean(gx * xhat, axis=-1, keepdims=True)
    )


def kernel(
    ndp,
    x_in, cot_in, qkvw, finw, outw, foutw, gains, shifts, outb, foutb, qkvb, finb, first_w, second_w,
    out_ref, gin_ref, grad_a, grad_b,
    W, n1, ga, gmx, q_ref, k_ref, v_ref, tr, low, x0, x1, m1, u0, u1, act, ctx, gctx, ctxT,
    part, rs1, rs2s, rs2r, party, rs1y, rs2ys, rs2yr, nx0, sy, syr, gqkv, gt_ref,
    acc, g_ref, gmid, own2, gsend, grecv, lse, outT, foutT, sdp, smp, vecs, bpad, bqkv, b1, packed, small_mp, aT,
    ssem, rsem, p0r,
):
    R = finw.shape[1]
    gk, gv = acc, g_ref
    d = lax.axis_index("dp")
    z = lax.axis_index("mp")
    k = d % 2
    j = d // 2
    zl = z % 2
    zh = z // 2
    qi = 2 * k + zl
    chip_bits = (ndp // 2).bit_length() - 1

    def col(dc, dz):
        zz = z
        if dz & 1:
            zz = zz + 1 - 2 * zl
        if dz & 2:
            zz = zz + 2 - 4 * zh
        return (d + 1 - 2 * k if dc else d, zz)

    sib, zp, swap = col(1, 0), col(0, 1), col(1, 2)
    count = [0]
    sends = []

    def sem():
        count[0] += 1
        return count[0] - 1

    def rcopy(src, dst, dev, keep=False):
        i = sem()
        cp = pltpu.make_async_remote_copy(
            src, dst, ssem.at[i], rsem.at[i], device_id=dev, device_id_type=MESH
        )
        cp.start()
        if keep:
            sends.append(cp.wait_send)
        return cp

    peers = [col(dc, dz) for dc in range(2) for dz in range(4) if dc or dz]
    peers += [(flip(d, bit + 1), z) for bit in range(chip_bits)]
    barrier = pltpu.get_barrier_semaphore()
    for dev in peers:
        pl.semaphore_signal(barrier, inc=1, device_id=dev, device_id_type=MESH)
    pl.semaphore_wait(barrier, len(peers))

    def swap_rows(src, dst_own, dst_other):
        i = sem()
        keep = pltpu.make_async_copy(src, dst_own, rsem.at[i])
        move = pltpu.make_async_remote_copy(
            src, dst_other, ssem.at[i], rsem.at[i], device_id=swap, device_id_type=MESH
        )

        @pl.when(k == zh)
        def _():
            keep.start()

        pl.when(k != zh)(move.start)

        def finish_send():
            @pl.when(k != zh)
            def _():
                move.wait_send()

        sends.append(finish_send)
        return keep.wait

    def many(start, size):
        if isinstance(start, int):
            return pl.ds(start, size)
        return pl.ds(pl.multiple_of(start, size), size)

    def block(b):
        return many(b * BLK, BLK)

    def half(h):
        return pl.ds(h * HALF, HALF)

    def spot(b, h):
        return many(h * 4 * HALF + b * HALF, HALF)

    def chunk(c):
        return many(c * BLK, BLK)

    def plain_rows(c):
        at = (c % 2) * 2 * BLK + (c // 2) * HALF
        return many(at, HALF), many(at + BLK, HALF)

    def plain(ref, c):
        one, two = plain_rows(c)
        return jnp.concatenate([ref[one, :], ref[two, :]], axis=0)

    def plain_store(ref, c, value):
        one, two = plain_rows(c)
        ref[one, :] = value[0:HALF]
        ref[two, :] = value[HALF:BLK]

    own_rows = pl.ds(pl.multiple_of(d * R, R), R)
    chip_rows = pl.ds(pl.multiple_of(j * (2 * R), 2 * R), 2 * R)
    slots = (0, 1 + zl, 2 - zl, 3 + zl, 4 - zl, 5, 6, 7)
    sources = {
        0: [(qkvw.at[0, n], n * 256, 256) for n in range(3)] + [(outT.at[0], 768, 256)],
        1: [(finw.at[0], 0, D)],
        3: [(foutT.at[0], 0, D)],
        5: [(qkvw.at[1, n], n * 256, 256) for n in range(3)] + [(outT.at[1], 768, 256)],
        6: [(finw.at[1], 0, D)],
        7: [(foutT.at[1], 0, D)],
    }

    holder = 2 * j + zh
    home = k == zh

    def near(item):
        arrived = p0r.at[item]
        i = sem()
        for src, at, width in sources[item]:
            dst = W.at[slots[item], own_rows, pl.ds(at, width)]

            @pl.when(home)
            def _(src=src, dst=dst):
                pltpu.make_async_copy(src, dst, arrived).start()

            @pl.when(jnp.logical_not(home))
            def _(src=src, dst=dst):
                pltpu.make_async_remote_copy(
                    src, dst, ssem.at[i], arrived, device_id=(holder, z), device_id_type=MESH
                ).start()

        slab = W.at[slots[item], own_rows, :]

        def finish():
            @pl.when(jnp.logical_not(home))
            def _():
                pltpu.make_async_copy(slab, slab, ssem.at[i]).wait()

        sends.append(finish)

    far_sem = {item: sem() for item in sources}

    def far(item):
        i = far_sem[item]
        for src, at, width in sources[item]:
            dst = W.at[slots[item], own_rows, pl.ds(at, width)]
            pltpu.make_async_remote_copy(
                src, dst, ssem.at[i], p0r.at[item], device_id=(holder, swap[1]), device_id_type=MESH
            ).start()

    for item in sources:
        slab = W.at[slots[item], own_rows, :]
        sends.append(pltpu.make_async_copy(slab, slab, ssem.at[far_sem[item]]).wait)

    pass_sem = {1: sem(), 3: sem()}

    def passing(item):
        slab = W.at[slots[item], chip_rows, :]
        i = pass_sem[item]
        return pltpu.make_async_remote_copy(
            slab, slab, ssem.at[i], rsem.at[i], device_id=zp, device_id_type=MESH
        )

    def pass_on(item):
        passing(item).start()

    for item in pass_sem:
        sends.append(passing(item).wait_send)

    def arrive(item):
        if item in (2, 4):
            passing(item - 1).wait_recv()
            return
        slab = W.at[slots[item], chip_rows, :]
        pltpu.make_async_copy(slab, slab, p0r.at[item]).wait()

    half_cols = (pl.ds(0, D // 2), pl.ds(D // 2, D // 2))
    order = (tuple(range(chip_bits)), tuple(reversed(range(chip_bits))))
    stage_sem = {
        (item, stage): (sem(), sem()) for item in range(PIECES) for stage in range(chip_bits)
    }

    def stage_slabs(item, stage):
        for cols, i in zip(half_cols, stage_sem[item, stage]):
            yield W.at[slots[item], pl.ds(0, (1 << stage) * 2 * R), cols], i

    for item, stage in stage_sem:
        for slab, i in stage_slabs(item, stage):
            sends.append(pltpu.make_async_copy(slab, slab, ssem.at[i]).wait)

    def start_stage(item, stage):
        for cols, bits, i in zip(half_cols, order, stage_sem[item, stage]):
            dev = (flip(d, bits[stage] + 1), z)

            def send(m, carry=0, bits=bits, cols=cols, dev=dev, i=i):
                chip = j
                for n, bit in enumerate(bits[:stage]):
                    chip = chip + ((m // (1 << n)) % 2) * (flip(j, bit) - j)
                ref = W.at[slots[item], pl.ds(pl.multiple_of(chip * (2 * R), 2 * R), 2 * R), cols]
                pltpu.make_async_remote_copy(
                    ref, ref, ssem.at[i], rsem.at[i], device_id=dev, device_id_type=MESH
                ).start()
                return carry

            if stage <= 1:
                for m in range(1 << stage):
                    send(m)
            else:
                lax.fori_loop(0, 1 << stage, send, 0)

    def wait_stage(item, stage):
        for slab, i in stage_slabs(item, stage):
            pltpu.make_async_copy(slab, slab, rsem.at[i]).wait()

    def first(*items):
        for item in items:
            arrive(item)
            start_stage(item, 0)

    def later(*items):
        for item in items:
            for stage in range(1, chip_bits):
                wait_stage(item, stage - 1)
                start_stage(item, stage)

    def ready(item):
        wait_stage(item, chip_bits - 1)

    def at_home(f):
        pl.when(home)(f)

    def away(f):
        pl.when(jnp.logical_not(home))(f)

    def share_heads():
        packed[...] = jnp.zeros_like(packed)
        up = ADAPTER_SCALE * second_w[...].astype(F32)
        heads = qkvb[...].astype(F32)
        hidden = finb[...].astype(F32)
        down = first_w[...].astype(F32)
        for layer in range(LAYERS):
            at = 16 * layer
            packed[at : at + 4, 0:256] = up[layer, 0]
            packed[at + 4 : at + 8, 512:768] = up[layer, 1]
            for n in range(3):
                packed[at + 8 : at + 9, n * 256 : (n + 1) * 256] = heads[n, layer : layer + 1]
            packed[at + 9 : at + 10, :] = hidden[layer : layer + 1]
        small_mp[...] = packed[...].astype(BF)
        i = sem()
        mine = smp.at[zl]
        copies = [
            pltpu.make_async_remote_copy(
                small_mp, mine, ssem.at[i], rsem.at[i], device_id=col(0, r), device_id_type=MESH
            )
            for r in (1, 2, 3)
        ]
        slab = W.at[0, pl.ds(0, 3 * 32), :]

        @at_home
        def _():
            for cp in copies:
                cp.start()
            pltpu.make_async_copy(small_mp, mine, rsem.at[i]).start()

        def finish():
            at_home(pltpu.make_async_copy(slab, slab, ssem.at[i]).wait)

        sends.append(finish)
        packed[...] = jnp.zeros_like(packed)
        for layer in range(LAYERS):
            at = 16 * layer
            packed[at : at + 4, :] = down[layer, 0]
            packed[at + 4 : at + 8, :] = down[layer, 1]
            aT[layer] = jnp.zeros((128, D), BF)
            aT[layer, 0:16, :] = packed[at : at + 16, :].astype(BF)
        return pltpu.make_async_copy(smp, smp, rsem.at[i]).wait

    def share_small():
        sdp[d] = jnp.zeros((16, 128), F32)
        norm = [gains[...].astype(F32), shifts[...].astype(F32)]
        bias = [outb[...].astype(F32), foutb[...].astype(F32)]
        for layer in range(LAYERS):
            for which in range(2):
                for n in range(2):
                    at = layer * 6 + 2 * which + n
                    sdp[d, at : at + 1, 0:R] = norm[n][layer, which : which + 1]
            for n in range(2):
                at = layer * 6 + 4 + n
                sdp[d, at : at + 1, 0:R] = bias[n][layer : layer + 1]
        bits = tuple(range(1, chip_bits + 1)) + (0,)
        for stage, bit in enumerate(bits):
            i = sem()

            def send(m, carry=0, i=i, bit=bit, stage=stage):
                slot = d
                for n, b in enumerate(bits[:stage]):
                    slot = slot + ((m // (1 << n)) % 2) * (flip(d, b) - d)
                pltpu.make_async_remote_copy(
                    sdp.at[slot], sdp.at[slot], ssem.at[i], rsem.at[i],
                    device_id=(flip(d, bit), z), device_id_type=MESH,
                ).start()
                return carry

            if stage <= 2:
                for m in range(1 << stage):
                    send(m)
            else:
                lax.fori_loop(0, 1 << stage, send, 0)
            slab = sdp.at[pl.ds(0, 1 << stage)]
            pltpu.make_async_copy(slab, slab, rsem.at[i]).wait()
            sends.append(pltpu.make_async_copy(slab, slab, ssem.at[i]).wait)
        for n in range(ndp):
            vecs[:, n * R : (n + 1) * R] = sdp[n, :, 0:R]

    def unpack_small():
        keep = lax.broadcasted_iota(jnp.int32, (16, 768), 0) < 8
        for layer in range(LAYERS):
            tile = smp[zl, 16 * layer : 16 * layer + 16, :].astype(F32)
            bpad[layer] = jnp.zeros((128, 768), BF)
            bpad[layer, 0:16, :] = jnp.where(keep, tile[:, 0:768], 0.0).astype(BF)
            bqkv[layer] = tile[8:9, 0:768]
            for s in range(2):
                b1[layer, s] = smp[s, 16 * layer : 16 * layer + 16, :].astype(F32)[9:10, :]

    def vec(layer, n):
        return vecs[layer * 6 + n : layer * 6 + n + 1, :]

    class Gather:
        def __init__(self, buf, h):
            mine = buf.at[spot(qi, h)]
            self.other = buf.at[spot(2 * k + 1 - zl, h)]
            self.to_z = rcopy(mine, mine, zp)
            self.to_s = rcopy(mine, mine, sib)

        def forward(self):
            self.to_z.wait_recv()
            self.fwd = rcopy(self.other, self.other, sib)

        def chip(self):
            self.to_s.wait_recv()

        def finish(self, chip=True):
            if chip:
                self.chip()
            self.fwd.wait_recv()
            for cp in (self.to_z, self.to_s, self.fwd):
                cp.wait_send()

    first_sums = (part, rs1, rs2s, rs2r)
    late_sums = (party, rs1y, rs2ys, rs2yr)

    class Scatter:
        def __init__(self, partial, h, buffers, dst, base=None):
            p, r1, r2s, r2r = buffers
            self.h, self.dst, self.r2r = h, dst, r2r
            p[h] = partial(2 * h + 1 - k).astype(BF)
            self.first = rcopy(p.at[h], r1.at[h], sib)
            own2[...] = partial(2 * h + k)
            self.first.wait_recv()
            away, here = many((1 - zl) * HALF, HALF), many(zl * HALF, HALF)
            r2s[h] = (own2[away, :] + r1[h, away, :].astype(F32)).astype(BF)
            self.second = rcopy(r2s.at[h], r2r.at[h], zp)
            total = own2[here, :] + r1[h, here, :].astype(F32)
            dst[half(h), :] = total if base is None else total + base(half(h))

        def finish(self):
            self.second.wait_recv()
            self.dst[half(self.h), :] += self.r2r[self.h].astype(F32)
            self.first.wait_send()
            self.second.wait_send()

    class Late:
        def __init__(self, first, second, dst, r2r, h):
            self.first, self.second, self.dst, self.r2r, self.h = first, second, dst, r2r, h

        def finish(self):
            self.second.wait_recv()
            self.dst[half(self.h), :] += self.r2r[self.h].astype(F32)
            self.first.wait_send()
            self.second.wait_send()

    def add_up(partial, buffers, dst):
        p, r1, r2s, r2r = buffers
        away, here = many((1 - zl) * HALF, HALF), many(zl * HALF, HALF)
        first, out = [], []
        for h in range(2):
            p[h] = partial(2 * h + 1 - k).astype(BF)
            first.append(rcopy(p.at[h], r1.at[h], sib))
        for h in range(2):
            own2[...] = partial(2 * h + k)
            first[h].wait_recv()
            r2s[h] = (own2[away, :] + r1[h, away, :].astype(F32)).astype(BF)
            second = rcopy(r2s.at[h], r2r.at[h], zp)
            dst[half(h), :] = own2[here, :] + r1[h, here, :].astype(F32)
            out.append(Late(first[h], second, dst, r2r, h))
        return out

    class Output:
        def begin(self):
            self.first = []
            for h in range(2):
                party[h] = nt(act[2 * h + 1 - k], W[7]).astype(BF)
                self.first.append(rcopy(party.at[h], rs1y.at[h], sib))
            for h in range(2):
                nx0[h] = nt(act[2 * h + k], W[7]).astype(BF)

        def middle(self):
            away, here = many((1 - zl) * HALF, HALF), many(zl * HALF, HALF)
            self.second = []
            for h in range(2):
                self.first[h].wait_recv()
                rs2ys[h] = (nx0[h, away, :].astype(F32) + rs1y[h, away, :].astype(F32)).astype(BF)
                self.second.append(rcopy(rs2ys.at[h], rs2yr.at[h], zp))
                m1[1, half(h), :] += (
                    vec(1, 5) + nx0[h, here, :].astype(F32) + rs1y[h, here, :].astype(F32)
                )

        def finish(self):
            for h in range(2):
                self.second[h].wait_recv()
                self.first[h].wait_send()
                self.second[h].wait_send()
                party[0, half(h), :] = (m1[1, half(h), :] + rs2yr[h].astype(F32)).astype(BF)

    def by_rows(h, f):
        def body(c, carry):
            f(many(h * HALF + c * 64, 64), c * 64)
            return carry

        lax.fori_loop(0, HALF // 64, body, 0)

    def norm_into(src, h, layer, which, dst, start):
        gain, shift = vec(layer, 2 * which), vec(layer, 2 * which + 1)

        def f(rows, at):
            xhat, _ = normed(src[rows, :].astype(F32))
            dst[many(start + at, 64), :] = (xhat * gain + shift).astype(BF)

        by_rows(h, f)

    def spot_start(h):
        return h * 4 * HALF + qi * HALF

    tri = lax.broadcasted_iota(jnp.int32, (BLK, BLK), 0) <= lax.broadcasted_iota(
        jnp.int32, (BLK, BLK), 1
    )
    lane_head = lax.broadcasted_iota(jnp.int32, (1, BLK), 1) // HD
    head_rows = (
        lax.broadcasted_iota(jnp.int32, (8, BLK), 1) // HD
        == lax.broadcasted_iota(jnp.int32, (8, BLK), 0)
    ).astype(BF)

    def project(layer, h):
        w = W.at[ATTENTION[layer]]

        def body(core, carry):
            c = 2 * h + core
            rows = n1[layer, chunk(c), :]
            t = nt(rows, aT[layer]).astype(BF)
            low[layer, chunk(c), :] = t
            pr = nn(rows, w[:, 0:768]) + bqkv[layer] + nn(t, bpad[layer])
            pr = pr.astype(BF)
            plain_store(q_ref.at[layer], c, pr[:, 0:256])
            plain_store(k_ref.at[layer], c, pr[:, 256:512])
            v = pr[:, 512:768]
            plain_store(v_ref.at[layer], c, v)
            vt = v.astype(F32).T.astype(BF)
            one, two = plain_rows(c)
            for n in range(4):
                tr[STEP * n : STEP * n + HD, one] = vt[n * HD : (n + 1) * HD, 0:HALF]
                tr[STEP * n : STEP * n + HD, two] = vt[n * HD : (n + 1) * HD, HALF:BLK]
            return carry

        lax.fori_loop(0, 2, body, 0)

    def attend(layer, i):
        lo = i * BLK
        kk, qq = k_ref.at[layer], q_ref.at[layer]
        for h in range(4):
            qm = qq[lo : lo + BLK, :] * jnp.where(lane_head == h, 0.125, 0.0).astype(BF)
            rows = pl.ds(STEP * h, STEP)
            sd = jnp.where(tri, nt(kk[lo : lo + BLK, :], qm), NEG)
            top = jnp.max(sd, axis=0, keepdims=True)
            if i:
                sa = nt(kk[0:lo, :], qm)
                top = jnp.maximum(top, jnp.max(sa, axis=0, keepdims=True))
            o = nn(tr[rows, lo : lo + BLK], jnp.exp(sd - top).astype(BF))
            if i:
                o = o + nn(tr[rows, 0:lo], jnp.exp(sa - top).astype(BF))
            total = o[HD : HD + 1]
            ctxT[h * HD : (h + 1) * HD, :] = o[0:HD] * (1.0 / total)
            lse[layer, h : h + 1, lo : lo + BLK] = top + jnp.log(total)
        ctx[layer, lo : lo + BLK, :] = ctxT[...].T.astype(BF)

    def attend_back(layer, i):
        lo = i * BLK
        kk, qq, vv = k_ref.at[layer], q_ref.at[layer], v_ref.at[layer]
        grad = gctx[lo : lo + BLK, :]
        product = grad.astype(F32) * ctx[layer, lo : lo + BLK, :].astype(F32)
        high = product.astype(BF)
        sums = nt(head_rows, high) + nt(head_rows, (product - high.astype(F32)).astype(BF))
        spans = [(lo, lo + BLK)] + ([(0, lo)] if i else [])
        for pair in range(2):
            queries, grads, parts = [], [], [([], []) for _ in spans]
            for h in (2 * pair, 2 * pair + 1):
                on = lane_head == h
                qm = qq[lo : lo + BLK, :] * jnp.where(on, 0.125, 0.0).astype(BF)
                gm = grad * jnp.where(on, 1.0, 0.0).astype(BF)
                ls = lse[layer, h : h + 1, lo : lo + BLK]
                dq = None
                for (a, b), (ps, gss) in zip(spans, parts):
                    p = jnp.exp(nt(kk[a:b, :], qm) - ls)
                    if a == lo:
                        p = jnp.where(tri, p, 0.0)
                    gs = (p * (nt(vv[a:b, :], gm) - sums[h : h + 1])).astype(BF)
                    y = nn(tr[STEP * h : STEP * h + HD, a:b], gs)
                    dq = y if dq is None else dq + y
                    ps.append(p.astype(BF))
                    gss.append(gs)
                ctxT[h * HD : (h + 1) * HD, :] = dq * 0.125
                queries.append(qm)
                grads.append(gm)
            queries, grads = jnp.concatenate(queries, axis=0), jnp.concatenate(grads, axis=0)
            for (a, b), (ps, gss) in zip(spans, parts):
                dv = nn(jnp.concatenate(ps, axis=1), grads)
                dk = nn(jnp.concatenate(gss, axis=1), queries)
                for c in range(a // BLK, b // BLK):
                    at = pl.ds(c * BLK, BLK)
                    gv[:, at] += dv[c * BLK - a : (c + 1) * BLK - a]
                    gk[:, at] += dk[c * BLK - a : (c + 1) * BLK - a]
        gqkv[lo : lo + BLK, 0:256] = ctxT[...].T.astype(BF)

    def out_partial(layer):
        w = W.at[ATTENTION[layer]]
        return lambda c: nt(plain(ctx.at[layer], c), w[:, 768:1024])

    x_moves = [swap_rows(x_in.at[half(h)], x0.at[half(h)], x0.at[half(h)]) for h in range(2)]
    outT[0] = outw[0].astype(F32).T.astype(BF)
    near(0)
    far(0)
    heads_here = share_heads()
    share_small()
    foutT[0] = foutw[0].astype(F32).T.astype(BF)
    near(1)
    near(3)
    at_home(lambda: first(0, 1, 3))
    for h in range(4):
        tr[STEP * h + HD : STEP * (h + 1), :] = jnp.ones((STEP - HD, D), BF)
    outT[1] = outw[1].astype(F32).T.astype(BF)
    foutT[1] = foutw[1].astype(F32).T.astype(BF)
    near(5)
    near(6)
    near(7)
    heads_here()
    unpack_small()
    ag = []
    for h in range(2):
        x_moves[h]()
        norm_into(x0, h, 0, 0, n1.at[0], spot_start(h))
        ag.append(Gather(n1.at[0], h))
    away(lambda: far(1))
    at_home(lambda: later(0, 1))
    away(lambda: first(0))
    at_home(lambda: later(3))
    ag[0].forward()
    at_home(lambda: far(1))
    at_home(lambda: first(5))

    @away
    def _():
        later(0)
        first(1)
        pass_on(1)

    ag[1].forward()
    at_home(lambda: pass_on(1))
    far(3)
    at_home(lambda: later(5))
    ag[0].finish()
    ag[1].finish()
    away(lambda: later(1))
    at_home(lambda: pass_on(3))
    ready(0)
    project(0, 0)
    project(0, 1)
    attend(0, 0)
    attend(0, 1)
    cot_here = [
        swap_rows(
            cot_in.at[half(h)], gmx.at[spot(qi, h)], gmx.at[spot(2 * (1 - k) + zl, h)]
        )
        for h in range(2)
    ]
    at_home(lambda: first(2))

    @away
    def _():
        first(3)
        pass_on(3)

    attend(0, 2)
    attend(0, 3)
    at_home(lambda: later(2))
    away(lambda: later(3))
    sums = add_up(out_partial(0), first_sums, acc)
    far(5)
    at_home(lambda: first(4))

    @away
    def _():
        first(2, 4)
        later(2, 4)

    nx = []
    for h in range(2):
        sums[h].finish()
        m1[0, half(h), :] = x0[half(h), :].astype(F32) + acc[half(h), :] + vec(0, 4)
        norm_into(m1.at[0], h, 0, 1, nx0.at[h], k * HALF)
        mine = nx0.at[h, many(k * HALF, HALF)]
        nx.append(rcopy(mine, mine, sib))
        if h == 0:
            at_home(lambda: later(4))
    for h in range(2):
        cot_here[h]()
    gm = [Gather(gmx, h) for h in range(2)]
    far(6)
    for cp in nx:
        cp.wait_recv()

    def hidden0(s):
        def body(h, carry):
            for hc in range(2):
                cols = pl.ds(hc * 512, 512)
                u = nn(nx0[h], W[1 + s, :, cols]) + b1[0, s, :, cols]
                u0[h, s, :, cols] = u.astype(BF)
                act[2 * h + s, :, cols] = gelu(u).astype(BF)
            return carry

        lax.fori_loop(0, 2, body, 0)

    ready(1)
    hidden0(zl)
    ready(2)
    hidden0(1 - zl)
    away(lambda: first(5))
    for cp in nx:
        cp.wait_send()
    ready(3)
    ready(4)

    def share0(h, value):
        own2[...] = value
        sy[h] = own2[many((1 - k) * HALF, HALF), :].astype(BF)
        cp = rcopy(sy.at[h], syr.at[h], sib)
        acc[half(h), :] = own2[many(k * HALF, HALF), :]

        def finish():
            cp.wait_recv()
            acc[half(h), :] += syr[h].astype(F32)
            cp.wait_send()

        return finish

    ag = []
    ends = [share0(h, nt(act[2 * h], W[3]) + nt(act[2 * h + 1], W[4])) for h in range(2)]
    away(lambda: later(5))
    for h in range(2):
        ends[h]()
        x1[half(h), :] = m1[0, half(h), :] + acc[half(h), :] + vec(0, 5)
        norm_into(x1, h, 1, 0, n1.at[1], spot_start(h))
        ag.append(Gather(n1.at[1], h))
    first(6)
    ag[0].forward()
    ag[0].finish()
    ready(5)
    project(1, 0)
    ag[1].forward()
    ag[1].finish()
    later(6)
    project(1, 1)
    far(7)
    attend(1, 0)
    attend(1, 1)
    gm[0].forward()
    gm[1].forward()
    attend(1, 2)
    attend(1, 3)
    sums = add_up(out_partial(1), first_sums, acc)
    first(7)
    ag = []
    for h in range(2):
        sums[h].finish()
        m1[1, half(h), :] = x1[half(h), :] + acc[half(h), :] + vec(1, 4)
        norm_into(m1.at[1], h, 1, 1, ga, spot_start(h))
        ag.append(Gather(ga, h))
        if h == 0:
            later(7)
    ready(6)

    def hidden1(h):
        def body(core, carry):
            c = 2 * h + core
            for hc in range(2):
                cols = pl.ds(hc * 512, 512)
                u = nn(ga[chunk(c), :], W[6, :, cols]) + b1[1, zl, :, cols]
                u1[c, :, cols] = u.astype(BF)
                act[c, :, cols] = gelu(u).astype(BF)
            return carry

        lax.fori_loop(0, 2, body, 0)

    def feed_back1(c):
        gh = nn(gmx[chunk(c), :], W[7])
        gu = (gh * gelu_slope(u1[c].astype(F32))).astype(BF)
        return nt(gu, W[6])

    sums = []
    for h in range(2):
        ag[h].forward()
        ag[h].finish()
        hidden1(h)
        if h == 0:
            ready(7)
            gm[0].finish()
            gm[1].finish()
        sums.append(Scatter(feed_back1, h, first_sums, acc))

    def mid_back(layer, h, g_rows):
        gain = vec(layer, 2)

        def f(rows, at):
            v = g_rows(rows, at) + norm_back(m1[layer, rows, :], acc[rows, :], gain)
            gmid[rows, :] = v
            ga[many(spot_start(h) + at, 64), :] = v.astype(BF)

        by_rows(h, f)

    hops = [(flip(d, b), z) for b in range(1, chip_bits + 1)] + [sib, zp, col(0, 2)]

    def reduce_all(layer):
        flight = []

        def hop():
            n = len(flight)
            if n:
                if n > len(hops):
                    return
                flight[-1].wait_recv()
                total = gsend[layer, (n - 1) % 2] + grecv[layer, n - 1]
                if n == len(hops):
                    for cp in flight[-2:]:
                        cp.wait_send()
                    for n in range(2):
                        grad_a[layer, n] = total[4 * n : 4 * n + 4]
                        grad_b[layer, n] = total[8 + 4 * n : 12 + 4 * n]
                    flight.append(None)
                    return
                if n > 1:
                    flight[n - 2].wait_send()
                gsend[layer, n % 2] = total
            flight.append(rcopy(gsend.at[layer, n % 2], grecv.at[layer, n], hops[n]))

        return hop

    def turn(layer):
        def body(c, carry):
            kt = k_ref[layer, block(c), :].astype(F32).T.astype(BF)
            for n in range(4):
                tr[STEP * n : STEP * n + HD, block(c)] = kt[n * HD : (n + 1) * HD]
            return carry

        lax.fori_loop(0, 4, body, 0)

    def attention_back(layer, ag, extra, hop):
        w = W.at[ATTENTION[layer]]

        def down(b):
            rows = jnp.concatenate([ga[spot(b, 0), :], ga[spot(b, 1), :]], axis=0)
            gctx[block(b), :] = nn(rows, w[:, 768:1024]).astype(BF)

        gk[...] = jnp.zeros_like(gk)
        gv[...] = jnp.zeros_like(gv)
        ag[0].chip()
        ag[1].chip()

        def back(mine, upper):
            for zz in range(2):
                i = 2 * upper + (zz if mine else 1 - zz)

                @pl.when(zl == zz)
                def _(i=i):
                    attend_back(layer, i)

        down(zl)
        down(2 + zl)
        back(True, 1)
        ag[0].forward()
        back(True, 0)
        ag[1].forward()
        ag[0].finish(False)
        ag[1].finish(False)
        extra()
        down(1 - zl)
        down(3 - zl)
        back(False, 1)
        back(False, 0)
        hop()

        def lows(c, carry):
            gqkv[block(c), 256:512] = gk[:, block(c)].astype(BF)
            gqkv[block(c), 512:768] = gv[:, block(c)].astype(BF)
            gt_ref[block(c), :] = nt(gqkv[block(c), :], bpad[layer]).astype(BF)
            return carry

        for c in range(4):
            lows(c, 0)
        step = reduce_all(layer)

        def adapters():
            def grads(c, carry):
                ga_sum, gb_sum = carry
                gtt = plain(gt_ref, c).astype(F32).T[0:16, :].astype(BF)
                tt = low[layer, chunk(c), :].astype(F32).T[0:16, :].astype(BF)
                return (
                    ga_sum + nn(gtt, n1[layer, chunk(c), :]),
                    gb_sum + nn(tt, plain(gqkv, c)),
                )

            ga_sum, gb_sum = jnp.zeros((16, D), F32), jnp.zeros((16, 768), F32)
            for c in range(4):
                ga_sum, gb_sum = grads(c, (ga_sum, gb_sum))
            gb = ADAPTER_SCALE * jnp.where(
                lax.broadcasted_iota(jnp.int32, (8, 256), 0) < 4, gb_sum[0:8, 0:256], gb_sum[0:8, 512:768]
            )
            gsend[layer, 0, 0:8, :] = ga_sum[0:8, :]
            gsend[layer, 0, 8:16, :] = jnp.zeros((8, D), F32)
            gsend[layer, 0, 8:16, many(qi * 256, 256)] = gb
            step()

        if layer == 0:
            adapters()
        sums = add_up(
            lambda c: nt(plain(gqkv, c), w[:, 0:768]) + nn(plain(gt_ref, c), aT[layer]),
            first_sums, acc,
        )
        if layer == 1:
            adapters()
        return sums, step

    def step_back(layer, h, src):
        gain = vec(layer, 0)

        def f(rows, at):
            g_ref[rows, :] = gmid[rows, :] + norm_back(src[rows, :].astype(F32), acc[rows, :], gain)

        by_rows(h, f)

    output = Output()
    output.begin()
    turn(1)
    ag = []
    for h in range(2):
        sums[h].finish()
        mid_back(
            1, h, lambda rows, at, h=h: gmx[many(spot_start(h) + at, 64), :].astype(F32)
        )
        ag.append(Gather(ga, h))
    sums, hop1 = attention_back(1, ag, output.middle, lambda: None)

    def feed_back0(h):
        total = None
        for s in range(2):
            gh = nn(nx0[h], W[3 + s])
            gu = (gh * gelu_slope(u0[h, s].astype(F32))).astype(BF)
            y = nt(gu, W[1 + s])
            total = y if total is None else total + y
        return total

    def next_rows(h):
        sums[h].finish()
        step_back(1, h, x1)
        nx0[h, many(k * HALF, HALF), :] = g_ref[half(h), :].astype(BF)
        mine = nx0.at[h, many(k * HALF, HALF)]
        return rcopy(mine, mine, sib)

    def after(h):
        ends[h]()
        mid_back(0, h, lambda rows, at: g_ref[rows, :])
        ag.append(Gather(ga, h))

    ag, ends = [], []
    nx = [next_rows(0)]
    turn(0)
    hop1()
    nx[0].wait_recv()
    ends.append(share0(0, feed_back0(0)))
    hop1()
    nx.append(next_rows(1))
    after(0)
    nx[1].wait_recv()
    ends.append(share0(1, feed_back0(1)))
    after(1)
    hop1()
    for cp in nx:
        cp.wait_send()
    out_here = []

    def give_output():
        output.finish()
        for h in range(2):
            out_here.append(
                swap_rows(party.at[0, half(h)], out_ref.at[half(h)], out_ref.at[half(h)])
            )

    sums, hop0 = attention_back(0, ag, lambda: (hop1(), give_output()), lambda: None)
    gin_here = []
    for _ in range(len(hops) - 3):
        hop0()
    for h in range(2):
        sums[h].finish()
        step_back(0, h, x0)
        party[1, half(h), :] = g_ref[half(h), :].astype(BF)
        gin_here.append(swap_rows(party.at[1, half(h)], gin_ref.at[half(h)], gin_ref.at[half(h)]))
        hop0()
    for _ in hops:
        hop0()
    for _ in hops:
        hop1()
    for h in range(2):
        out_here[h]()
        gin_here[h]()
    for w in sends:
        w()


def shards(
    inputs, qkv_w, qkv_b, out_w, out_b, fin_w, fin_b, fout_w, fout_b, gains, shifts, first, second,
    cotangent,
):
    ndp = lax.axis_size("dp")
    R = qkv_w.shape[1]
    hops = ndp.bit_length() - 1 + 2
    anyspec = pl.BlockSpec(memory_space=pl.ANY)
    vm = pl.BlockSpec(memory_space=pltpu.VMEM)
    V = pltpu.VMEM
    scratch = [
        V((PIECES, D, D), BF),
        V((LAYERS, D, D), BF),
        V((D, D), BF),
        V((D, D), BF),
        V((LAYERS, D, 256), BF),
        V((LAYERS, D, 256), BF),
        V((LAYERS, D, 256), BF),
        V((4 * STEP, D), BF),
        V((LAYERS, D, 128), BF),
        V((BLK, D), BF),
        V((BLK, D), F32),
        V((LAYERS, BLK, D), F32),
        V((2, 2, BLK, D), BF),
        V((4, BLK, D), BF),
        V((4, BLK, D), BF),
        V((LAYERS, D, 256), BF),
        V((D, 256), BF),
        V((256, 256), F32),
        V((2, BLK, D), BF),
        V((2, BLK, D), BF),
        V((2, HALF, D), BF),
        V((2, HALF, D), BF),
        V((2, BLK, D), BF),
        V((2, BLK, D), BF),
        V((2, HALF, D), BF),
        V((2, HALF, D), BF),
        V((2, BLK, D), BF),
        V((2, HALF, D), BF),
        V((2, HALF, D), BF),
        V((D, 768), BF),
        V((D, 128), BF),
        V((BLK, D), F32),
        V((BLK, D), F32),
        V((BLK, D), F32),
        V((BLK, D), F32),
        V((LAYERS, 2, 16, D), F32),
        V((LAYERS, hops, 16, D), F32),
        V((LAYERS, 8, D), F32),
        V((LAYERS, R, 256), BF),
        V((LAYERS, R, D), BF),
        V((ndp, 16, 128), F32),
        V((2, 32, D), BF),
        V((16, D), F32),
        V((LAYERS, 128, 768), BF),
        V((LAYERS, 1, 768), F32),
        V((LAYERS, 2, 1, D), F32),
        V((LAYERS * 16, D), F32),
        V((LAYERS * 16, D), BF),
        V((LAYERS, 128, D), BF),
        pltpu.SemaphoreType.DMA((200,)),
        pltpu.SemaphoreType.DMA((200,)),
        pltpu.SemaphoreType.DMA((PIECES,)),
    ]
    out, gin, grad_a, grad_b = pl.pallas_call(
        functools.partial(kernel, ndp),
        out_shape=(
            jax.ShapeDtypeStruct((BLK, D), BF),
            jax.ShapeDtypeStruct((BLK, D), BF),
            jax.ShapeDtypeStruct((LAYERS, 2, 4, D), F32),
            jax.ShapeDtypeStruct((LAYERS, 2, 4, D), F32),
        ),
        in_specs=[anyspec] * 4 + [vm] * 10,
        out_specs=(anyspec, anyspec, vm, vm),
        scratch_shapes=scratch,
        compiler_params=pltpu.CompilerParams(
            collective_id=0, has_side_effects=True, vmem_limit_bytes=63 * 2**20
        ),
        name="two_blocks",
    )(
        inputs, cotangent, jnp.swapaxes(qkv_w, 1, 2), fin_w, out_w, fout_w,
        gains, shifts, out_b, fout_b, jnp.swapaxes(qkv_b, 0, 1), fin_b, jnp.swapaxes(first, 2, 3), second,
    )
    return (out, gin, jnp.swapaxes(grad_a, 2, 3), grad_b)


def solution(mesh):
    placed = (
        P(("dp", "mp"), None),
        P(None, "dp", None, "mp"),
        P(None, None, "mp"),
        P(None, "mp", "dp"),
        P(None, "dp"),
        P(None, "dp", "mp"),
        P(None, "mp"),
        P(None, "mp", "dp"),
        P(None, "dp"),
        P(None, None, "dp"),
        P(None, None, "dp"),
        P(),
        P(None, None, None, "mp"),
        P(("dp", "mp"), None),
    )
    return jax.shard_map(
        shards,
        mesh=mesh,
        in_specs=placed,
        out_specs=(P(("dp", "mp"), None), P(("dp", "mp"), None), P(), P()),
        check_vma=False,
    )
```
